32 devices in a mesh: dp: 16 (over z, x, core), tensor: 2 (over y).
Axes of the slice: x: 2, y: 2, z: 4, core: 2. Of those that a mesh axis runs over, the one named last changes fastest.
Arguments:
- block_input: bfloat16 [16384, 1024], P(('dp', 'tensor')), may hold values from -6 to 6
- segment_ids: int32 [16, 1024], P('dp'), may hold values from 0 to 3, never falling along the last dimension, each value on 1 to 512 neighbouring positions
- out_grad: bfloat16 [16384, 1024], P(('dp', 'tensor')), may hold values from -6 to 6
- gating_weight: bfloat16 [1024, 1536], P(None, 'tensor'), may hold values from -0.1875 to 0.1875
- inner_weight: bfloat16 [1024, 1536], P(None, 'tensor'), may hold values from -0.1875 to 0.1875
- state_weight: bfloat16 [1024, 256], replicated, may hold values from -0.1875 to 0.1875
- step_weight: bfloat16 [1024, 24], P(None, 'tensor'), may hold values from -0.1875 to 0.1875
- step_bias: float32 [24], P('tensor'), may hold values from -6.5 to -2.5
- decay_log: float32 [24], P('tensor'), may hold values from 0 to 2.77
- skip_scale: float32 [24], P('tensor'), may hold values from 0.5 to 1.5
- inner_conv: bfloat16 [4, 1536], P(None, 'tensor'), may hold values from -3 to 3
- state_conv: bfloat16 [4, 256], replicated, may hold values from -3 to 3
- mixer_gain: bfloat16 [1536], P('tensor'), may hold values from 0.5 to 1.5
- mixer_proj: bfloat16 [1536, 1024], P('tensor'), may hold values from -0.15625 to 0.15625
- query_weight: bfloat16 [1024, 512], P(None, 'tensor'), may hold values from -0.1875 to 0.1875
- key_weight: bfloat16 [1024, 128], P(None, 'tensor'), may hold values from -0.1875 to 0.1875
- value_weight: bfloat16 [1024, 128], P(None, 'tensor'), may hold values from -0.1875 to 0.1875
- attention_out: bfloat16 [512, 1024], P('tensor'), may hold values from -1 to 1
- first_gain: bfloat16 [1024], replicated, may hold values from 0.5 to 1.5
- second_gain: bfloat16 [1024], replicated, may hold values from 0.5 to 1.5
- gate_weight: bfloat16 [1024, 2048], P(None, 'tensor'), may hold values from -0.1875 to 0.1875
- up_weight: bfloat16 [1024, 2048], P(None, 'tensor'), may hold values from -0.1875 to 0.1875
- down_projection_weight: bfloat16 [2048, 1024], P('tensor'), may hold values from -0.125 to 0.125
Outputs:
- block_output: bfloat16 [16384, 1024], P(('dp', 'tensor'))
- input_grad: float32 [16384, 1024], P(('dp', 'tensor'))
- grad_gating: float32 [1024, 1536], P(None, 'tensor')
- grad_inner: float32 [1024, 1536], P(None, 'tensor')
- grad_state: float32 [1024, 256], replicated
- grad_step: float32 [1024, 24], P(None, 'tensor')
- grad_step_bias: float32 [24], P('tensor')
- grad_decay_log: float32 [24], P('tensor')
- grad_skip_scale: float32 [24], P('tensor')
- grad_inner_conv: float32 [4, 1536], P(None, 'tensor')
- grad_state_conv: float32 [4, 256], replicated
- grad_mixer_gain: float32 [1536], P('tensor')
- grad_mixer_proj: float32 [1536, 1024], P('tensor')
- grad_query: float32 [1024, 512], P(None, 'tensor')
- grad_key: float32 [1024, 128], P(None, 'tensor')
- grad_value: float32 [1024, 128], P(None, 'tensor')
- attention_output_gradient: float32 [512, 1024], P('tensor')
- grad_first_gain: float32 [1024], replicated
- grad_second_gain: float32 [1024], replicated
- grad_gate: float32 [1024, 2048], P(None, 'tensor')
- grad_up: float32 [1024, 2048], P(None, 'tensor')
- grad_down: float32 [2048, 1024], P('tensor')
The draws below stay inside these ranges and needn't reach their ends.
Inputs may be any that keep to these rules, and one draw needn't show every extreme that they name: `segment_ids`: segment numbers never fall along a sequence; each segment has at most 512 tokens.
All inputs are finite; a program needn't handle non-finite values.
Results may differ from the reference program's by a relative error of at most 0.014.
Values may be sent and summed in bfloat16 or wider, within the bound.
No kernel may reach another device: no remote copies, remote signals or barrier semaphores. Data moves between devices by JAX's collectives and lax.ppermute only.
A program may use at most 192 MiB of HBM per device.

```python
import math
import jax
import jax.numpy as jnp
import numpy as np
from jax import lax

D = 1024
FF = 2048
H_SSM = 24
P_SIZE = 64
N_STATE = 128
K_CONV = 4
H_Q = 8
H_KV = 2
HD = 64
SEQ_LEN = 1024
SPAN = 128
ATT_BLOCK = 512
SEG_COUNT = 4
SEG_MOST = 512
SEQS = 16
TOKENS = 16384


def block_levels(stream_key, shape, split, least, high):
    level = 1.0
    for position, shards_of in split:
        heights = jax.random.uniform(jax.random.fold_in(jax.random.fold_in(stream_key, 6), position), (shards_of,), jnp.float32, least / len(split), high / len(split))
        level = level * jnp.repeat(jnp.exp(heights), shape[position] // shards_of).reshape((-1,) + (1,) * (len(shape) - 1 - position))
    return level


def split_up(count, total, most, lean):
    weights = [(1 << 20) // math.isqrt(standing ** lean) + 1 for standing in range(2, count + 1)]
    rest, holding = total - most - (count - 1), [1] * (count - 1)
    while rest > 0:
        free = [i for i in range(count - 1) if holding[i] < most]
        pool, remaining = sum([weights[i] for i in free]), rest
        for i in free:
            more = min(most - holding[i], max(1, remaining * weights[i] // pool), rest)
            holding[i] = holding[i] + more
            rest = rest - more
    return np.array([most] + holding)


def uneven_parts(own_key, count, total, limit, skew):
    if count == 2:
        one = jax.random.randint(own_key, (), max(1, total - limit), min(limit, total - 1) + 1)
        return jnp.stack([one, total - one])
    lengths = jnp.asarray(split_up(count, total, limit, skew), jnp.int32)
    couples = (count - 1) // 2
    source_of, sink = lengths[1:1 + 2 * couples:2], lengths[2:2 + 2 * couples:2]
    margin = jnp.minimum(source_of - 1, limit - sink)
    moved = jax.random.randint(jax.random.fold_in(own_key, 1), (couples,), 0, 1 << 20) % (margin + 1)
    lengths = lengths.at[1:1 + 2 * couples:2].set(source_of - moved).at[2:2 + 2 * couples:2].set(sink + moved)
    return lengths[jax.random.permutation(jax.random.fold_in(own_key, 2), count)]


def normal_values(own_key, extent, width, bound, cuts=(), held_as=jnp.bfloat16):
    values = width * jax.random.normal(own_key, extent, jnp.float32)
    if cuts:
        values = values * block_levels(own_key, extent, cuts, -0.22, 0.18)
    return jnp.clip(values, -bound, bound).astype(held_as)


def setup_inputs(seed: int = 0) -> dict:
    seeds = jax.random.split(jax.random.key(seed), 24)
    return {
        "block_input": normal_values(seeds[0], (TOKENS, D), 1.0, 6.0, ((0, 32),)),
        "segment_ids": jax.vmap(lambda own: jnp.searchsorted(jnp.cumsum(uneven_parts(own, SEG_COUNT, SEQ_LEN, SEG_MOST, 2)), jnp.arange(SEQ_LEN), side="right"))(jax.random.split(seeds[1], SEQS)).reshape((SEQS, SEQ_LEN)).astype(jnp.int32),
        "out_grad": normal_values(seeds[2], (TOKENS, D), 1.0, 6.0, ((0, 32),)),
        "gating_weight": normal_values(seeds[3], (D, H_SSM * P_SIZE), D ** -0.5, 0.1875, ((1, 2),)),
        "inner_weight": normal_values(seeds[4], (D, H_SSM * P_SIZE), D ** -0.5, 0.1875, ((1, 2),)),
        "state_weight": normal_values(seeds[5], (D, 2 * N_STATE), D ** -0.5, 0.1875),
        "step_weight": normal_values(seeds[6], (D, H_SSM), D ** -0.5, 0.1875, ((1, 2),)),
        "step_bias": jnp.clip(-6.5 + 4.0 * jax.random.uniform(seeds[7], (H_SSM,), jnp.float32) ** block_levels(seeds[7], (H_SSM,), ((0, 2),), -0.2, 0.2), -6.5, -2.5),
        "decay_log": jnp.clip(2.77 * jax.random.uniform(seeds[8], (H_SSM,), jnp.float32) ** block_levels(seeds[8], (H_SSM,), ((0, 2),), -0.2, 0.2), 0.0, 2.77),
        "skip_scale": jnp.clip(0.5 + 1.0 * jax.random.uniform(seeds[9], (H_SSM,), jnp.float32) ** block_levels(seeds[9], (H_SSM,), ((0, 2),), -0.2, 0.2), 0.5, 1.5),
        "inner_conv": normal_values(seeds[10], (K_CONV, H_SSM * P_SIZE), K_CONV ** -0.5, 3.0, ((1, 2),)),
        "state_conv": normal_values(seeds[11], (K_CONV, 2 * N_STATE), K_CONV ** -0.5, 3.0),
        "mixer_gain": jnp.clip(1.0 + 0.1 * jax.random.normal(seeds[12], (H_SSM * P_SIZE,), jnp.float32), 0.5, 1.5).astype(jnp.bfloat16),
        "mixer_proj": normal_values(seeds[13], (H_SSM * P_SIZE, D), (H_SSM * P_SIZE) ** -0.5, 0.15625, ((0, 2),)),
        "query_weight": normal_values(seeds[14], (D, H_Q * HD), D ** -0.5, 0.1875, ((1, 2),)),
        "key_weight": normal_values(seeds[15], (D, H_KV * HD), D ** -0.5, 0.1875, ((1, 2),)),
        "value_weight": normal_values(seeds[16], (D, H_KV * HD), D ** -0.5, 0.1875, ((1, 2),)),
        "attention_out": normal_values(seeds[17], (H_Q * HD, D), (H_Q * HD // 16) ** -0.5, 1.0, ((0, 2),)),
        "first_gain": jnp.clip(1.0 + 0.1 * jax.random.normal(seeds[18], (D,), jnp.float32), 0.5, 1.5).astype(jnp.bfloat16),
        "second_gain": jnp.clip(1.0 + 0.1 * jax.random.normal(seeds[19], (D,), jnp.float32), 0.5, 1.5).astype(jnp.bfloat16),
        "gate_weight": normal_values(seeds[20], (D, FF), D ** -0.5, 0.1875, ((1, 2),)),
        "up_weight": normal_values(seeds[21], (D, FF), D ** -0.5, 0.1875, ((1, 2),)),
        "down_projection_weight": normal_values(seeds[22], (FF, D), FF ** -0.5, 0.125, ((0, 2),)),
    }


epsilon = 1e-05
rope_base = 100000000000.0
top_precision = lax.Precision.HIGHEST

@jax.custom_vjp
def low(v):
    return lax.optimization_barrier(v.astype(jnp.bfloat16)).astype(jnp.float32)

@jax.custom_vjp
def low_back(v):
    return v

def low_keep(v):
    return (low(v), None)

def low_pass(kept, grad):
    return (grad,)

def back_keep(v):
    return (v, None)

def back_low(kept, grad):
    return (low(grad),)
low.defvjp(low_keep, low_pass)
low_back.defvjp(back_keep, back_low)

def root_norm(value_tensor, gain_vector):
    inverse = lax.rsqrt(lax.optimization_barrier(jnp.mean(value_tensor * value_tensor, axis=-1, keepdims=True)) + epsilon)
    return value_tensor * inverse * gain_vector

def project(value_tensor, weight_matrix):
    return jnp.einsum('kuy,ym->kum', value_tensor, weight_matrix, precision=top_precision)

def causal_conv(value_tensor, kernel):
    tap_count = kernel.shape[0]
    length = value_tensor.shape[1]
    padded = jnp.pad(value_tensor, ((0, 0), (tap_count - 1, 0), (0, 0)))
    result = padded[:, 0:length] * kernel[0]
    for offset in range(1, tap_count):
        result = result + padded[:, offset:offset + length] * kernel[offset]
    return result

def rope_tables(length, head_size):
    positions = jnp.arange(length, dtype=jnp.float32)
    frequency = rope_base ** (-jnp.arange(0, head_size, 2, dtype=jnp.float32) / head_size)
    angles = positions[:, None] * frequency[None, :]
    angles = jnp.concatenate([angles, angles], axis=-1)
    return (jnp.cos(angles)[:, None, :], jnp.sin(angles)[:, None, :])

def rotate(value_tensor, cosine, sine_table):
    half_size = value_tensor.shape[-1] // 2
    turned = jnp.concatenate([-value_tensor[..., half_size:], value_tensor[..., :half_size]], axis=-1)
    return value_tensor * cosine + turned * sine_table

def ssd_spans(inner, in_vec, out_vec, step_sizes, decay_rate):
    seq_count, length, head_count, head_size = inner.shape
    state_size = in_vec.shape[-1]
    block_count = length // SPAN

    def to_blocks(value_tensor):
        return jnp.swapaxes(value_tensor.reshape((seq_count, block_count, SPAN) + value_tensor.shape[2:]), 0, 1)
    lower_mask = jnp.arange(SPAN)[:, None] >= jnp.arange(SPAN)[None, :]

    def one_block(carry_state, pieces):
        inner_block, in_block, out_block, step_block = pieces
        cumulative = jnp.cumsum(step_block * decay_rate, axis=1)
        log_gaps = cumulative[:, :, None, :] - cumulative[:, None, :, :]
        within = jnp.exp(jnp.where(lower_mask[None, :, :, None], log_gaps, -1e+30))
        scores = jnp.einsum('stn,sun->stu', out_block, in_block, precision=top_precision)
        mixing = scores[..., None] * within * step_block[:, None, :, :]
        within_block = jnp.einsum('stuh,suhp->sthp', mixing, inner_block, precision=top_precision)
        from_state = jnp.einsum('stn,shpn->sthp', out_block, carry_state, precision=top_precision) * jnp.exp(cumulative)[..., None]
        tail_weight = jnp.exp(cumulative[:, -1:, :] - cumulative) * step_block
        carry_state = carry_state * jnp.exp(cumulative[:, -1, :])[:, :, None, None] + jnp.einsum('suh,suhp,sun->shpn', tail_weight, inner_block, in_block, precision=top_precision)
        return (carry_state, within_block + from_state)
    initial = jnp.zeros((seq_count, head_count, head_size, state_size), inner.dtype)
    final_state, outputs = lax.scan(jax.checkpoint(one_block), initial, (to_blocks(inner), to_blocks(in_vec), to_blocks(out_vec), to_blocks(step_sizes)))
    return jnp.swapaxes(outputs, 0, 1).reshape(seq_count, length, head_count, head_size)

def attend(queries, key_rows, value_rows, segments):
    seq_count, length, kv_heads, group_width, head_size = queries.shape
    scale_factor = head_size ** (-0.5)
    positions = jnp.arange(length)

    def one_block(block_start):
        query_block = lax.dynamic_slice_in_dim(queries, block_start, ATT_BLOCK, 1)
        seg_block = lax.dynamic_slice_in_dim(segments, block_start, ATT_BLOCK, 1)
        row_index = block_start + jnp.arange(ATT_BLOCK)
        allowed = (positions[None, :] <= row_index[:, None])[None] & (seg_block[:, :, None] == segments[:, None, :])
        scores = jnp.einsum('sqkgd,slkd->skgql', query_block, key_rows, precision=top_precision) * scale_factor
        scores = low_back(jnp.where(allowed[:, None, None], scores, -1e+30))
        shifted = scores - lax.optimization_barrier(jnp.max(scores, axis=-1, keepdims=True))
        weights = jnp.exp(shifted)
        attn_probs = low(weights / lax.optimization_barrier(jnp.sum(weights, axis=-1, keepdims=True)))
        return jnp.einsum('skgql,slkd->sqkgd', attn_probs, value_rows, precision=top_precision)
    starts = (jnp.arange(length // ATT_BLOCK) * ATT_BLOCK).astype(jnp.int32)
    blocks = lax.map(jax.checkpoint(one_block), starts)
    return jnp.swapaxes(blocks, 0, 1).reshape(seq_count, length, kv_heads * group_width * head_size)

def forward(params, tokens, segments):
    gating_weight, inner_weight, state_weight, step_weight, step_bias, decay_log, skip_scale, inner_conv, state_conv, mixer_gain, mixer_proj, query_weight, key_weight, value_weight, attention_out, first_gain, second_gain, gate_weight, up_weight, down_projection_weight = params
    seq_count, length, model_width = tokens.shape
    normed = low(root_norm(tokens, first_gain))
    gating_pre = low_back(project(normed, gating_weight))
    inner_pre = low_back(project(normed, inner_weight))
    state_pre = low_back(project(normed, state_weight))
    step_pre = low_back(project(normed, step_weight))
    inner_act = jax.nn.silu(causal_conv(inner_pre, inner_conv))
    state_act = jax.nn.silu(causal_conv(state_pre, state_conv))
    step_sizes = jax.nn.softplus(step_pre + step_bias)
    decay_rate = -jnp.exp(decay_log)
    split_act = inner_act.reshape(seq_count, length, H_SSM, P_SIZE)
    scanned = ssd_spans(split_act, state_act[..., :N_STATE], state_act[..., N_STATE:], step_sizes, decay_rate)
    scanned = scanned + skip_scale[:, None] * split_act
    gated = scanned.reshape(seq_count, length, H_SSM * P_SIZE) * jax.nn.silu(gating_pre)
    mixer_part = project(low(root_norm(gated, mixer_gain)), mixer_proj)
    cosine, sine_table = rope_tables(length, HD)
    queries = low(rotate(low_back(project(normed, query_weight)).reshape(seq_count, length, H_Q, HD), cosine, sine_table))
    key_rows = low(rotate(low_back(project(normed, key_weight)).reshape(seq_count, length, H_KV, HD), cosine, sine_table))
    value_rows = low(low_back(project(normed, value_weight))).reshape(seq_count, length, H_KV, HD)
    attended = attend(queries.reshape(seq_count, length, H_KV, H_Q // H_KV, HD), key_rows, value_rows, segments)
    attn_part = project(low(low_back(attended)), attention_out)
    residual = tokens + low_back(mixer_part + attn_part)
    normed_two = low(root_norm(residual, second_gain))
    gate_pre = low_back(project(normed_two, gate_weight))
    up_pre = low_back(project(normed_two, up_weight))
    hidden = low(jax.nn.silu(gate_pre) * up_pre)
    return residual + low_back(project(hidden, down_projection_weight))

def reference(block_input, segment_ids, out_grad, gating_weight, inner_weight, state_weight, step_weight, step_bias, decay_log, skip_scale, inner_conv, state_conv, mixer_gain, mixer_proj, query_weight, key_weight, value_weight, attention_out, first_gain, second_gain, gate_weight, up_weight, down_projection_weight):
    params = tuple((weight.astype(jnp.float32) for weight in (gating_weight, inner_weight, state_weight, step_weight, step_bias, decay_log, skip_scale, inner_conv, state_conv, mixer_gain, mixer_proj, query_weight, key_weight, value_weight, attention_out, first_gain, second_gain, gate_weight, up_weight, down_projection_weight)))
    group_seqs = max(1, min(4, 4096 // SEQ_LEN))
    group_count = SEQS // group_seqs
    inputs = block_input.astype(jnp.float32).reshape(group_count, group_seqs, SEQ_LEN, D)
    cotangents = out_grad.astype(jnp.float32).reshape(group_count, group_seqs, SEQ_LEN, D)
    segments = segment_ids.reshape(group_count, group_seqs, SEQ_LEN)

    def one_group(totals, pieces):
        tokens, seg_group, cotangent = pieces

        def run_group(weights, value_tensor):
            return forward(weights, value_tensor, seg_group)
        result, pullback = jax.vjp(run_group, params, tokens)
        weight_grads, token_grad = pullback(cotangent)
        totals = jax.tree.map(jnp.add, totals, weight_grads)
        return (totals, (result, token_grad))
    initial = tuple((jnp.zeros_like(weight) for weight in params))
    totals, (results, token_grads) = lax.scan(one_group, initial, (inputs, segments, cotangents))
    return (results.reshape(TOKENS, D).astype(jnp.bfloat16), token_grads.reshape(TOKENS, D), totals[0], totals[1], totals[2], totals[3], totals[4], totals[5], totals[6], totals[7], totals[8], totals[9], totals[10], totals[11], totals[12], totals[13], totals[14], totals[15], totals[16], totals[17], totals[18], totals[19])
```

```python
import jax
import jax.numpy as jnp
from jax import lax
from jax.sharding import PartitionSpec as P

H_SSM = 24
P_SIZE = 64
HD = 64
SPAN = 128
ATT_BLOCK = 512


epsilon = 1e-05
rope_base = 100000000000.0
top_precision = lax.Precision.HIGHEST


def dense(left_side, right_side):
    return jnp.dot(left_side, right_side, preferred_element_type=jnp.float32)


def row_dot(left_side, right_side):
    return lax.dot_general(
        left_side, right_side, (((0,), (0,)), ((), ())), preferred_element_type=jnp.float32
    )


def back_dot(left_side, right_side):
    return lax.dot_general(
        left_side, right_side, (((1,), (1,)), ((), ())), preferred_element_type=jnp.float32
    )


def causal_conv(value_tensor, kernel):
    tap_count = kernel.shape[0]
    length = value_tensor.shape[1]
    padded = jnp.pad(value_tensor, ((0, 0), (tap_count - 1, 0), (0, 0)))
    result = padded[:, 0:length] * kernel[0]
    for offset in range(1, tap_count):
        result = result + padded[:, offset : offset + length] * kernel[offset]
    return result


def rope_tables(length, head_size):
    positions = jnp.arange(length, dtype=jnp.float32)
    frequency = rope_base ** (-jnp.arange(0, head_size, 2, dtype=jnp.float32) / head_size)
    angles = positions[:, None] * frequency[None, :]
    angles = jnp.concatenate([angles, angles], axis=-1)
    return (jnp.cos(angles)[:, None, :], jnp.sin(angles)[:, None, :])


def rotate(value_tensor, cosine, sine_table):
    half_size = value_tensor.shape[-1] // 2
    turned = jnp.concatenate(
        [-value_tensor[..., half_size:], value_tensor[..., :half_size]], axis=-1
    )
    return value_tensor * cosine + turned * sine_table


def unrotate(grad_values, cosine, sine_table):
    half_size = grad_values.shape[-1] // 2
    product = grad_values * sine_table
    turned = jnp.concatenate([product[..., half_size:], -product[..., :half_size]], axis=-1)
    return grad_values * cosine + turned


def norm_back(grad_values, value_tensor, inverse, gain_vector):
    scaled = grad_values * gain_vector
    return inverse * scaled - value_tensor * inverse**3 * jnp.mean(
        value_tensor * scaled, axis=-1, keepdims=True
    )


def swap_tensor(value):
    return lax.ppermute(value, "tensor", [(0, 1), (1, 0)])


def both(value):
    return value + swap_tensor(value)


def in_order(place, own, other):
    first = jnp.where(place == 0, own, other)
    second = jnp.where(place == 0, other, own)
    return jnp.concatenate([first, second], axis=0)


def gather_rows(share):
    return in_order(lax.axis_index("tensor"), share, swap_tensor(share))


def half_of(value, place):
    half = value.shape[0] // 2
    return lax.dynamic_slice_in_dim(value, place * half, half, 0)


def scatter_rows(partial):
    place = lax.axis_index("tensor")
    got = swap_tensor(half_of(partial, 1 - place).astype(jnp.bfloat16))
    return half_of(partial, place).astype(jnp.float32) + got.astype(jnp.float32)


def flip(value, bit):
    size = lax.axis_size("dp")
    return lax.ppermute(value, "dp", [(i, i ^ bit) for i in range(size)])


def bits_in_order(far_first):
    count = lax.axis_size("dp").bit_length() - 1
    bits = [1 << i for i in range(count)]
    return bits[:1] + bits[2:] + bits[1:2] if far_first else bits


def sum_over_dp(arrays, far_first, over_tensor=False):
    index = lax.axis_index("dp")
    bits = bits_in_order(far_first)
    places = [(index // bit) % 2 for bit in bits]

    def joined(parts):
        return parts[0] if len(parts) == 1 else jnp.concatenate(parts, axis=0)

    current = None
    for bit, place in zip(bits, places):
        if current is None:
            keep = joined([half_of(a, place).astype(jnp.bfloat16) for a in arrays])
            send = joined([half_of(a, 1 - place).astype(jnp.bfloat16) for a in arrays])
        else:
            keep, send = half_of(current, place), half_of(current, 1 - place)
        got = flip(send, bit)
        current = (keep.astype(jnp.float32) + got.astype(jnp.float32)).astype(jnp.bfloat16)
    if over_tensor:
        current = (current.astype(jnp.float32) + swap_tensor(current).astype(jnp.float32)).astype(jnp.bfloat16)
    for bit, place in list(zip(bits, places))[:0:-1]:
        current = in_order(place, current, flip(current, bit))
    other = flip(current, bits[0])
    results, start = [], 0
    for a in arrays:
        rows = a.shape[0] // 2
        results.append(
            in_order(places[0], current[start : start + rows], other[start : start + rows]).astype(jnp.float32)
        )
        start += rows
    return results


def sum_small(value):
    size = lax.axis_size("dp")
    bit = 1
    while bit < size:
        value = value + flip(value, bit)
        bit *= 2
    return value


def ssd_spans(inner, in_vec, out_vec, step_sizes, decay_rate):
    seq_count, length, head_count, head_size = inner.shape
    state_size = in_vec.shape[-1]
    block_count = length // SPAN

    def to_blocks(value_tensor):
        return jnp.swapaxes(
            value_tensor.reshape((seq_count, block_count, SPAN) + value_tensor.shape[2:]), 0, 1
        )

    lower_mask = jnp.arange(SPAN)[:, None] >= jnp.arange(SPAN)[None, :]

    def one_block(carry_state, pieces):
        inner_block, in_block, out_block, step_block = pieces
        cumulative = jnp.einsum(
            "ts,bsh->bth", lower_mask.astype(jnp.float32), step_block * decay_rate, precision=top_precision
        )
        log_gaps = cumulative[:, :, None, :] - cumulative[:, None, :, :]
        within = jnp.exp(jnp.where(lower_mask[None, :, :, None], log_gaps, -1e30))
        scores = jnp.einsum("stn,sun->stu", out_block, in_block, precision=top_precision)
        mixing = scores[..., None] * within * step_block[:, None, :, :]
        within_block = jnp.einsum("stuh,suhp->sthp", mixing, inner_block, precision=top_precision)
        from_state = (
            jnp.einsum("stn,shpn->sthp", out_block, carry_state, precision=top_precision)
            * jnp.exp(cumulative)[..., None]
        )
        tail_weight = jnp.exp(cumulative[:, -1:, :] - cumulative) * step_block
        carry_state = carry_state * jnp.exp(cumulative[:, -1, :])[:, :, None, None] + jnp.einsum(
            "suh,suhp,sun->shpn", tail_weight, inner_block, in_block, precision=top_precision
        )
        return (carry_state, within_block + from_state)

    initial = jnp.zeros((seq_count, head_count, head_size, state_size), inner.dtype)
    final_state, outputs = lax.scan(
        jax.checkpoint(one_block),
        initial,
        (to_blocks(inner), to_blocks(in_vec), to_blocks(out_vec), to_blocks(step_sizes)),
    )
    return jnp.swapaxes(outputs, 0, 1).reshape(seq_count, length, head_count, head_size)


def state_piece(pre_values, conv_kernel):
    return jax.nn.silu(causal_conv(pre_values, conv_kernel))


def mixer_piece(
    inner_pre, state_act, step_pre, gating_pre, inner_conv, step_bias, decay_log, skip_scale
):
    seq_count, length, channels = inner_pre.shape
    head_count = step_pre.shape[-1]
    state_size = state_act.shape[-1] // 2
    inner_act = jax.nn.silu(causal_conv(inner_pre, inner_conv))
    step_sizes = jax.nn.softplus(step_pre + step_bias)
    decay_rate = -jnp.exp(decay_log)
    split_act = inner_act.reshape(seq_count, length, head_count, channels // head_count)
    scanned = ssd_spans(
        split_act, state_act[..., :state_size], state_act[..., state_size:], step_sizes, decay_rate
    )
    scanned = scanned + skip_scale[:, None] * split_act
    return scanned.reshape(seq_count, length, channels) * jax.nn.silu(gating_pre)


def on_device(
    block_input,
    segment_ids,
    out_grad,
    gating_weight,
    inner_weight,
    state_weight,
    step_weight,
    step_bias,
    decay_log,
    skip_scale,
    inner_conv,
    state_conv,
    mixer_gain,
    mixer_proj,
    query_weight,
    key_weight,
    value_weight,
    attention_out,
    first_gain,
    second_gain,
    gate_weight,
    up_weight,
    down_projection_weight,
):
    seq_count, seq_len = segment_ids.shape
    token_count = seq_count * seq_len
    channels = inner_weight.shape[1]
    head_local = step_weight.shape[1]
    query_heads = query_weight.shape[1] // HD
    kv_heads = key_weight.shape[1] // HD
    group_width = query_heads // kv_heads
    scale_factor = HD ** (-0.5)
    mixer_width = H_SSM * P_SIZE

    def as_sequences(value_tensor):
        return value_tensor.reshape(seq_count, seq_len, value_tensor.shape[-1])

    def to_rows(value_tensor):
        return value_tensor.reshape(token_count, -1).astype(jnp.bfloat16)

    tokens = block_input.astype(jnp.float32)
    first_inverse = lax.rsqrt(jnp.mean(tokens * tokens, axis=-1, keepdims=True) + epsilon)
    first_vector = first_gain.astype(jnp.float32)
    normed_share = (tokens * first_inverse * first_vector).astype(jnp.bfloat16)
    normed = gather_rows(normed_share)
    gating_pre = dense(normed, gating_weight)
    inner_pre = dense(normed, inner_weight)
    state_pre = dense(normed, state_weight)
    step_pre = dense(normed, step_weight)
    state_act, state_back = jax.vjp(
        state_piece, as_sequences(state_pre), state_conv.astype(jnp.float32)
    )
    gated, mixer_back = jax.vjp(
        mixer_piece,
        as_sequences(inner_pre),
        state_act,
        as_sequences(step_pre),
        as_sequences(gating_pre),
        inner_conv.astype(jnp.float32),
        step_bias,
        decay_log,
        skip_scale,
    )
    gated_squares = both(jnp.sum(gated * gated, axis=-1))
    mixer_inverse = lax.rsqrt(gated_squares / mixer_width + epsilon)[..., None]
    mixer_vector = mixer_gain.astype(jnp.float32)
    mixer_normed = (
        (gated * mixer_inverse * mixer_vector).astype(jnp.bfloat16).reshape(token_count, channels)
    )
    mixer_part = dense(mixer_normed, mixer_proj)
    cosine, sine_table = rope_tables(seq_len, HD)
    query_pre = dense(normed, query_weight).reshape(seq_count, seq_len, query_heads, HD)
    key_pre = dense(normed, key_weight).reshape(seq_count, seq_len, kv_heads, HD)
    value_pre = dense(normed, value_weight)
    queries = (
        rotate(query_pre, cosine, sine_table)
        .astype(jnp.bfloat16)
        .reshape(seq_count, seq_len, kv_heads, group_width, HD)
    )
    key_rows = rotate(key_pre, cosine, sine_table).astype(jnp.bfloat16)
    value_rows = value_pre.astype(jnp.bfloat16).reshape(seq_count, seq_len, kv_heads, HD)
    positions = jnp.arange(seq_len)

    def block_scores(block_start):
        query_block = queries[:, block_start : block_start + ATT_BLOCK]
        seg_block = segment_ids[:, block_start : block_start + ATT_BLOCK]
        row_index = block_start + jnp.arange(ATT_BLOCK)
        allowed = (positions[None, :] <= row_index[:, None])[None] & (
            seg_block[:, :, None] == segment_ids[:, None, :]
        )
        scores = (
            jnp.einsum(
                "sqkgd,slkd->skgql", query_block, key_rows, preferred_element_type=jnp.float32
            )
            * scale_factor
        )
        return (query_block, jnp.where(allowed[:, None, None], scores, -1e30))

    block_starts = list(range(0, seq_len, ATT_BLOCK))
    attended_blocks = []
    log_totals = []
    for block_start in block_starts:
        query_block, scores = block_scores(block_start)
        row_max = jnp.max(scores, axis=-1, keepdims=True)
        exponents = jnp.exp(scores - row_max)
        row_total = jnp.sum(exponents, axis=-1, keepdims=True)
        attn_probs = (exponents / row_total).astype(jnp.bfloat16)
        log_totals.append(row_max + jnp.log(row_total))
        attended_blocks.append(
            jnp.einsum(
                "skgql,slkd->sqkgd", attn_probs, value_rows, preferred_element_type=jnp.float32
            )
        )
    attended = (
        jnp.concatenate(attended_blocks, axis=1)
        .astype(jnp.bfloat16)
        .reshape(token_count, query_heads * HD)
    )
    attn_part = dense(attended, attention_out)
    branch_share = scatter_rows(mixer_part + attn_part)
    residual = tokens + branch_share
    second_inverse = lax.rsqrt(jnp.mean(residual * residual, axis=-1, keepdims=True) + epsilon)
    second_vector = second_gain.astype(jnp.float32)
    normed_two_share = (residual * second_inverse * second_vector).astype(jnp.bfloat16)
    normed_two = gather_rows(normed_two_share)
    full_grad = gather_rows(out_grad)
    gate_pre = dense(normed_two, gate_weight)
    up_pre = dense(normed_two, up_weight)
    gate_sigmoid = jax.nn.sigmoid(gate_pre)
    gate_act = gate_pre * gate_sigmoid
    hidden = (gate_act * up_pre).astype(jnp.bfloat16)
    ffn_share = scatter_rows(dense(hidden, down_projection_weight))
    block_output = (residual + ffn_share).astype(jnp.bfloat16)
    grad_down = row_dot(hidden, full_grad)
    grad_hidden = back_dot(full_grad, down_projection_weight)
    grad_gate_pre = (
        grad_hidden * up_pre * gate_sigmoid * (1.0 + gate_pre * (1.0 - gate_sigmoid))
    ).astype(jnp.bfloat16)
    grad_up_pre = (grad_hidden * gate_act).astype(jnp.bfloat16)
    grad_gate = row_dot(normed_two, grad_gate_pre)
    grad_up = row_dot(normed_two, grad_up_pre)
    second_back = back_dot(grad_gate_pre, gate_weight) + back_dot(grad_up_pre, up_weight)
    grad_normed_two = scatter_rows(second_back)
    grad_second_gain = jnp.sum(grad_normed_two * residual * second_inverse, axis=0)
    grad_residual = out_grad.astype(jnp.float32) + norm_back(
        grad_normed_two, residual, second_inverse, second_vector
    )
    branch_grad = gather_rows(grad_residual.astype(jnp.bfloat16))
    grad_mixer_proj = row_dot(mixer_normed, branch_grad)
    grad_mixer_normed = back_dot(branch_grad, mixer_proj).reshape(seq_count, seq_len, channels)
    grad_mixer_gain = jnp.sum(grad_mixer_normed * gated * mixer_inverse, axis=(0, 1))
    mixer_scaled = grad_mixer_normed * mixer_vector
    cross_sum = both(jnp.sum(gated * mixer_scaled, axis=-1))
    grad_gated = (
        mixer_inverse * mixer_scaled
        - gated * mixer_inverse**3 * (cross_sum / mixer_width)[..., None]
    )
    (
        grad_inner_pre,
        grad_state_act,
        grad_step_pre,
        grad_gating_pre,
        grad_inner_conv,
        grad_step_bias,
        grad_decay_log,
        grad_skip_scale,
    ) = mixer_back(grad_gated)
    grad_state_pre, grad_state_conv = state_back(grad_state_act)
    gating_rows = to_rows(grad_gating_pre)
    inner_rows = to_rows(grad_inner_pre)
    state_rows = to_rows(grad_state_pre)
    step_rows = to_rows(grad_step_pre)
    grad_attended = (
        back_dot(branch_grad, attention_out)
        .astype(jnp.bfloat16)
        .reshape(seq_count, seq_len, kv_heads, group_width, HD)
    )
    attention_output_gradient = row_dot(attended, branch_grad)
    key_gradients = jnp.zeros((seq_count, seq_len, kv_heads, HD), jnp.float32)
    grad_values = jnp.zeros((seq_count, seq_len, kv_heads, HD), jnp.float32)
    query_grads = []
    for block_index in range(len(block_starts)):
        block_start = block_starts[block_index]
        query_block, scores = block_scores(block_start)
        attn_probs = jnp.exp(scores - log_totals[block_index])
        grad_block = grad_attended[:, block_start : block_start + ATT_BLOCK]
        grad_probs = jnp.einsum(
            "sqkgd,slkd->skgql", grad_block, value_rows, preferred_element_type=jnp.float32
        )
        row_delta = jnp.sum(attn_probs * grad_probs, axis=-1, keepdims=True)
        grad_scores = (attn_probs * (grad_probs - row_delta)).astype(jnp.bfloat16)
        query_grads.append(
            jnp.einsum(
                "skgql,slkd->sqkgd", grad_scores, key_rows, preferred_element_type=jnp.float32
            )
            * scale_factor
        )
        key_gradients = (
            key_gradients
            + jnp.einsum(
                "skgql,sqkgd->slkd", grad_scores, query_block, preferred_element_type=jnp.float32
            )
            * scale_factor
        )
        grad_values = grad_values + jnp.einsum(
            "skgql,sqkgd->slkd",
            attn_probs.astype(jnp.bfloat16),
            grad_block,
            preferred_element_type=jnp.float32,
        )
    grad_query_pre = unrotate(
        jnp.concatenate(query_grads, axis=1).reshape(seq_count, seq_len, query_heads, HD),
        cosine,
        sine_table,
    )
    grad_key_pre = unrotate(key_gradients, cosine, sine_table)
    query_rows = to_rows(grad_query_pre)
    key_grad_rows = to_rows(grad_key_pre)
    value_grad_rows = to_rows(grad_values)
    first_back = (
        back_dot(gating_rows, gating_weight)
        + back_dot(inner_rows, inner_weight)
        + back_dot(step_rows, step_weight)
        + back_dot(state_rows, state_weight)
    )
    first_back = (
        first_back
        + back_dot(query_rows, query_weight)
        + back_dot(key_grad_rows, key_weight)
        + back_dot(value_grad_rows, value_weight)
    )
    grad_normed = scatter_rows(first_back)
    grad_first_gain = jnp.sum(grad_normed * tokens * first_inverse, axis=0)
    input_grad = grad_residual + norm_back(grad_normed, tokens, first_inverse, first_vector)
    model_width = normed.shape[1]
    step_padded = jnp.pad(step_rows, ((0, 0), (0, 128 - head_local)))
    input_rows = jnp.concatenate(
        [gating_rows, inner_rows, query_rows, key_grad_rows, value_grad_rows, step_padded], axis=1
    )
    grad_inputs = row_dot(normed, input_rows)
    grad_state = row_dot(normed, state_rows)
    grad_gate, grad_up, grad_down = sum_over_dp([grad_gate, grad_up, grad_down], False)
    grad_mixer_proj, attention_output_gradient = sum_over_dp(
        [grad_mixer_proj, attention_output_gradient], True
    )
    (grad_inputs,) = sum_over_dp([grad_inputs], False)
    (grad_state,) = sum_over_dp([grad_state], True, over_tensor=True)
    grad_gating, grad_inner, grad_query, grad_key, grad_value, grad_step = jnp.split(
        grad_inputs,
        [
            channels,
            2 * channels,
            2 * channels + query_heads * HD,
            2 * channels + (query_heads + kv_heads) * HD,
            2 * channels + (query_heads + 2 * kv_heads) * HD,
        ],
        axis=1,
    )
    state_width = state_weight.shape[1]
    shared_small = jnp.concatenate(
        [grad_state_conv.reshape(-1), grad_first_gain, grad_second_gain]
    )
    own_small = jnp.concatenate(
        [
            grad_inner_conv.reshape(-1),
            grad_mixer_gain,
            grad_step_bias,
            grad_decay_log,
            grad_skip_scale,
        ]
    )
    small = sum_small(jnp.concatenate([both(shared_small), own_small]))
    shared_small, own_small = small[: shared_small.shape[0]], small[shared_small.shape[0] :]
    taps = inner_conv.shape[0]
    grad_state_conv, grad_first_gain, grad_second_gain = jnp.split(
        shared_small, [taps * state_width, taps * state_width + model_width]
    )
    starts = [taps * channels, (taps + 1) * channels]
    starts = starts + [starts[1] + head_local, starts[1] + 2 * head_local]
    grad_inner_conv, grad_mixer_gain, grad_step_bias, grad_decay_log, grad_skip_scale = jnp.split(
        own_small, starts
    )
    return (
        block_output,
        input_grad,
        grad_gating,
        grad_inner,
        grad_state,
        grad_step[:, :head_local],
        grad_step_bias,
        grad_decay_log,
        grad_skip_scale,
        grad_inner_conv.reshape(taps, channels),
        grad_state_conv.reshape(taps, state_width),
        grad_mixer_gain,
        grad_mixer_proj,
        grad_query,
        grad_key,
        grad_value,
        attention_output_gradient,
        grad_first_gain,
        grad_second_gain,
        grad_gate,
        grad_up,
        grad_down,
    )


def solution(mesh):
    placed = (
        P(("dp", "tensor"), None),
        P("dp", None),
        P(("dp", "tensor"), None),
        P(None, "tensor"),
        P(None, "tensor"),
        P(),
        P(None, "tensor"),
        P("tensor"),
        P("tensor"),
        P("tensor"),
        P(None, "tensor"),
        P(),
        P("tensor"),
        P("tensor", None),
        P(None, "tensor"),
        P(None, "tensor"),
        P(None, "tensor"),
        P("tensor", None),
        P(),
        P(),
        P(None, "tensor"),
        P(None, "tensor"),
        P("tensor", None),
    )
    return jax.shard_map(
        on_device,
        mesh=mesh,
        in_specs=placed,
        out_specs=(
            P(("dp", "tensor"), None),
            P(("dp", "tensor"), None),
            P(None, "tensor"),
            P(None, "tensor"),
            P(),
            P(None, "tensor"),
            P("tensor"),
            P("tensor"),
            P("tensor"),
            P(None, "tensor"),
            P(),
            P("tensor"),
            P("tensor", None),
            P(None, "tensor"),
            P(None, "tensor"),
            P(None, "tensor"),
            P("tensor", None),
            P(),
            P(),
            P(None, "tensor"),
            P(None, "tensor"),
            P("tensor", None),
        ),
        check_vma=False,
    )
```

```python
import jax
import jax.numpy as jnp
from jax import lax
from jax.experimental import pallas as pl
from jax.experimental.pallas import tpu as pltpu
from jax.sharding import PartitionSpec as P

H_SSM = 24
P_SIZE = 64
HD = 64
SPAN = 128
ATT_BLOCK = 512
N_STATE = 128
LANES = 128


epsilon = 1e-05
rope_base = 100000000000.0
top_precision = lax.Precision.HIGHEST


def dense(left_side, right_side):
    return jnp.dot(left_side, right_side, preferred_element_type=jnp.float32)


def row_dot(left_side, right_side):
    return lax.dot_general(
        left_side, right_side, (((0,), (0,)), ((), ())), preferred_element_type=jnp.float32
    )


def back_dot(left_side, right_side):
    return lax.dot_general(
        left_side, right_side, (((1,), (1,)), ((), ())), preferred_element_type=jnp.float32
    )


def rope_tables(length, head_size):
    positions = jnp.arange(length, dtype=jnp.float32)
    frequency = rope_base ** (-jnp.arange(0, head_size, 2, dtype=jnp.float32) / head_size)
    angles = positions[:, None] * frequency[None, :]
    angles = jnp.concatenate([angles, angles], axis=-1)
    return (jnp.cos(angles)[:, None, :], jnp.sin(angles)[:, None, :])


def rotate(value_tensor, cosine, sine_table):
    half_size = value_tensor.shape[-1] // 2
    turned = jnp.concatenate(
        [-value_tensor[..., half_size:], value_tensor[..., :half_size]], axis=-1
    )
    return value_tensor * cosine + turned * sine_table


def unrotate(grad_values, cosine, sine_table):
    half_size = grad_values.shape[-1] // 2
    product = grad_values * sine_table
    turned = jnp.concatenate([product[..., half_size:], -product[..., :half_size]], axis=-1)
    return grad_values * cosine + turned


def norm_back(grad_values, value_tensor, inverse, gain_vector):
    scaled = grad_values * gain_vector
    return inverse * scaled - value_tensor * inverse**3 * jnp.mean(
        value_tensor * scaled, axis=-1, keepdims=True
    )


def swap_tensor(value):
    return lax.ppermute(value, "tensor", [(0, 1), (1, 0)])


def both(value):
    return value + swap_tensor(value)


def in_order(place, own, other):
    first = jnp.where(place == 0, own, other)
    second = jnp.where(place == 0, other, own)
    return jnp.concatenate([first, second], axis=0)


def gather_rows(share):
    return in_order(lax.axis_index("tensor"), share, swap_tensor(share))


def half_of(value, place):
    half = value.shape[0] // 2
    return lax.dynamic_slice_in_dim(value, place * half, half, 0)


def scatter_rows(partial):
    place = lax.axis_index("tensor")
    got = swap_tensor(half_of(partial, 1 - place).astype(jnp.bfloat16))
    return half_of(partial, place).astype(jnp.float32) + got.astype(jnp.float32)


def flip(value, bit):
    size = lax.axis_size("dp")
    return lax.ppermute(value, "dp", [(i, i ^ bit) for i in range(size)])


def bits_in_order(far_first):
    count = lax.axis_size("dp").bit_length() - 1
    bits = [1 << i for i in range(count)]
    return bits[:1] + bits[2:] + bits[1:2] if far_first else bits


def sum_over_dp(arrays, far_first, tensor_columns=None):
    index = lax.axis_index("dp")
    bits = bits_in_order(far_first)
    places = [(index // bit) % 2 for bit in bits]

    def joined(parts):
        return parts[0] if len(parts) == 1 else jnp.concatenate(parts, axis=0)

    current = None
    for bit, place in zip(bits, places):
        if current is None:
            keep = joined([half_of(a, place).astype(jnp.bfloat16) for a in arrays])
            send = joined([half_of(a, 1 - place).astype(jnp.bfloat16) for a in arrays])
        else:
            keep, send = half_of(current, place), half_of(current, 1 - place)
        got = flip(send, bit)
        current = (keep.astype(jnp.float32) + got.astype(jnp.float32)).astype(jnp.bfloat16)
    if tensor_columns is not None:
        start, stop = tensor_columns
        part = current[:, start:stop]
        part = (part.astype(jnp.float32) + swap_tensor(part).astype(jnp.float32)).astype(jnp.bfloat16)
        current = jnp.concatenate([current[:, :start], part, current[:, stop:]], axis=1)
    for bit, place in list(zip(bits, places))[:0:-1]:
        current = in_order(place, current, flip(current, bit))
    other = flip(current, bits[0])
    results, start = [], 0
    for a in arrays:
        rows = a.shape[0] // 2
        results.append(
            in_order(places[0], current[start : start + rows], other[start : start + rows]).astype(jnp.float32)
        )
        start += rows
    return results


def sum_small(value):
    size = lax.axis_size("dp")
    bit = 1
    while bit < size:
        value = value + flip(value, bit)
        bit *= 2
    return value


def sigmoid(v):
    return 1.0 / (1.0 + jnp.exp(-v))


def softplus(v):
    return jnp.maximum(v, 0.0) + jnp.log1p(jnp.exp(-jnp.abs(v)))


def low(v):
    return v.astype(jnp.bfloat16)


def conv_taps(ext, taps, rows):
    result = ext[5 : 5 + rows] * taps[0:1]
    for j in range(1, 4):
        result = result + ext[5 + j : 5 + j + rows] * taps[j : j + 1]
    return result


def exact_dot(left_side, right_side):
    return jnp.dot(
        left_side, right_side, preferred_element_type=jnp.float32, precision=top_precision
    )


def grid_of(rows, columns, axis):
    return lax.broadcasted_iota(jnp.int32, (rows, columns), axis)


def pair_wide(values, pair):
    rows = values.shape[0]
    low_half = jnp.broadcast_to(values[:, 2 * pair : 2 * pair + 1], (rows, LANES))
    high_half = jnp.broadcast_to(values[:, 2 * pair + 1 : 2 * pair + 2], (rows, LANES))
    return jnp.where(grid_of(rows, LANES, 1) < P_SIZE, low_half, high_half)


def split_pair(values):
    left = grid_of(values.shape[0], LANES, 1) < P_SIZE
    zero = jnp.zeros_like(values)
    return jnp.concatenate([jnp.where(left, values, zero), jnp.where(left, zero, values)], axis=0)


def step_terms(step_ref, head_ref):
    rows = step_ref.shape[0]
    shifted = step_ref[...] + head_ref[0:1]
    steps = softplus(shifted)
    rate = head_ref[1:2]
    lower = (grid_of(rows, rows, 0) >= grid_of(rows, rows, 1)).astype(jnp.float32)
    cumulative = exact_dot(lower, steps * rate)
    return shifted, steps, rate, cumulative


def mixer_forward_kernel(
    inner_ref, gating_ref, state_ref, step_ref, inner_taps_ref, state_taps_ref, head_ref, skip_ref,
    gated_ref, scanned_ref, squares_ref, saved_ref,
    inner_tail, state_tail, carry,
):
    rows, channels = inner_ref.shape

    @pl.when(pl.program_id(0) == 0)
    def _():
        inner_tail[...] = jnp.zeros_like(inner_tail)
        state_tail[...] = jnp.zeros_like(state_tail)
        carry[...] = jnp.zeros_like(carry)

    state_pre = state_ref[...]
    state_conv = conv_taps(
        jnp.concatenate([state_tail[...], state_pre], axis=0), state_taps_ref[...], rows
    )
    state_tail[...] = state_pre[rows - 8 :]
    state_act = state_conv * sigmoid(state_conv)
    in_vec = low(state_act[:, :N_STATE])
    out_vec = low(state_act[:, N_STATE:])
    in_turned = in_vec.T
    _, steps, _, cumulative = step_terms(step_ref, head_ref)
    turned = cumulative.T
    grown = jnp.exp(cumulative)
    tail_weight = jnp.exp(cumulative[rows - 1 : rows] - cumulative) * steps
    decay = grown[rows - 1 : rows]
    lower_mask = grid_of(rows, rows, 0) >= grid_of(rows, rows, 1)
    scores = back_dot(out_vec, in_vec)
    saved_ref[0] = low(carry[...])
    squares = jnp.zeros((rows, 1), jnp.float32)
    for pair in range(channels // LANES):
        lanes = slice(pair * LANES, (pair + 1) * LANES)
        inner_pre = inner_ref[:, lanes]
        conv = conv_taps(
            jnp.concatenate([inner_tail[:, lanes], inner_pre], axis=0),
            inner_taps_ref[:, lanes],
            rows,
        )
        inner_tail[:, lanes] = inner_pre[rows - 8 :]
        act = conv * sigmoid(conv)
        mixing = []
        for head in (2 * pair, 2 * pair + 1):
            gaps = cumulative[:, head : head + 1] - turned[head : head + 1, :]
            mixing.append(low(scores * jnp.exp(jnp.where(lower_mask, gaps, -1e30))))
        mixing = jnp.concatenate(mixing, axis=1)
        scanned = dense(mixing, split_pair(low(act * pair_wide(steps, pair))))
        old = carry[:, lanes]
        scanned = scanned + dense(out_vec, low(old)) * pair_wide(grown, pair)
        scanned = scanned + act * skip_ref[:, lanes]
        carry[:, lanes] = old * pair_wide(decay, pair) + dense(
            in_turned, low(act * pair_wide(tail_weight, pair))
        )
        gating = gating_ref[:, lanes]
        gated = scanned * (gating * sigmoid(gating))
        gated_ref[:, lanes] = gated
        scanned_ref[:, lanes] = low(scanned)
        squares = squares + jnp.sum(gated * gated, axis=1, keepdims=True)
    squares_ref[...] = squares


def mixer_backward_kernel(
    grad_ref, stats_ref, scanned_ref, inner_ref, inner_before_ref, gating_ref, state_ref,
    state_before_ref, step_ref, saved_ref, inner_taps_ref, state_taps_ref, head_ref, skip_ref, gain_ref,
    rows_ref, inner_sums_ref, state_sums_ref, head_sums_ref,
    inner_next, state_next, carry, turned_sums,
):
    rows, channels = inner_ref.shape
    place = pl.program_id(0)
    chunk = pl.num_programs(0) - 1 - place

    @pl.when(place == 0)
    def _():
        inner_next[...] = jnp.zeros_like(inner_next)
        state_next[...] = jnp.zeros_like(state_next)
        carry[...] = jnp.zeros_like(carry)
        inner_sums_ref[...] = jnp.zeros_like(inner_sums_ref)
        state_sums_ref[...] = jnp.zeros_like(state_sums_ref)
        head_sums_ref[...] = jnp.zeros_like(head_sums_ref)
        turned_sums[...] = jnp.zeros_like(turned_sums)

    first = chunk == 0
    state_ext = jnp.concatenate(
        [jnp.where(first, 0.0, state_before_ref[...]), state_ref[...]], axis=0
    )
    state_conv = conv_taps(state_ext, state_taps_ref[...], rows)
    state_sigmoid = sigmoid(state_conv)
    state_act = state_conv * state_sigmoid
    in_vec = low(state_act[:, :N_STATE])
    out_vec = low(state_act[:, N_STATE:])
    out_turned = out_vec.T
    shifted, steps, rate, cumulative = step_terms(step_ref, head_ref)
    turned = cumulative.T
    steps_turned = steps.T
    grown = jnp.exp(cumulative)
    fade = jnp.exp(cumulative[rows - 1 : rows] - cumulative)
    tail_weight = fade * steps
    decay = grown[rows - 1 : rows]
    row_at, column_at = grid_of(rows, rows, 0), grid_of(rows, rows, 1)
    lower_mask = row_at >= column_at
    scores = back_dot(out_vec, in_vec)
    inverse, slope = stats_ref[:, 0:1], stats_ref[:, 1:2]
    lane_at = grid_of(rows, LANES, 1)
    score_grad = jnp.zeros((rows, rows), jnp.float32)
    out_grad = jnp.zeros((rows, N_STATE), jnp.float32)
    in_grad = jnp.zeros((rows, N_STATE), jnp.float32)
    row_sums = jnp.zeros((rows, LANES), jnp.float32)
    read_sums = jnp.zeros((rows, LANES), jnp.float32)
    write_sums = jnp.zeros((rows, LANES), jnp.float32)
    state_sums = jnp.zeros((1, LANES), jnp.float32)
    segment_row, segment_column = grid_of(LANES, LANES, 0), grid_of(LANES, LANES, 1)
    first_lane = grid_of(1, LANES, 1)
    for pair in range(channels // LANES):
        lanes = slice(pair * LANES, (pair + 1) * LANES)
        inner_ext = jnp.concatenate(
            [jnp.where(first, 0.0, inner_before_ref[:, lanes]), inner_ref[:, lanes]], axis=0
        )
        taps = inner_taps_ref[:, lanes]
        conv = conv_taps(inner_ext, taps, rows)
        conv_sigmoid = sigmoid(conv)
        act = conv * conv_sigmoid
        act_low = low(act)
        gating = gating_ref[:, lanes]
        gate_sigmoid = sigmoid(gating)
        gate_act = gating * gate_sigmoid
        scanned = scanned_ref[:, lanes].astype(jnp.float32)
        gated = scanned * gate_act
        grad = grad_ref[:, lanes].astype(jnp.float32)
        gated_grad = inverse * grad * gain_ref[:, lanes] - gated * slope
        rows_ref[:, lanes] = low(
            gated_grad * scanned * gate_sigmoid * (1.0 + gating * (1.0 - gate_sigmoid))
        )
        scan_grad = gated_grad * gate_act
        gain_sum = jnp.sum(grad * gated * inverse, axis=0, keepdims=True)
        skip_sum = jnp.sum(scan_grad * act, axis=0, keepdims=True)
        blocks = split_pair(low(scan_grad))
        mixing_grad = back_dot(blocks, act_low)
        mixing = []
        for side in range(2):
            head = 2 * pair + side
            gaps = cumulative[:, head : head + 1] - turned[head : head + 1, :]
            within = jnp.exp(jnp.where(lower_mask, gaps, -1e30))
            part = mixing_grad[side * rows : (side + 1) * rows] * within
            step_row = steps_turned[head : head + 1, :]
            score_grad = score_grad + part * step_row
            product = part * scores
            turned_sums[head : head + 1, :] = jnp.sum(product, axis=0, keepdims=True)
            row_sum = jnp.sum(product * step_row, axis=1, keepdims=True)
            row_sums = jnp.where(lane_at == head, row_sum, row_sums)
            mixing.append(low(scores * within))
        act_grad = row_dot(jnp.concatenate(mixing, axis=0), blocks) * pair_wide(steps, pair)
        act_grad = act_grad + skip_ref[:, lanes] * scan_grad
        saved = saved_ref[0, :, lanes]
        later = carry[:, lanes]
        later_low = low(later)
        wide_tail = pair_wide(tail_weight, pair)
        wide_grown = pair_wide(grown, pair)
        through = dense(in_vec, later_low)
        act_grad = act_grad + wide_tail * through
        raised = low(scan_grad * wide_grown)
        to_segments = (segment_column == 2 * pair + segment_row // P_SIZE).astype(jnp.bfloat16)

        def segments(values):
            high = low(values)
            rest = low(values - high.astype(jnp.float32))
            return dense(high, to_segments) + dense(rest, to_segments)

        read_sums = read_sums + segments(scan_grad * wide_grown * dense(out_vec, saved))
        write_sums = write_sums + segments(act * through)
        overlap = jnp.sum(later * saved.astype(jnp.float32), axis=0, keepdims=True)
        left = first_lane < P_SIZE
        left_sum = jnp.sum(jnp.where(left, overlap, 0.0), axis=1, keepdims=True)
        right_sum = jnp.sum(jnp.where(left, 0.0, overlap), axis=1, keepdims=True)
        state_sums = jnp.where(first_lane == 2 * pair, left_sum, state_sums)
        state_sums = jnp.where(first_lane == 2 * pair + 1, right_sum, state_sums)
        carry[:, lanes] = later * pair_wide(decay, pair) + dense(out_turned, raised)
        out_grad = out_grad + back_dot(raised, saved)
        in_grad = in_grad + back_dot(low(act * wide_tail), later_low)
        conv_grad = act_grad * conv_sigmoid * (1.0 + conv * (1.0 - conv_sigmoid))
        ext = jnp.concatenate([conv_grad, inner_next[:, lanes]], axis=0)
        inner_next[:, lanes] = conv_grad[:8]
        pre_grad = ext[3 : 3 + rows] * taps[0:1]
        for j in range(1, 4):
            pre_grad = pre_grad + ext[3 - j : 3 - j + rows] * taps[j : j + 1]
        rows_ref[:, channels + pair * LANES : channels + (pair + 1) * LANES] = low(pre_grad)
        sums = [
            jnp.sum(conv_grad * inner_ext[5 + j : 5 + j + rows], axis=0, keepdims=True)
            for j in range(4)
        ]
        zero = jnp.zeros((2, LANES), jnp.float32)
        inner_sums_ref[:, lanes] += jnp.concatenate(sums + [gain_sum, skip_sum, zero], axis=0)

    score_low = low(score_grad)
    out_grad = out_grad + dense(score_low, in_vec)
    in_grad = in_grad + row_dot(score_low, out_vec)
    column_sums = turned_sums[...].T
    upper = (column_at >= row_at).astype(jnp.float32)
    strict = (column_at < row_at).astype(jnp.float32)
    log_grad = (
        exact_dot(upper, row_sums - steps * column_sums + read_sums)
        + exact_dot(strict, tail_weight * write_sums)
        + decay * state_sums
    )
    step_grad = column_sums + log_grad * rate + fade * write_sums
    step_pre_grad = step_grad * sigmoid(shifted)
    bias_sum = jnp.sum(step_pre_grad, axis=0, keepdims=True)
    decay_sum = jnp.sum(log_grad * steps, axis=0, keepdims=True) * rate
    head_sums_ref[...] += jnp.concatenate(
        [bias_sum, decay_sum, jnp.zeros((6, LANES), jnp.float32)], axis=0
    )
    state_grad = jnp.concatenate([in_grad, out_grad], axis=1)
    state_grad = state_grad * state_sigmoid * (1.0 + state_conv * (1.0 - state_sigmoid))
    taps = state_taps_ref[...]
    ext = jnp.concatenate([state_grad, state_next[...]], axis=0)
    state_next[...] = state_grad[:8]
    pre_grad = ext[3 : 3 + rows] * taps[0:1]
    for j in range(1, 4):
        pre_grad = pre_grad + ext[3 - j : 3 - j + rows] * taps[j : j + 1]
    width = state_grad.shape[1]
    rows_ref[:, 2 * channels : 2 * channels + width] = low(pre_grad)
    rows_ref[:, 2 * channels + width :] = low(step_pre_grad)
    sums = [
        jnp.sum(state_grad * state_ext[5 + j : 5 + j + rows], axis=0, keepdims=True)
        for j in range(4)
    ]
    state_sums_ref[...] += jnp.concatenate(sums + [jnp.zeros((4, width), jnp.float32)], axis=0)


def whole(shape):
    return pl.BlockSpec(shape, lambda i: (0,) * len(shape))


def mixer_sizes(projected, tables):
    return projected.shape[0], tables[0].shape[1], tables[1].shape[1]


def mixer_forward(projected, tables):
    length, channels, state_width = mixer_sizes(projected, tables)
    count = length // SPAN

    def rows_of(width, place=0):
        return pl.BlockSpec((SPAN, width), lambda i: (i, place))

    state_place = 2 * channels // state_width
    step_place = (2 * channels + state_width) // LANES

    return pl.pallas_call(
        mixer_forward_kernel,
        grid=(count,),
        in_specs=[
            rows_of(channels, 1), rows_of(channels), rows_of(state_width, state_place), rows_of(LANES, step_place),
            whole((8, channels)), whole((8, state_width)), whole((8, LANES)), whole((1, channels)),
        ],
        out_specs=[
            rows_of(channels), rows_of(channels), rows_of(1),
            pl.BlockSpec((1, N_STATE, channels), lambda i: (i, 0, 0)),
        ],
        out_shape=[
            jax.ShapeDtypeStruct((length, channels), jnp.float32),
            jax.ShapeDtypeStruct((length, channels), jnp.bfloat16),
            jax.ShapeDtypeStruct((length, 1), jnp.float32),
            jax.ShapeDtypeStruct((count, N_STATE, channels), jnp.bfloat16),
        ],
        scratch_shapes=[
            pltpu.VMEM((8, channels), jnp.float32),
            pltpu.VMEM((8, state_width), jnp.float32),
            pltpu.VMEM((N_STATE, channels), jnp.float32),
        ],
        compiler_params=pltpu.CompilerParams(vmem_limit_bytes=40 * 2**20),
        cost_estimate=pl.CostEstimate(
            flops=6 * 10**9, bytes_accessed=14 * 2**20, transcendentals=4 * 10**6
        ),
        name="mixer_forward",
    )(projected, projected, projected, projected, *tables)


def mixer_backward(grad, stats, scanned, projected, saved, tables, gain_wide):
    length, channels, state_width = mixer_sizes(projected, tables)
    count = length // SPAN
    total = 2 * channels + state_width + LANES

    def rows_of(width, place=0):
        return pl.BlockSpec((SPAN, width), lambda i: (count - 1 - i, place))

    def before(width, place):
        return pl.BlockSpec(
            (8, width), lambda i: (jnp.maximum((count - 1 - i) * (SPAN // 8) - 1, 0), place)
        )

    state_place = 2 * channels // state_width
    step_place = (2 * channels + state_width) // LANES

    return pl.pallas_call(
        mixer_backward_kernel,
        grid=(count,),
        in_specs=[
            rows_of(channels), rows_of(2), rows_of(channels), rows_of(channels, 1), before(channels, 1),
            rows_of(channels), rows_of(state_width, state_place), before(state_width, state_place),
            rows_of(LANES, step_place),
            pl.BlockSpec((1, N_STATE, channels), lambda i: (count - 1 - i, 0, 0)),
            whole((8, channels)), whole((8, state_width)), whole((8, LANES)), whole((1, channels)),
            whole((1, channels)),
        ],
        out_specs=[
            rows_of(total), whole((8, channels)), whole((8, state_width)), whole((8, LANES)),
        ],
        out_shape=[
            jax.ShapeDtypeStruct((length, total), jnp.bfloat16),
            jax.ShapeDtypeStruct((8, channels), jnp.float32),
            jax.ShapeDtypeStruct((8, state_width), jnp.float32),
            jax.ShapeDtypeStruct((8, LANES), jnp.float32),
        ],
        scratch_shapes=[
            pltpu.VMEM((8, channels), jnp.float32),
            pltpu.VMEM((8, state_width), jnp.float32),
            pltpu.VMEM((N_STATE, channels), jnp.float32),
            pltpu.VMEM((LANES, SPAN), jnp.float32),
        ],
        compiler_params=pltpu.CompilerParams(vmem_limit_bytes=40 * 2**20),
        cost_estimate=pl.CostEstimate(
            flops=20 * 10**9, bytes_accessed=20 * 2**20, transcendentals=8 * 10**6
        ),
        name="mixer_backward",
    )(
        grad, stats, scanned, projected, projected, projected, projected, projected, projected, saved,
        *tables, gain_wide,
    )


def on_device(
    block_input,
    segment_ids,
    out_grad,
    gating_weight,
    inner_weight,
    state_weight,
    step_weight,
    step_bias,
    decay_log,
    skip_scale,
    inner_conv,
    state_conv,
    mixer_gain,
    mixer_proj,
    query_weight,
    key_weight,
    value_weight,
    attention_out,
    first_gain,
    second_gain,
    gate_weight,
    up_weight,
    down_projection_weight,
):
    seq_count, seq_len = segment_ids.shape
    token_count = seq_count * seq_len
    channels = inner_weight.shape[1]
    head_local = step_weight.shape[1]
    query_heads = query_weight.shape[1] // HD
    kv_heads = key_weight.shape[1] // HD
    group_width = query_heads // kv_heads
    scale_factor = HD ** (-0.5)
    mixer_width = H_SSM * P_SIZE

    def as_sequences(value_tensor):
        return value_tensor.reshape(seq_count, seq_len, value_tensor.shape[-1])

    def to_rows(value_tensor):
        return value_tensor.reshape(token_count, -1).astype(jnp.bfloat16)

    tokens = block_input.astype(jnp.float32)
    first_inverse = lax.rsqrt(jnp.mean(tokens * tokens, axis=-1, keepdims=True) + epsilon)
    first_vector = first_gain.astype(jnp.float32)
    normed_share = (tokens * first_inverse * first_vector).astype(jnp.bfloat16)
    normed = gather_rows(normed_share)
    state_width = state_weight.shape[1]
    mixer_weights = jnp.concatenate(
        [gating_weight, inner_weight, state_weight, jnp.pad(step_weight, ((0, 0), (0, LANES - head_local)))],
        axis=1,
    )
    projected = dense(normed, mixer_weights)

    def eight_rows(values):
        return jnp.pad(values.astype(jnp.float32), ((0, 8 - values.shape[0]), (0, 0)))

    head_table = jnp.pad(
        jnp.stack([step_bias, -jnp.exp(decay_log)]), ((0, 6), (0, LANES - head_local))
    )
    skip_wide = jnp.repeat(skip_scale, P_SIZE)[None]
    tables = (eight_rows(inner_conv), eight_rows(state_conv), head_table, skip_wide)
    gated, scanned, squares, saved_states = mixer_forward(projected, tables)
    gated_squares = both(squares)
    mixer_inverse = lax.rsqrt(gated_squares / mixer_width + epsilon)
    mixer_vector = mixer_gain.astype(jnp.float32)
    mixer_normed = (gated * mixer_inverse * mixer_vector).astype(jnp.bfloat16)
    mixer_part = dense(mixer_normed, mixer_proj)
    cosine, sine_table = rope_tables(seq_len, HD)
    query_pre = dense(normed, query_weight).reshape(seq_count, seq_len, query_heads, HD)
    key_pre = dense(normed, key_weight).reshape(seq_count, seq_len, kv_heads, HD)
    value_pre = dense(normed, value_weight)
    queries = (
        rotate(query_pre, cosine, sine_table)
        .astype(jnp.bfloat16)
        .reshape(seq_count, seq_len, kv_heads, group_width, HD)
    )
    key_rows = rotate(key_pre, cosine, sine_table).astype(jnp.bfloat16)
    value_rows = value_pre.astype(jnp.bfloat16).reshape(seq_count, seq_len, kv_heads, HD)
    positions = jnp.arange(seq_len)

    def block_scores(block_start):
        query_block = queries[:, block_start : block_start + ATT_BLOCK]
        seg_block = segment_ids[:, block_start : block_start + ATT_BLOCK]
        row_index = block_start + jnp.arange(ATT_BLOCK)
        allowed = (positions[None, :] <= row_index[:, None])[None] & (
            seg_block[:, :, None] == segment_ids[:, None, :]
        )
        scores = (
            jnp.einsum(
                "sqkgd,slkd->skgql", query_block, key_rows, preferred_element_type=jnp.float32
            )
            * scale_factor
        )
        return (query_block, jnp.where(allowed[:, None, None], scores, -1e30))

    block_starts = list(range(0, seq_len, ATT_BLOCK))
    attended_blocks = []
    log_totals = []
    for block_start in block_starts:
        query_block, scores = block_scores(block_start)
        row_max = jnp.max(scores, axis=-1, keepdims=True)
        exponents = jnp.exp(scores - row_max)
        row_total = jnp.sum(exponents, axis=-1, keepdims=True)
        attn_probs = (exponents / row_total).astype(jnp.bfloat16)
        log_totals.append(row_max + jnp.log(row_total))
        attended_blocks.append(
            jnp.einsum(
                "skgql,slkd->sqkgd", attn_probs, value_rows, preferred_element_type=jnp.float32
            )
        )
    attended = (
        jnp.concatenate(attended_blocks, axis=1)
        .astype(jnp.bfloat16)
        .reshape(token_count, query_heads * HD)
    )
    attn_part = dense(attended, attention_out)
    branch_share = scatter_rows(mixer_part + attn_part)
    residual = tokens + branch_share
    second_inverse = lax.rsqrt(jnp.mean(residual * residual, axis=-1, keepdims=True) + epsilon)
    second_vector = second_gain.astype(jnp.float32)
    normed_two_share = (residual * second_inverse * second_vector).astype(jnp.bfloat16)
    normed_two = gather_rows(normed_two_share)
    full_grad = gather_rows(out_grad)
    gate_pre = dense(normed_two, gate_weight)
    up_pre = dense(normed_two, up_weight)
    gate_sigmoid = jax.nn.sigmoid(gate_pre)
    gate_act = gate_pre * gate_sigmoid
    hidden = (gate_act * up_pre).astype(jnp.bfloat16)
    ffn_share = scatter_rows(dense(hidden, down_projection_weight))
    block_output = (residual + ffn_share).astype(jnp.bfloat16)
    grad_down = row_dot(hidden, full_grad)
    grad_hidden = back_dot(full_grad, down_projection_weight)
    grad_gate_pre = (
        grad_hidden * up_pre * gate_sigmoid * (1.0 + gate_pre * (1.0 - gate_sigmoid))
    ).astype(jnp.bfloat16)
    grad_up_pre = (grad_hidden * gate_act).astype(jnp.bfloat16)
    grad_gate = row_dot(normed_two, grad_gate_pre)
    grad_up = row_dot(normed_two, grad_up_pre)
    second_back = back_dot(grad_gate_pre, gate_weight) + back_dot(grad_up_pre, up_weight)
    grad_normed_two = scatter_rows(second_back)
    grad_second_gain = jnp.sum(grad_normed_two * residual * second_inverse, axis=0)
    grad_residual = out_grad.astype(jnp.float32) + norm_back(
        grad_normed_two, residual, second_inverse, second_vector
    )
    branch_grad = gather_rows(grad_residual.astype(jnp.bfloat16))
    grad_mixer_proj = row_dot(mixer_normed, branch_grad)
    grad_mixer_normed = back_dot(branch_grad, mixer_proj)
    cross_sum = both(jnp.sum(gated * (grad_mixer_normed * mixer_vector), axis=-1, keepdims=True))
    stats = jnp.concatenate(
        [mixer_inverse, mixer_inverse**3 * (cross_sum / mixer_width)], axis=1
    )
    mixer_rows, inner_sums, state_sums, head_sums = mixer_backward(
        grad_mixer_normed, stats, scanned, projected, saved_states, tables, mixer_vector[None]
    )
    state_rows = mixer_rows[:, 2 * channels : 2 * channels + state_width]
    grad_attended = (
        back_dot(branch_grad, attention_out)
        .astype(jnp.bfloat16)
        .reshape(seq_count, seq_len, kv_heads, group_width, HD)
    )
    attention_output_gradient = row_dot(attended, branch_grad)
    key_gradients = jnp.zeros((seq_count, seq_len, kv_heads, HD), jnp.float32)
    grad_values = jnp.zeros((seq_count, seq_len, kv_heads, HD), jnp.float32)
    query_grads = []
    for block_index in range(len(block_starts)):
        block_start = block_starts[block_index]
        query_block, scores = block_scores(block_start)
        attn_probs = jnp.exp(scores - log_totals[block_index])
        grad_block = grad_attended[:, block_start : block_start + ATT_BLOCK]
        grad_probs = jnp.einsum(
            "sqkgd,slkd->skgql", grad_block, value_rows, preferred_element_type=jnp.float32
        )
        row_delta = jnp.sum(attn_probs * grad_probs, axis=-1, keepdims=True)
        grad_scores = (attn_probs * (grad_probs - row_delta)).astype(jnp.bfloat16)
        query_grads.append(
            jnp.einsum(
                "skgql,slkd->sqkgd", grad_scores, key_rows, preferred_element_type=jnp.float32
            )
            * scale_factor
        )
        key_gradients = (
            key_gradients
            + jnp.einsum(
                "skgql,sqkgd->slkd", grad_scores, query_block, preferred_element_type=jnp.float32
            )
            * scale_factor
        )
        grad_values = grad_values + jnp.einsum(
            "skgql,sqkgd->slkd",
            attn_probs.astype(jnp.bfloat16),
            grad_block,
            preferred_element_type=jnp.float32,
        )
    grad_query_pre = unrotate(
        jnp.concatenate(query_grads, axis=1).reshape(seq_count, seq_len, query_heads, HD),
        cosine,
        sine_table,
    )
    grad_key_pre = unrotate(key_gradients, cosine, sine_table)
    query_rows = to_rows(grad_query_pre)
    key_grad_rows = to_rows(grad_key_pre)
    value_grad_rows = to_rows(grad_values)
    first_back = back_dot(mixer_rows, mixer_weights)
    first_back = (
        first_back
        + back_dot(query_rows, query_weight)
        + back_dot(key_grad_rows, key_weight)
        + back_dot(value_grad_rows, value_weight)
    )
    grad_normed = scatter_rows(first_back)
    grad_first_gain = jnp.sum(grad_normed * tokens * first_inverse, axis=0)
    input_grad = grad_residual + norm_back(grad_normed, tokens, first_inverse, first_vector)
    model_width = normed.shape[1]
    input_rows = jnp.concatenate([mixer_rows, query_rows, key_grad_rows, value_grad_rows], axis=1)
    grad_inputs = row_dot(normed, input_rows)
    grad_gate, grad_up, grad_down = sum_over_dp([grad_gate, grad_up, grad_down], False)
    grad_mixer_proj, attention_output_gradient = sum_over_dp(
        [grad_mixer_proj, attention_output_gradient], True
    )
    state_columns = (2 * channels, 2 * channels + state_width)
    (grad_inputs,) = sum_over_dp([grad_inputs], False, state_columns)
    step_start = 2 * channels + state_width
    query_start = step_start + LANES
    key_start = query_start + query_heads * HD
    value_start = key_start + kv_heads * HD
    grad_gating, grad_inner, grad_state, grad_step, grad_query, grad_key, grad_value = jnp.split(
        grad_inputs,
        [channels, *state_columns, query_start, key_start, value_start],
        axis=1,
    )
    taps = inner_conv.shape[0]
    grad_inner_conv, grad_mixer_gain = inner_sums[:taps], inner_sums[taps]
    grad_skip_scale = jnp.sum(inner_sums[taps + 1].reshape(head_local, P_SIZE), axis=1)
    grad_state_conv = state_sums[:taps]
    grad_step_bias, grad_decay_log = head_sums[0, :head_local], head_sums[1, :head_local]
    shared_small = jnp.concatenate(
        [grad_state_conv.reshape(-1), grad_first_gain, grad_second_gain]
    )
    own_small = jnp.concatenate(
        [
            grad_inner_conv.reshape(-1),
            grad_mixer_gain,
            grad_step_bias,
            grad_decay_log,
            grad_skip_scale,
        ]
    )
    small = sum_small(jnp.concatenate([both(shared_small), own_small]))
    shared_small, own_small = small[: shared_small.shape[0]], small[shared_small.shape[0] :]
    grad_state_conv, grad_first_gain, grad_second_gain = jnp.split(
        shared_small, [taps * state_width, taps * state_width + model_width]
    )
    starts = [taps * channels, (taps + 1) * channels]
    starts = starts + [starts[1] + head_local, starts[1] + 2 * head_local]
    grad_inner_conv, grad_mixer_gain, grad_step_bias, grad_decay_log, grad_skip_scale = jnp.split(
        own_small, starts
    )
    return (
        block_output,
        input_grad,
        grad_gating,
        grad_inner,
        grad_state,
        grad_step[:, :head_local],
        grad_step_bias,
        grad_decay_log,
        grad_skip_scale,
        grad_inner_conv.reshape(taps, channels),
        grad_state_conv.reshape(taps, state_width),
        grad_mixer_gain,
        grad_mixer_proj,
        grad_query,
        grad_key,
        grad_value,
        attention_output_gradient,
        grad_first_gain,
        grad_second_gain,
        grad_gate,
        grad_up,
        grad_down,
    )


def solution(mesh):
    placed = (
        P(("dp", "tensor"), None),
        P("dp", None),
        P(("dp", "tensor"), None),
        P(None, "tensor"),
        P(None, "tensor"),
        P(),
        P(None, "tensor"),
        P("tensor"),
        P("tensor"),
        P("tensor"),
        P(None, "tensor"),
        P(),
        P("tensor"),
        P("tensor", None),
        P(None, "tensor"),
        P(None, "tensor"),
        P(None, "tensor"),
        P("tensor", None),
        P(),
        P(),
        P(None, "tensor"),
        P(None, "tensor"),
        P("tensor", None),
    )
    return jax.shard_map(
        on_device,
        mesh=mesh,
        in_specs=placed,
        out_specs=(
            P(("dp", "tensor"), None),
            P(("dp", "tensor"), None),
            P(None, "tensor"),
            P(None, "tensor"),
            P(),
            P(None, "tensor"),
            P("tensor"),
            P("tensor"),
            P("tensor"),
            P(None, "tensor"),
            P(),
            P("tensor"),
            P("tensor", None),
            P(None, "tensor"),
            P(None, "tensor"),
            P(None, "tensor"),
            P("tensor", None),
            P(),
            P(),
            P(None, "tensor"),
            P(None, "tensor"),
            P("tensor", None),
        ),
        check_vma=False,
    )
```

```python
import jax
import jax.numpy as jnp
from jax import lax
from jax.experimental import pallas as pl
from jax.experimental.pallas import tpu as pltpu
from jax.sharding import PartitionSpec as P

H_SSM = 24
P_SIZE = 64
HD = 64
SPAN = 128
QUERY_BLOCK = 256
PIECES = 2
SEG_MOST = 512
N_STATE = 128
LANES = 128


epsilon = 1e-05
rope_base = 100000000000.0
top_precision = lax.Precision.HIGHEST


def dense(left_side, right_side):
    return jnp.dot(left_side, right_side, preferred_element_type=jnp.float32)


def row_dot(left_side, right_side):
    return lax.dot_general(
        left_side, right_side, (((0,), (0,)), ((), ())), preferred_element_type=jnp.float32
    )


def back_dot(left_side, right_side):
    return lax.dot_general(
        left_side, right_side, (((1,), (1,)), ((), ())), preferred_element_type=jnp.float32
    )


def rope_tables(length):
    positions = jnp.arange(length, dtype=jnp.float32)
    frequency = rope_base ** (-jnp.arange(0, HD, 2, dtype=jnp.float32) / HD)
    angles = positions[:, None] * frequency[None, :]
    copies = [1] * (2 * LANES // HD)
    cosine, sine = jnp.cos(angles), jnp.sin(angles)
    return (
        jnp.concatenate([cosine for _ in copies], axis=1),
        jnp.concatenate([sine for _ in copies], axis=1),
    )


def norm_back(grad_values, value_tensor, inverse, gain_vector):
    scaled = grad_values * gain_vector
    return inverse * scaled - value_tensor * inverse**3 * jnp.mean(
        value_tensor * scaled, axis=-1, keepdims=True
    )


def swap_tensor(value):
    return lax.ppermute(value, "tensor", [(0, 1), (1, 0)])


def both(value):
    return value + swap_tensor(value)


def in_order(place, own, other):
    first = jnp.where(place == 0, own, other)
    second = jnp.where(place == 0, other, own)
    return jnp.concatenate([first, second], axis=0)


def gather_rows(share):
    return in_order(lax.axis_index("tensor"), share, swap_tensor(share))


def half_of(value, place):
    half = value.shape[0] // 2
    return lax.dynamic_slice_in_dim(value, place * half, half, 0)


def rows_at(value, start, count):
    return lax.dynamic_slice_in_dim(value, start, count, 0)


def swapped_sum(own, other):
    return own + swap_tensor(low(other)).astype(jnp.float32)


def flip(value, bit):
    size = lax.axis_size("dp")
    return lax.ppermute(value, "dp", [(i, i ^ bit) for i in range(size)])


def bits_in_order(far_first):
    count = lax.axis_size("dp").bit_length() - 1
    bits = [1 << i for i in range(count)]
    return bits[:1] + bits[2:] + bits[1:2] if far_first else bits


def dp_stages(whole, split=None, tensor_columns=None):
    index = lax.axis_index("dp")
    near, far = bits_in_order(False), bits_in_order(True)
    orders = [far] if split is None else [near, far]

    def place_of(bit):
        return (index // bit) % 2

    def exchange(value, bit):
        place = place_of(bit)
        return half_of(value, place), flip(half_of(value, 1 - place), bit)

    def total(keep, got):
        return low(keep.astype(jnp.float32) + got.astype(jnp.float32))

    keep, got = exchange(whole, near[0])
    (got,) = yield [got]
    share = total(keep, got)
    parts = [share] if split is None else [share[:, :split], share[:, split:]]
    for step in range(1, len(near)):
        pairs = [exchange(part, order[step]) for part, order in zip(parts, orders)]
        arrived = yield [got for _, got in pairs]
        parts = [total(keep, got) for (keep, _), got in zip(pairs, arrived)]
    if tensor_columns is not None:
        start, stop = tensor_columns
        part = parts[-1][:, start:stop]
        (got,) = yield [swap_tensor(part)]
        parts[-1] = jnp.concatenate(
            [parts[-1][:, :start], total(part, got), parts[-1][:, stop:]], axis=1
        )
    for step in range(len(near) - 1, 0, -1):
        got = [flip(part, order[step]) for part, order in zip(parts, orders)]
        got = yield got
        parts = [
            in_order(place_of(order[step]), part, other)
            for part, order, other in zip(parts, orders, got)
        ]
    share = parts[0] if split is None else jnp.concatenate(parts, axis=1)
    (got,) = yield [flip(share, near[0])]
    return in_order(place_of(near[0]), share, got)


class DpSum:
    def __init__(self, whole, split=None, tensor_columns=None):
        self.stages = dp_stages(low(whole), split, tensor_columns)
        self.arrived = next(self.stages)
        self.result = None

    def advance(self, *others):
        if self.result is not None:
            return []
        arrived = self.arrived
        flat = [one for several in others for one in several]
        if flat:
            arrived = list(lax.optimization_barrier((*arrived, *flat))[: len(arrived)])
        try:
            self.arrived = self.stages.send(arrived)
        except StopIteration as end:
            self.result = end.value
        return arrived

    def finish(self):
        while self.result is None:
            self.advance()
        return self.result


def after(value, *arrived):
    flat = [one for several in arrived for one in several]
    return lax.optimization_barrier((value, *flat))[0] if flat else value


def sum_small(value):
    size = lax.axis_size("dp")
    bit = 1
    while bit < size:
        value = value + flip(value, bit)
        bit *= 2
    return value


def sigmoid(v):
    return 1.0 / (1.0 + jnp.exp(-v))


def softplus(v):
    return jnp.maximum(v, 0.0) + jnp.log1p(jnp.exp(-jnp.abs(v)))


def low(v):
    return v.astype(jnp.bfloat16)


def conv_taps(ext, taps, rows):
    result = ext[5 : 5 + rows] * taps[0:1]
    for j in range(1, 4):
        result = result + ext[5 + j : 5 + j + rows] * taps[j : j + 1]
    return result


def exact_dot(left_side, right_side):
    return jnp.dot(
        left_side, right_side, preferred_element_type=jnp.float32, precision=top_precision
    )


def grid_of(rows, columns, axis):
    return lax.broadcasted_iota(jnp.int32, (rows, columns), axis)


def pair_wide(values, pair):
    rows = values.shape[0]
    low_half = jnp.broadcast_to(values[:, 2 * pair : 2 * pair + 1], (rows, LANES))
    high_half = jnp.broadcast_to(values[:, 2 * pair + 1 : 2 * pair + 2], (rows, LANES))
    return jnp.where(grid_of(rows, LANES, 1) < P_SIZE, low_half, high_half)


def split_pair(values):
    left = grid_of(values.shape[0], LANES, 1) < P_SIZE
    zero = jnp.zeros_like(values)
    return jnp.concatenate([jnp.where(left, values, zero), jnp.where(left, zero, values)], axis=0)


def step_terms(step_ref, head_ref):
    rows = step_ref.shape[0]
    shifted = step_ref[...] + head_ref[0:1]
    steps = softplus(shifted)
    rate = head_ref[1:2]
    lower = (grid_of(rows, rows, 0) >= grid_of(rows, rows, 1)).astype(jnp.float32)
    cumulative = exact_dot(lower, steps * rate)
    return shifted, steps, rate, cumulative


def mixer_forward_kernel(
    inner_ref, gating_ref, state_ref, step_ref, inner_taps_ref, state_taps_ref, head_ref, skip_ref,
    gated_ref, scanned_ref, squares_ref, saved_ref,
    inner_tail, state_tail, carry,
):
    rows, channels = inner_ref.shape

    @pl.when(pl.program_id(0) == 0)
    def _():
        inner_tail[...] = jnp.zeros_like(inner_tail)
        state_tail[...] = jnp.zeros_like(state_tail)
        carry[...] = jnp.zeros_like(carry)

    state_pre = state_ref[...]
    state_conv = conv_taps(
        jnp.concatenate([state_tail[...], state_pre], axis=0), state_taps_ref[...], rows
    )
    state_tail[...] = state_pre[rows - 8 :]
    state_act = state_conv * sigmoid(state_conv)
    in_vec = low(state_act[:, :N_STATE])
    out_vec = low(state_act[:, N_STATE:])
    in_turned = in_vec.T
    _, steps, _, cumulative = step_terms(step_ref, head_ref)
    turned = cumulative.T
    grown = jnp.exp(cumulative)
    tail_weight = jnp.exp(cumulative[rows - 1 : rows] - cumulative) * steps
    decay = grown[rows - 1 : rows]
    lower_mask = grid_of(rows, rows, 0) >= grid_of(rows, rows, 1)
    scores = back_dot(out_vec, in_vec)
    saved_ref[0] = low(carry[...])
    squares = jnp.zeros((rows, 1), jnp.float32)
    for pair in range(channels // LANES):
        lanes = slice(pair * LANES, (pair + 1) * LANES)
        inner_pre = inner_ref[:, lanes]
        conv = conv_taps(
            jnp.concatenate([inner_tail[:, lanes], inner_pre], axis=0),
            inner_taps_ref[:, lanes],
            rows,
        )
        inner_tail[:, lanes] = inner_pre[rows - 8 :]
        act = conv * sigmoid(conv)
        mixing = []
        for head in (2 * pair, 2 * pair + 1):
            gaps = cumulative[:, head : head + 1] - turned[head : head + 1, :]
            mixing.append(low(scores * jnp.exp(jnp.where(lower_mask, gaps, -1e30))))
        mixing = jnp.concatenate(mixing, axis=1)
        scanned = dense(mixing, split_pair(low(act * pair_wide(steps, pair))))
        old = carry[:, lanes]
        scanned = scanned + dense(out_vec, low(old)) * pair_wide(grown, pair)
        scanned = scanned + act * skip_ref[:, lanes]
        carry[:, lanes] = old * pair_wide(decay, pair) + dense(
            in_turned, low(act * pair_wide(tail_weight, pair))
        )
        gating = gating_ref[:, lanes]
        gated = scanned * (gating * sigmoid(gating))
        gated_ref[:, lanes] = gated
        scanned_ref[:, lanes] = low(scanned)
        squares = squares + jnp.sum(gated * gated, axis=1, keepdims=True)
    squares_ref[...] = squares


def mixer_backward_kernel(
    grad_ref, stats_ref, scanned_ref, inner_ref, inner_before_ref, gating_ref, state_ref,
    state_before_ref, step_ref, saved_ref, inner_taps_ref, state_taps_ref, head_ref, skip_ref, gain_ref,
    rows_ref, inner_sums_ref, state_sums_ref, head_sums_ref,
    inner_next, state_next, carry, turned_sums,
):
    rows, channels = inner_ref.shape
    place = pl.program_id(0)
    chunk = pl.num_programs(0) - 1 - place

    @pl.when(place == 0)
    def _():
        inner_next[...] = jnp.zeros_like(inner_next)
        state_next[...] = jnp.zeros_like(state_next)
        carry[...] = jnp.zeros_like(carry)
        inner_sums_ref[...] = jnp.zeros_like(inner_sums_ref)
        state_sums_ref[...] = jnp.zeros_like(state_sums_ref)
        head_sums_ref[...] = jnp.zeros_like(head_sums_ref)
        turned_sums[...] = jnp.zeros_like(turned_sums)

    first = chunk == 0
    state_ext = jnp.concatenate(
        [jnp.where(first, 0.0, state_before_ref[...]), state_ref[...]], axis=0
    )
    state_conv = conv_taps(state_ext, state_taps_ref[...], rows)
    state_sigmoid = sigmoid(state_conv)
    state_act = state_conv * state_sigmoid
    in_vec = low(state_act[:, :N_STATE])
    out_vec = low(state_act[:, N_STATE:])
    out_turned = out_vec.T
    shifted, steps, rate, cumulative = step_terms(step_ref, head_ref)
    turned = cumulative.T
    steps_turned = steps.T
    grown = jnp.exp(cumulative)
    fade = jnp.exp(cumulative[rows - 1 : rows] - cumulative)
    tail_weight = fade * steps
    decay = grown[rows - 1 : rows]
    row_at, column_at = grid_of(rows, rows, 0), grid_of(rows, rows, 1)
    lower_mask = row_at >= column_at
    scores = back_dot(out_vec, in_vec)
    inverse, slope = stats_ref[:, 0:1], stats_ref[:, 1:2]
    lane_at = grid_of(rows, LANES, 1)
    score_grad = jnp.zeros((rows, rows), jnp.float32)
    out_grad = jnp.zeros((rows, N_STATE), jnp.float32)
    in_grad = jnp.zeros((rows, N_STATE), jnp.float32)
    row_sums = jnp.zeros((rows, LANES), jnp.float32)
    read_sums = jnp.zeros((rows, LANES), jnp.float32)
    write_sums = jnp.zeros((rows, LANES), jnp.float32)
    state_sums = jnp.zeros((1, LANES), jnp.float32)
    segment_row, segment_column = grid_of(LANES, LANES, 0), grid_of(LANES, LANES, 1)
    first_lane = grid_of(1, LANES, 1)
    for pair in range(channels // LANES):
        lanes = slice(pair * LANES, (pair + 1) * LANES)
        inner_ext = jnp.concatenate(
            [jnp.where(first, 0.0, inner_before_ref[:, lanes]), inner_ref[:, lanes]], axis=0
        )
        taps = inner_taps_ref[:, lanes]
        conv = conv_taps(inner_ext, taps, rows)
        conv_sigmoid = sigmoid(conv)
        act = conv * conv_sigmoid
        act_low = low(act)
        gating = gating_ref[:, lanes]
        gate_sigmoid = sigmoid(gating)
        gate_act = gating * gate_sigmoid
        scanned = scanned_ref[:, lanes].astype(jnp.float32)
        gated = scanned * gate_act
        grad = grad_ref[:, lanes].astype(jnp.float32)
        gated_grad = inverse * grad * gain_ref[:, lanes] - gated * slope
        rows_ref[:, lanes] = low(
            gated_grad * scanned * gate_sigmoid * (1.0 + gating * (1.0 - gate_sigmoid))
        )
        scan_grad = gated_grad * gate_act
        gain_sum = jnp.sum(grad * gated * inverse, axis=0, keepdims=True)
        skip_sum = jnp.sum(scan_grad * act, axis=0, keepdims=True)
        blocks = split_pair(low(scan_grad))
        mixing_grad = back_dot(blocks, act_low)
        mixing = []
        for side in range(2):
            head = 2 * pair + side
            gaps = cumulative[:, head : head + 1] - turned[head : head + 1, :]
            within = jnp.exp(jnp.where(lower_mask, gaps, -1e30))
            part = mixing_grad[side * rows : (side + 1) * rows] * within
            step_row = steps_turned[head : head + 1, :]
            score_grad = score_grad + part * step_row
            product = part * scores
            turned_sums[head : head + 1, :] = jnp.sum(product, axis=0, keepdims=True)
            row_sum = jnp.sum(product * step_row, axis=1, keepdims=True)
            row_sums = jnp.where(lane_at == head, row_sum, row_sums)
            mixing.append(low(scores * within))
        act_grad = row_dot(jnp.concatenate(mixing, axis=0), blocks) * pair_wide(steps, pair)
        act_grad = act_grad + skip_ref[:, lanes] * scan_grad
        saved = saved_ref[0, :, lanes]
        later = carry[:, lanes]
        later_low = low(later)
        wide_tail = pair_wide(tail_weight, pair)
        wide_grown = pair_wide(grown, pair)
        through = dense(in_vec, later_low)
        act_grad = act_grad + wide_tail * through
        raised = low(scan_grad * wide_grown)
        to_segments = (segment_column == 2 * pair + segment_row // P_SIZE).astype(jnp.bfloat16)

        def segments(values):
            high = low(values)
            rest = low(values - high.astype(jnp.float32))
            return dense(high, to_segments) + dense(rest, to_segments)

        read_sums = read_sums + segments(scan_grad * wide_grown * dense(out_vec, saved))
        write_sums = write_sums + segments(act * through)
        overlap = jnp.sum(later * saved.astype(jnp.float32), axis=0, keepdims=True)
        left = first_lane < P_SIZE
        left_sum = jnp.sum(jnp.where(left, overlap, 0.0), axis=1, keepdims=True)
        right_sum = jnp.sum(jnp.where(left, 0.0, overlap), axis=1, keepdims=True)
        state_sums = jnp.where(first_lane == 2 * pair, left_sum, state_sums)
        state_sums = jnp.where(first_lane == 2 * pair + 1, right_sum, state_sums)
        carry[:, lanes] = later * pair_wide(decay, pair) + dense(out_turned, raised)
        out_grad = out_grad + back_dot(raised, saved)
        in_grad = in_grad + back_dot(low(act * wide_tail), later_low)
        conv_grad = act_grad * conv_sigmoid * (1.0 + conv * (1.0 - conv_sigmoid))
        ext = jnp.concatenate([conv_grad, inner_next[:, lanes]], axis=0)
        inner_next[:, lanes] = conv_grad[:8]
        pre_grad = ext[3 : 3 + rows] * taps[0:1]
        for j in range(1, 4):
            pre_grad = pre_grad + ext[3 - j : 3 - j + rows] * taps[j : j + 1]
        rows_ref[:, channels + pair * LANES : channels + (pair + 1) * LANES] = low(pre_grad)
        sums = [
            jnp.sum(conv_grad * inner_ext[5 + j : 5 + j + rows], axis=0, keepdims=True)
            for j in range(4)
        ]
        zero = jnp.zeros((2, LANES), jnp.float32)
        inner_sums_ref[:, lanes] += jnp.concatenate(sums + [gain_sum, skip_sum, zero], axis=0)

    score_low = low(score_grad)
    out_grad = out_grad + dense(score_low, in_vec)
    in_grad = in_grad + row_dot(score_low, out_vec)
    column_sums = turned_sums[...].T
    upper = (column_at >= row_at).astype(jnp.float32)
    strict = (column_at < row_at).astype(jnp.float32)
    log_grad = (
        exact_dot(upper, row_sums - steps * column_sums + read_sums)
        + exact_dot(strict, tail_weight * write_sums)
        + decay * state_sums
    )
    step_grad = column_sums + log_grad * rate + fade * write_sums
    step_pre_grad = step_grad * sigmoid(shifted)
    bias_sum = jnp.sum(step_pre_grad, axis=0, keepdims=True)
    decay_sum = jnp.sum(log_grad * steps, axis=0, keepdims=True) * rate
    head_sums_ref[...] += jnp.concatenate(
        [bias_sum, decay_sum, jnp.zeros((6, LANES), jnp.float32)], axis=0
    )
    state_grad = jnp.concatenate([in_grad, out_grad], axis=1)
    state_grad = state_grad * state_sigmoid * (1.0 + state_conv * (1.0 - state_sigmoid))
    taps = state_taps_ref[...]
    ext = jnp.concatenate([state_grad, state_next[...]], axis=0)
    state_next[...] = state_grad[:8]
    pre_grad = ext[3 : 3 + rows] * taps[0:1]
    for j in range(1, 4):
        pre_grad = pre_grad + ext[3 - j : 3 - j + rows] * taps[j : j + 1]
    width = state_grad.shape[1]
    rows_ref[:, 2 * channels : 2 * channels + width] = low(pre_grad)
    rows_ref[:, 2 * channels + width :] = low(step_pre_grad)
    sums = [
        jnp.sum(state_grad * state_ext[5 + j : 5 + j + rows], axis=0, keepdims=True)
        for j in range(4)
    ]
    state_sums_ref[...] += jnp.concatenate(sums + [jnp.zeros((4, width), jnp.float32)], axis=0)


def turn(values):
    first = grid_of(values.shape[0], LANES, 1) % HD < HD // 2
    ahead = pltpu.roll(values, LANES - HD // 2, 1)
    behind = pltpu.roll(values, HD // 2, 1)
    return first, ahead, behind


def rotated(values, cosine, sine):
    first, ahead, behind = turn(values)
    return values * cosine + jnp.where(first, -ahead, behind) * sine


def rotated_back(values, cosine, sine):
    first, ahead, behind = turn(values * sine)
    return values * cosine + jnp.where(first, ahead, -behind)


def doubled(pair):
    left = grid_of(pair.shape[0], LANES, 1) < HD
    turned = pltpu.roll(pair, HD, 1)
    return jnp.where(left, pair, turned), jnp.where(left, turned, pair)


def attention_blocks(length):
    for start in range(0, length, QUERY_BLOCK):
        yield start, max(0, start - SEG_MOST), start + QUERY_BLOCK


def allowed_keys(start, low_key, high_key, segment_column_ref, segment_row_ref):
    shape = (QUERY_BLOCK, high_key - low_key)
    query_at = start + lax.broadcasted_iota(jnp.int32, shape, 0)
    key_at = low_key + lax.broadcasted_iota(jnp.int32, shape, 1)
    same = segment_column_ref[start : start + QUERY_BLOCK] == segment_row_ref[:, low_key:high_key]
    return (key_at <= query_at) & same


def attention_forward_kernel(
    projected_ref, segment_column_ref, segment_row_ref, cosine_ref, sine_ref, attended_ref, totals_ref,
    keys_ref, values_ref,
):
    length, width = projected_ref.shape
    query_width = width - LANES
    key_part, value_part = doubled(projected_ref[:, query_width:])
    keys_ref[...] = low(rotated(key_part, cosine_ref[...], sine_ref[...]))
    values_ref[...] = low(value_part)
    left = grid_of(QUERY_BLOCK, LANES, 1) < HD
    for start, low_key, high_key in attention_blocks(length):
        rows = slice(start, start + QUERY_BLOCK)
        allowed = allowed_keys(start, low_key, high_key, segment_column_ref, segment_row_ref)
        keys, values = keys_ref[low_key:high_key], values_ref[low_key:high_key]
        for pair in range(query_width // LANES):
            lanes = slice(pair * LANES, (pair + 1) * LANES)
            queries = low(rotated(projected_ref[rows, lanes], cosine_ref[rows], sine_ref[rows]))
            both_heads = split_pair(queries)
            outputs = []
            for side in range(2):
                one = both_heads[side * QUERY_BLOCK : (side + 1) * QUERY_BLOCK]
                scores = jnp.where(allowed, back_dot(one, keys) * HD**-0.5, -1e30)
                row_max = jnp.max(scores, axis=1, keepdims=True)
                weights = jnp.exp(scores - row_max)
                row_total = jnp.sum(weights, axis=1, keepdims=True)
                outputs.append(dense(low(weights * (1.0 / row_total)), values))
                head = 2 * pair + side
                totals_ref[rows, head : head + 1] = row_max + jnp.log(row_total)
            attended_ref[rows, lanes] = low(jnp.where(left, outputs[0], outputs[1]))


def attention_backward_kernel(
    projected_ref, grad_ref, totals_ref, segment_column_ref, segment_row_ref, cosine_ref, sine_ref,
    rows_ref, keys_ref, values_ref, keys_grad_ref, values_grad_ref,
):
    length, width = projected_ref.shape
    query_width = width - LANES
    key_part, value_part = doubled(projected_ref[:, query_width:])
    keys_ref[...] = low(rotated(key_part, cosine_ref[...], sine_ref[...]))
    values_ref[...] = low(value_part)
    keys_grad_ref[...] = jnp.zeros_like(keys_grad_ref)
    values_grad_ref[...] = jnp.zeros_like(values_grad_ref)
    left = grid_of(QUERY_BLOCK, LANES, 1) < HD
    for start, low_key, high_key in attention_blocks(length):
        rows = slice(start, start + QUERY_BLOCK)
        allowed = allowed_keys(start, low_key, high_key, segment_column_ref, segment_row_ref)
        keys, values = keys_ref[low_key:high_key], values_ref[low_key:high_key]
        for pair in range(query_width // LANES):
            lanes = slice(pair * LANES, (pair + 1) * LANES)
            queries = low(rotated(projected_ref[rows, lanes], cosine_ref[rows], sine_ref[rows]))
            both_heads = split_pair(queries)
            both_grads = split_pair(grad_ref[rows, lanes])
            outputs = []
            for side in range(2):
                half = slice(side * QUERY_BLOCK, (side + 1) * QUERY_BLOCK)
                one, grad = both_heads[half], both_grads[half]
                head = 2 * pair + side
                scores = jnp.where(allowed, back_dot(one, keys) * HD**-0.5, -1e30)
                probs = jnp.exp(scores - totals_ref[rows, head : head + 1])
                probs_grad = back_dot(grad, values)
                delta = jnp.sum(probs * probs_grad, axis=1, keepdims=True)
                scores_grad = low(probs * (probs_grad - delta))
                outputs.append(dense(scores_grad, keys) * HD**-0.5)
                keys_grad_ref[low_key:high_key] += row_dot(scores_grad, one) * HD**-0.5
                values_grad_ref[low_key:high_key] += row_dot(low(probs), grad)
            query_grad = jnp.where(left, outputs[0], outputs[1])
            rows_ref[rows, lanes] = low(rotated_back(query_grad, cosine_ref[rows], sine_ref[rows]))
    keys_grad = keys_grad_ref[...]
    keys_grad = keys_grad + pltpu.roll(keys_grad, HD, 1)
    keys_grad = rotated_back(keys_grad, cosine_ref[...], sine_ref[...])
    values_grad = values_grad_ref[...]
    values_grad = values_grad + pltpu.roll(values_grad, HD, 1)
    left = grid_of(length, LANES, 1) < HD
    rows_ref[:, query_width:] = low(jnp.where(left, keys_grad, values_grad))


def attention_forward(projected, segment_column, segment_row, cosine, sine):
    length, width = projected.shape
    query_width = width - LANES
    return pl.pallas_call(
        attention_forward_kernel,
        out_shape=[
            jax.ShapeDtypeStruct((length, query_width), jnp.bfloat16),
            jax.ShapeDtypeStruct((length, query_width // HD), jnp.float32),
        ],
        scratch_shapes=[
            pltpu.VMEM((length, LANES), jnp.bfloat16),
            pltpu.VMEM((length, LANES), jnp.bfloat16),
        ],
        compiler_params=pltpu.CompilerParams(vmem_limit_bytes=40 * 2**20),
        cost_estimate=pl.CostEstimate(
            flops=5 * 10**9, bytes_accessed=5 * 2**20, transcendentals=3 * 10**6
        ),
        name="attention_forward",
    )(projected, segment_column, segment_row, cosine, sine)


def attention_backward(projected, grad, totals, segment_column, segment_row, cosine, sine):
    length, width = projected.shape
    return pl.pallas_call(
        attention_backward_kernel,
        out_shape=jax.ShapeDtypeStruct((length, width), jnp.bfloat16),
        scratch_shapes=[
            pltpu.VMEM((length, LANES), jnp.bfloat16),
            pltpu.VMEM((length, LANES), jnp.bfloat16),
            pltpu.VMEM((length, LANES), jnp.float32),
            pltpu.VMEM((length, LANES), jnp.float32),
        ],
        compiler_params=pltpu.CompilerParams(vmem_limit_bytes=40 * 2**20),
        cost_estimate=pl.CostEstimate(
            flops=10**10, bytes_accessed=6 * 2**20, transcendentals=3 * 10**6
        ),
        name="attention_backward",
    )(projected, grad, totals, segment_column, segment_row, cosine, sine)


def whole(shape):
    return pl.BlockSpec(shape, lambda i: (0,) * len(shape))


def mixer_sizes(projected, tables):
    return projected.shape[0], tables[0].shape[1], tables[1].shape[1]


def mixer_forward(projected, tables):
    length, channels, state_width = mixer_sizes(projected, tables)
    count = length // SPAN

    def rows_of(width, place=0):
        return pl.BlockSpec((SPAN, width), lambda i: (i, place))

    state_place = 2 * channels // state_width
    step_place = (2 * channels + state_width) // LANES

    return pl.pallas_call(
        mixer_forward_kernel,
        grid=(count,),
        in_specs=[
            rows_of(channels, 1), rows_of(channels), rows_of(state_width, state_place), rows_of(LANES, step_place),
            whole((8, channels)), whole((8, state_width)), whole((8, LANES)), whole((1, channels)),
        ],
        out_specs=[
            rows_of(channels), rows_of(channels), rows_of(1),
            pl.BlockSpec((1, N_STATE, channels), lambda i: (i, 0, 0)),
        ],
        out_shape=[
            jax.ShapeDtypeStruct((length, channels), jnp.float32),
            jax.ShapeDtypeStruct((length, channels), jnp.bfloat16),
            jax.ShapeDtypeStruct((length, 1), jnp.float32),
            jax.ShapeDtypeStruct((count, N_STATE, channels), jnp.bfloat16),
        ],
        scratch_shapes=[
            pltpu.VMEM((8, channels), jnp.float32),
            pltpu.VMEM((8, state_width), jnp.float32),
            pltpu.VMEM((N_STATE, channels), jnp.float32),
        ],
        compiler_params=pltpu.CompilerParams(vmem_limit_bytes=40 * 2**20),
        cost_estimate=pl.CostEstimate(
            flops=6 * 10**9, bytes_accessed=14 * 2**20, transcendentals=4 * 10**6
        ),
        name="mixer_forward",
    )(projected, projected, projected, projected, *tables)


def mixer_backward(grad, stats, scanned, projected, saved, tables, gain_wide):
    length, channels, state_width = mixer_sizes(projected, tables)
    count = length // SPAN
    total = 2 * channels + state_width + LANES

    def rows_of(width, place=0):
        return pl.BlockSpec((SPAN, width), lambda i: (count - 1 - i, place))

    def before(width, place):
        return pl.BlockSpec(
            (8, width), lambda i: (jnp.maximum((count - 1 - i) * (SPAN // 8) - 1, 0), place)
        )

    state_place = 2 * channels // state_width
    step_place = (2 * channels + state_width) // LANES

    return pl.pallas_call(
        mixer_backward_kernel,
        grid=(count,),
        in_specs=[
            rows_of(channels), rows_of(2), rows_of(channels), rows_of(channels, 1), before(channels, 1),
            rows_of(channels), rows_of(state_width, state_place), before(state_width, state_place),
            rows_of(LANES, step_place),
            pl.BlockSpec((1, N_STATE, channels), lambda i: (count - 1 - i, 0, 0)),
            whole((8, channels)), whole((8, state_width)), whole((8, LANES)), whole((1, channels)),
            whole((1, channels)),
        ],
        out_specs=[
            rows_of(total), whole((8, channels)), whole((8, state_width)), whole((8, LANES)),
        ],
        out_shape=[
            jax.ShapeDtypeStruct((length, total), jnp.bfloat16),
            jax.ShapeDtypeStruct((8, channels), jnp.float32),
            jax.ShapeDtypeStruct((8, state_width), jnp.float32),
            jax.ShapeDtypeStruct((8, LANES), jnp.float32),
        ],
        scratch_shapes=[
            pltpu.VMEM((8, channels), jnp.float32),
            pltpu.VMEM((8, state_width), jnp.float32),
            pltpu.VMEM((N_STATE, channels), jnp.float32),
            pltpu.VMEM((LANES, SPAN), jnp.float32),
        ],
        compiler_params=pltpu.CompilerParams(vmem_limit_bytes=40 * 2**20),
        cost_estimate=pl.CostEstimate(
            flops=20 * 10**9, bytes_accessed=20 * 2**20, transcendentals=8 * 10**6
        ),
        name="mixer_backward",
    )(
        grad, stats, scanned, projected, projected, projected, projected, projected, projected, saved,
        *tables, gain_wide,
    )


def on_device(
    block_input,
    segment_ids,
    out_grad,
    gating_weight,
    inner_weight,
    state_weight,
    step_weight,
    step_bias,
    decay_log,
    skip_scale,
    inner_conv,
    state_conv,
    mixer_gain,
    mixer_proj,
    query_weight,
    key_weight,
    value_weight,
    attention_out,
    first_gain,
    second_gain,
    gate_weight,
    up_weight,
    down_projection_weight,
):
    seq_count, seq_len = segment_ids.shape
    channels = inner_weight.shape[1]
    head_local = step_weight.shape[1]
    query_heads = query_weight.shape[1] // HD
    kv_heads = key_weight.shape[1] // HD
    mixer_width = H_SSM * P_SIZE

    tokens = block_input.astype(jnp.float32)
    first_inverse = lax.rsqrt(jnp.mean(tokens * tokens, axis=-1, keepdims=True) + epsilon)
    first_vector = first_gain.astype(jnp.float32)
    normed_share = (tokens * first_inverse * first_vector).astype(jnp.bfloat16)
    normed = gather_rows(normed_share)
    model_width = normed.shape[1]
    place = lax.axis_index("tensor")
    share_rows = tokens.shape[0]
    piece_rows = share_rows // PIECES
    other_grad = swap_tensor(after(out_grad, [normed]))
    state_width = state_weight.shape[1]
    mixer_weights = jnp.concatenate(
        [gating_weight, inner_weight, state_weight, jnp.pad(step_weight, ((0, 0), (0, LANES - head_local)))],
        axis=1,
    )
    projected = dense(normed, mixer_weights)

    def eight_rows(values):
        return jnp.pad(values.astype(jnp.float32), ((0, 8 - values.shape[0]), (0, 0)))

    head_table = jnp.pad(
        jnp.stack([step_bias, -jnp.exp(decay_log)]), ((0, 6), (0, LANES - head_local))
    )
    skip_wide = jnp.repeat(skip_scale, P_SIZE)[None]
    tables = (eight_rows(inner_conv), eight_rows(state_conv), head_table, skip_wide)
    gated, scanned, squares, saved_states = mixer_forward(projected, tables)
    gated_squares = both(squares)
    mixer_inverse = lax.rsqrt(gated_squares / mixer_width + epsilon)
    mixer_vector = mixer_gain.astype(jnp.float32)
    mixer_normed = (gated * mixer_inverse * mixer_vector).astype(jnp.bfloat16)
    cosine, sine = rope_tables(seq_len)
    segments = (segment_ids.reshape(seq_len, 1), segment_ids.reshape(1, seq_len))
    attention_weights = jnp.concatenate([query_weight, key_weight, value_weight], axis=1)
    attention_inputs = dense(normed, attention_weights)
    attended, log_totals = attention_forward(attention_inputs, *segments, cosine, sine)
    second_vector = second_gain.astype(jnp.float32)

    def branch_rows(start):
        return dense(rows_at(mixer_normed, start, piece_rows), mixer_proj) + dense(
            rows_at(attended, start, piece_rows), attention_out
        )

    def piece_of(value, piece):
        return value[piece * piece_rows : (piece + 1) * piece_rows]

    residuals, second_inverses, kept, outputs, second_grads = [], [], [], [], []
    branch_own, branch_other, first_residual_grads = [], [], []
    for piece in range(PIECES):
        offset = piece * piece_rows
        other_part = branch_rows((1 - place) * share_rows + offset)
        residual = piece_of(tokens, piece) + swapped_sum(
            branch_rows(place * share_rows + offset), other_part
        )
        inverse = lax.rsqrt(jnp.mean(residual * residual, axis=-1, keepdims=True) + epsilon)
        residuals.append(residual)
        second_inverses.append(inverse)
    normed_pieces = []
    for residual, inverse in zip(residuals, second_inverses):
        normed_own = low(residual * inverse * second_vector)
        normed_pieces.append(jnp.concatenate([normed_own, swap_tensor(normed_own)], axis=0))
    gradient_pieces = []
    for piece in range(PIECES):
        normed_two = normed_pieces[piece]
        full_grad = jnp.concatenate([piece_of(out_grad, piece), piece_of(other_grad, piece)], axis=0)
        gate_pre = dense(normed_two, gate_weight)
        up_pre = dense(normed_two, up_weight)
        gate_sigmoid = jax.nn.sigmoid(gate_pre)
        gate_act = gate_pre * gate_sigmoid
        hidden = low(gate_act * up_pre)
        grad_hidden = back_dot(full_grad, down_projection_weight)
        grad_gate_pre = low(
            grad_hidden * up_pre * gate_sigmoid * (1.0 + gate_pre * (1.0 - gate_sigmoid))
        )
        grad_up_pre = low(grad_hidden * gate_act)
        kept.append((hidden, full_grad, jnp.concatenate([grad_gate_pre, grad_up_pre], axis=1)))

        def second_back(rows):
            return back_dot(grad_gate_pre[rows], gate_weight) + back_dot(grad_up_pre[rows], up_weight)

        own, other = slice(0, piece_rows), slice(piece_rows, 2 * piece_rows)
        second_grads.append(swapped_sum(second_back(own), second_back(other)))
        outputs.append((dense(hidden[own], down_projection_weight), dense(hidden[other], down_projection_weight)))
    hidden_rows, full_rows, gate_up_rows = [jnp.concatenate(parts, axis=0) for parts in zip(*kept)]
    normed_rows = jnp.concatenate(normed_pieces, axis=0)
    ffn_grads = jnp.concatenate(
        [low(row_dot(hidden_rows, full_rows)), low(row_dot(normed_rows, gate_up_rows))], axis=1
    )
    second_grads[-1] = after(second_grads[-1], [ffn_grads])
    ffn_share = lax.psum_scatter(ffn_grads, "dp", scatter_dimension=0, tiled=True)
    ffn_sums = lax.all_gather(ffn_share, "dp", axis=0, tiled=True)
    for piece in range(PIECES):
        residual, inverse = residuals[piece], second_inverses[piece]
        grad_residual = piece_of(out_grad, piece).astype(jnp.float32) + norm_back(
            second_grads[piece], residual, inverse, second_vector
        )
        first_residual_grads.append(grad_residual)
        branch_own.append(low(grad_residual))
        branch_other.append(swap_tensor(branch_own[-1]))
    residual = jnp.concatenate(residuals, axis=0)
    grad_normed_two = jnp.concatenate(second_grads, axis=0)
    grad_second_gain = jnp.sum(
        grad_normed_two * residual * jnp.concatenate(second_inverses, axis=0), axis=0
    )
    grad_residual = jnp.concatenate(first_residual_grads, axis=0)
    branch_grad = in_order(
        place, jnp.concatenate(branch_own, axis=0), jnp.concatenate(branch_other, axis=0)
    )
    block_output = jnp.concatenate(
        [
            low(residuals[piece] + swapped_sum(own, after(other, [branch_grad])))
            for piece, (own, other) in enumerate(outputs)
        ],
        axis=0,
    )
    grad_mixer_normed = back_dot(branch_grad, mixer_proj)
    cross_part = jnp.sum(gated * (grad_mixer_normed * mixer_vector), axis=-1, keepdims=True)
    cross_sum = both(cross_part)
    grad_attended = low(back_dot(branch_grad, attention_out))
    branch_sum = DpSum(
        jnp.concatenate(
            [low(row_dot(mixer_normed, branch_grad)), low(row_dot(attended, branch_grad))], axis=0
        )
    )
    attention_rows = attention_backward(
        attention_inputs, after(grad_attended, [cross_part]), log_totals, *segments, cosine, sine
    )
    stats = jnp.concatenate(
        [mixer_inverse, mixer_inverse**3 * (cross_sum / mixer_width)], axis=1
    )
    stats = after(stats, branch_sum.advance(), [attention_rows])
    mixer_rows, inner_sums, state_sums, head_sums = mixer_backward(
        grad_mixer_normed, stats, scanned, projected, saved_states, tables, mixer_vector[None]
    )
    normed_again = after(normed, [mixer_rows])

    def first_back(start):
        return back_dot(rows_at(mixer_rows, start, share_rows), mixer_weights) + back_dot(
            rows_at(attention_rows, start, share_rows), attention_weights
        )

    grad_inputs = jnp.concatenate(
        [low(row_dot(normed_again, mixer_rows)), low(row_dot(normed_again, attention_rows))], axis=1
    )
    split = grad_inputs.shape[1] // (2 * LANES) * LANES
    input_sum = DpSum(
        grad_inputs, split, (2 * channels - split, 2 * channels + state_width - split)
    )
    mixer_rows = after(mixer_rows, [grad_inputs])
    other_part = first_back((1 - place) * share_rows)
    grad_normed = swapped_sum(first_back(place * share_rows), other_part)
    grad_first_gain = jnp.sum(grad_normed * tokens * first_inverse, axis=0)
    input_grad = grad_residual + norm_back(grad_normed, tokens, first_inverse, first_vector)
    ffn_width = gate_weight.shape[1]
    input_sum.advance(branch_sum.advance())
    input_sum.advance(branch_sum.advance())
    input_sum.advance(branch_sum.advance(), [ffn_sums])
    grad_down, grad_gate, grad_up = jnp.split(
        ffn_sums.astype(jnp.float32), [model_width, model_width + ffn_width], axis=1
    )
    input_sum.advance(branch_sum.advance())
    input_sum.advance(branch_sum.advance())
    input_sum.advance(branch_sum.advance(), [grad_down, grad_gate, grad_up])
    input_sum.advance(branch_sum.advance())
    branch_sums = branch_sum.finish().astype(jnp.float32)
    grad_mixer_proj, attention_output_gradient = branch_sums[:channels], branch_sums[channels:]
    input_sum.advance([grad_mixer_proj, attention_output_gradient])
    step_start = 2 * channels + state_width
    query_start = step_start + LANES
    key_start = query_start + query_heads * HD
    grad_gating, grad_inner, grad_state, grad_step, grad_query, grad_key, grad_value = jnp.split(
        input_sum.finish().astype(jnp.float32),
        [channels, 2 * channels, step_start, query_start, key_start, key_start + kv_heads * HD],
        axis=1,
    )
    taps = inner_conv.shape[0]
    grad_inner_conv, grad_mixer_gain = inner_sums[:taps], inner_sums[taps]
    grad_skip_scale = jnp.sum(inner_sums[taps + 1].reshape(head_local, P_SIZE), axis=1)
    grad_state_conv = state_sums[:taps]
    grad_step_bias, grad_decay_log = head_sums[0, :head_local], head_sums[1, :head_local]
    shared_small = jnp.concatenate(
        [grad_state_conv.reshape(-1), grad_first_gain, grad_second_gain]
    )
    own_small = jnp.concatenate(
        [
            grad_inner_conv.reshape(-1),
            grad_mixer_gain,
            grad_step_bias,
            grad_decay_log,
            grad_skip_scale,
        ]
    )
    small = sum_small(jnp.concatenate([both(shared_small), own_small]))
    shared_small, own_small = small[: shared_small.shape[0]], small[shared_small.shape[0] :]
    grad_state_conv, grad_first_gain, grad_second_gain = jnp.split(
        shared_small, [taps * state_width, taps * state_width + model_width]
    )
    starts = [taps * channels, (taps + 1) * channels]
    starts = starts + [starts[1] + head_local, starts[1] + 2 * head_local]
    grad_inner_conv, grad_mixer_gain, grad_step_bias, grad_decay_log, grad_skip_scale = jnp.split(
        own_small, starts
    )
    return (
        block_output,
        input_grad,
        grad_gating,
        grad_inner,
        grad_state,
        grad_step[:, :head_local],
        grad_step_bias,
        grad_decay_log,
        grad_skip_scale,
        grad_inner_conv.reshape(taps, channels),
        grad_state_conv.reshape(taps, state_width),
        grad_mixer_gain,
        grad_mixer_proj,
        grad_query,
        grad_key,
        grad_value,
        attention_output_gradient,
        grad_first_gain,
        grad_second_gain,
        grad_gate,
        grad_up,
        grad_down,
    )


def solution(mesh):
    placed = (
        P(("dp", "tensor"), None),
        P("dp", None),
        P(("dp", "tensor"), None),
        P(None, "tensor"),
        P(None, "tensor"),
        P(),
        P(None, "tensor"),
        P("tensor"),
        P("tensor"),
        P("tensor"),
        P(None, "tensor"),
        P(),
        P("tensor"),
        P("tensor", None),
        P(None, "tensor"),
        P(None, "tensor"),
        P(None, "tensor"),
        P("tensor", None),
        P(),
        P(),
        P(None, "tensor"),
        P(None, "tensor"),
        P("tensor", None),
    )
    return jax.shard_map(
        on_device,
        mesh=mesh,
        in_specs=placed,
        out_specs=(
            P(("dp", "tensor"), None),
            P(("dp", "tensor"), None),
            P(None, "tensor"),
            P(None, "tensor"),
            P(),
            P(None, "tensor"),
            P("tensor"),
            P("tensor"),
            P("tensor"),
            P(None, "tensor"),
            P(),
            P("tensor"),
            P("tensor", None),
            P(None, "tensor"),
            P(None, "tensor"),
            P(None, "tensor"),
            P("tensor", None),
            P(),
            P(),
            P(None, "tensor"),
            P(None, "tensor"),
            P("tensor", None),
        ),
        check_vma=False,
    )
```

```python
import functools

import jax
import jax.numpy as jnp
from jax import lax
from jax.experimental import pallas as pl
from jax.experimental.pallas import tpu as pltpu
from jax.sharding import PartitionSpec as P

H_SSM = 24
P_SIZE = 64
HD = 64
SPAN = 128
QUERY_BLOCK = 256
PIECES = 2
SEG_MOST = 512
N_STATE = 128
LANES = 128


epsilon = 1e-05
rope_base = 100000000000.0
top_precision = lax.Precision.HIGHEST


def dense(left_side, right_side):
    return jnp.dot(left_side, right_side, preferred_element_type=jnp.float32)


def row_dot(left_side, right_side):
    return lax.dot_general(
        left_side, right_side, (((0,), (0,)), ((), ())), preferred_element_type=jnp.float32
    )


def back_dot(left_side, right_side):
    return lax.dot_general(
        left_side, right_side, (((1,), (1,)), ((), ())), preferred_element_type=jnp.float32
    )


def rope_tables(length):
    positions = jnp.arange(length, dtype=jnp.float32)
    frequency = rope_base ** (-jnp.arange(0, HD, 2, dtype=jnp.float32) / HD)
    angles = positions[:, None] * frequency[None, :]
    copies = [1] * (2 * LANES // HD)
    cosine, sine = jnp.cos(angles), jnp.sin(angles)
    return (
        jnp.concatenate([cosine for _ in copies], axis=1),
        jnp.concatenate([sine for _ in copies], axis=1),
    )


def norm_back(grad_values, value_tensor, inverse, gain_vector):
    scaled = grad_values * gain_vector
    return inverse * scaled - value_tensor * inverse**3 * jnp.mean(
        value_tensor * scaled, axis=-1, keepdims=True
    )


def swap_tensor(value):
    return lax.ppermute(value, "tensor", [(0, 1), (1, 0)])


def both(value):
    return value + swap_tensor(value)


def in_order(place, own, other):
    first = jnp.where(place == 0, own, other)
    second = jnp.where(place == 0, other, own)
    return jnp.concatenate([first, second], axis=0)


def gather_rows(share):
    return in_order(lax.axis_index("tensor"), share, swap_tensor(share))


def half_of(value, place):
    half = value.shape[0] // 2
    return lax.dynamic_slice_in_dim(value, place * half, half, 0)


def rows_at(value, start, count):
    return lax.dynamic_slice_in_dim(value, start, count, 0)


def swapped_sum(own, other):
    return own + swap_tensor(low(other)).astype(jnp.float32)


def flip(value, bit):
    size = lax.axis_size("dp")
    return lax.ppermute(value, "dp", [(i, i ^ bit) for i in range(size)])


def bits_in_order(far_first):
    count = lax.axis_size("dp").bit_length() - 1
    bits = [1 << i for i in range(count)]
    return bits[:1] + bits[2:] + bits[1:2] if far_first else bits


def dp_stages(whole, split=None, tensor_columns=None):
    index = lax.axis_index("dp")
    near, far = bits_in_order(False), bits_in_order(True)
    orders = [far] if split is None else [near, far]

    def place_of(bit):
        return (index // bit) % 2

    def exchange(value, bit):
        place = place_of(bit)
        return half_of(value, place), flip(half_of(value, 1 - place), bit)

    def total(keep, got):
        return low(keep.astype(jnp.float32) + got.astype(jnp.float32))

    keep, got = exchange(whole, near[0])
    (got,) = yield [got]
    share = total(keep, got)
    parts = [share] if split is None else [share[:, :split], share[:, split:]]
    for step in range(1, len(near)):
        pairs = [exchange(part, order[step]) for part, order in zip(parts, orders)]
        arrived = yield [got for _, got in pairs]
        parts = [total(keep, got) for (keep, _), got in zip(pairs, arrived)]
    if tensor_columns is not None:
        start, stop = tensor_columns
        part = parts[-1][:, start:stop]
        (got,) = yield [swap_tensor(part)]
        parts[-1] = jnp.concatenate(
            [parts[-1][:, :start], total(part, got), parts[-1][:, stop:]], axis=1
        )
    for step in range(len(near) - 1, 0, -1):
        got = [flip(part, order[step]) for part, order in zip(parts, orders)]
        got = yield got
        parts = [
            in_order(place_of(order[step]), part, other)
            for part, order, other in zip(parts, orders, got)
        ]
    share = parts[0] if split is None else jnp.concatenate(parts, axis=1)
    (got,) = yield [flip(share, near[0])]
    if split is not None:
        return share, got, place_of(near[0])
    return in_order(place_of(near[0]), share, got)


def unpack_kernel(starts, place_ref, own_ref, other_ref, *output_refs):
    half = pl.program_id(0) // (pl.num_programs(0) // 2)
    values = jnp.where(half == place_ref[0], own_ref[...], other_ref[...]).astype(jnp.float32)
    for start, output_ref in zip(starts, output_refs):
        output_ref[...] = values[:, start : start + output_ref.shape[1]]


def unpack(own, other, place, columns):
    half_rows, width = own.shape
    steps = half_rows // SPAN
    rows = pl.BlockSpec((SPAN, width), lambda i: (i % steps, 0))
    return pl.pallas_call(
        functools.partial(unpack_kernel, [start for start, _ in columns]),
        grid=(2 * steps,),
        in_specs=[pl.BlockSpec(memory_space=pltpu.SMEM), rows, rows],
        out_specs=[pl.BlockSpec((SPAN, size), lambda i: (i, 0)) for _, size in columns],
        out_shape=[jax.ShapeDtypeStruct((2 * half_rows, size), jnp.float32) for _, size in columns],
        compiler_params=pltpu.CompilerParams(vmem_limit_bytes=40 * 2**20),
        cost_estimate=pl.CostEstimate(
            flops=0, bytes_accessed=16 * half_rows * width, transcendentals=0
        ),
        name="unpack",
    )(place.reshape(1).astype(jnp.int32), own, other)


class DpSum:
    def __init__(self, whole, split=None, tensor_columns=None):
        self.stages = dp_stages(low(whole), split, tensor_columns)
        self.arrived = next(self.stages)
        self.result = None

    def advance(self, *others):
        if self.result is not None:
            return []
        arrived = self.arrived
        flat = [one for several in others for one in several]
        if flat:
            arrived = list(lax.optimization_barrier((*arrived, *flat))[: len(arrived)])
        try:
            self.arrived = self.stages.send(arrived)
        except StopIteration as end:
            self.result = end.value
        return arrived

    def finish(self):
        while self.result is None:
            self.advance()
        return self.result


def after(value, *arrived):
    flat = [one for several in arrived for one in several]
    return lax.optimization_barrier((value, *flat))[0] if flat else value


def sigmoid(v):
    return 1.0 / (1.0 + jnp.exp(-v))


def softplus(v):
    return jnp.maximum(v, 0.0) + jnp.log1p(jnp.exp(-jnp.abs(v)))


def low(v):
    return v.astype(jnp.bfloat16)


def conv_taps(ext, taps, rows):
    result = ext[5 : 5 + rows] * taps[0:1]
    for j in range(1, 4):
        result = result + ext[5 + j : 5 + j + rows] * taps[j : j + 1]
    return result


def exact_dot(left_side, right_side):
    return jnp.dot(
        left_side, right_side, preferred_element_type=jnp.float32, precision=top_precision
    )


def grid_of(rows, columns, axis):
    return lax.broadcasted_iota(jnp.int32, (rows, columns), axis)


def pair_wide(values, pair):
    rows = values.shape[0]
    low_half = jnp.broadcast_to(values[:, 2 * pair : 2 * pair + 1], (rows, LANES))
    high_half = jnp.broadcast_to(values[:, 2 * pair + 1 : 2 * pair + 2], (rows, LANES))
    return jnp.where(grid_of(rows, LANES, 1) < P_SIZE, low_half, high_half)


def split_pair(values):
    left = grid_of(values.shape[0], LANES, 1) < P_SIZE
    zero = jnp.zeros_like(values)
    return jnp.concatenate([jnp.where(left, values, zero), jnp.where(left, zero, values)], axis=0)


def step_terms(step_ref, head_ref):
    rows = step_ref.shape[0]
    shifted = step_ref[...] + head_ref[0:1]
    steps = softplus(shifted)
    rate = head_ref[1:2]
    lower = (grid_of(rows, rows, 0) >= grid_of(rows, rows, 1)).astype(jnp.float32)
    cumulative = exact_dot(lower, steps * rate)
    return shifted, steps, rate, cumulative


def mixer_forward_kernel(
    inner_ref, gating_ref, state_ref, step_ref, inner_taps_ref, state_taps_ref, head_ref, skip_ref,
    gated_ref, scanned_ref, squares_ref, saved_ref,
    inner_tail, state_tail, carry, written,
):
    rows, channels = inner_ref.shape

    @pl.when(pl.program_id(0) == 0)
    def _():
        inner_tail[...] = jnp.zeros_like(inner_tail)
        state_tail[...] = jnp.zeros_like(state_tail)
        carry[...] = jnp.zeros_like(carry)

    state_pre = state_ref[...]
    state_conv = conv_taps(
        jnp.concatenate([state_tail[...], state_pre], axis=0), state_taps_ref[...], rows
    )
    state_tail[...] = state_pre[rows - 8 :]
    state_act = state_conv * sigmoid(state_conv)
    in_vec = low(state_act[:, :N_STATE])
    out_vec = low(state_act[:, N_STATE:])
    in_turned = in_vec.T
    _, steps, _, cumulative = step_terms(step_ref, head_ref)
    turned = cumulative.T
    grown = jnp.exp(cumulative)
    tail_weight = jnp.exp(cumulative[rows - 1 : rows] - cumulative) * steps
    decay = grown[rows - 1 : rows]
    lower_mask = grid_of(rows, rows, 0) >= grid_of(rows, rows, 1)
    scores = back_dot(out_vec, in_vec)
    saved = low(carry[...])
    saved_ref[0] = saved
    from_state = dense(out_vec, saved)
    squares = jnp.zeros((rows, 1), jnp.float32)
    for pair in range(channels // LANES):
        lanes = slice(pair * LANES, (pair + 1) * LANES)
        inner_pre = inner_ref[:, lanes]
        conv = conv_taps(
            jnp.concatenate([inner_tail[:, lanes], inner_pre], axis=0),
            inner_taps_ref[:, lanes],
            rows,
        )
        inner_tail[:, lanes] = inner_pre[rows - 8 :]
        act = conv * sigmoid(conv)
        mixing = []
        for head in (2 * pair, 2 * pair + 1):
            gaps = cumulative[:, head : head + 1] - turned[head : head + 1, :]
            mixing.append(low(scores * jnp.exp(jnp.where(lower_mask, gaps, -1e30))))
        mixing = jnp.concatenate(mixing, axis=1)
        scanned = dense(mixing, split_pair(low(act * pair_wide(steps, pair))))
        scanned = scanned + from_state[:, lanes] * pair_wide(grown, pair)
        scanned = scanned + act * skip_ref[:, lanes]
        written[:, lanes] = low(act * pair_wide(tail_weight, pair))
        gating = gating_ref[:, lanes]
        gated = scanned * (gating * sigmoid(gating))
        gated_ref[:, lanes] = gated
        scanned_ref[:, lanes] = low(scanned)
        squares = squares + jnp.sum(gated * gated, axis=1, keepdims=True)
    squares_ref[...] = squares
    update = dense(in_turned, written[...])
    for pair in range(channels // LANES):
        lanes = slice(pair * LANES, (pair + 1) * LANES)
        carry[:, lanes] = carry[:, lanes] * pair_wide(decay, pair) + update[:, lanes]


def mixer_backward_kernel(
    grad_ref, stats_ref, scanned_ref, inner_ref, inner_before_ref, gating_ref, state_ref,
    state_before_ref, step_ref, saved_ref, inner_taps_ref, state_taps_ref, head_ref, skip_ref, gain_ref,
    rows_ref, inner_sums_ref, state_sums_ref, head_sums_ref,
    inner_next, state_next, carry, turned_sums,
):
    rows, channels = inner_ref.shape
    place = pl.program_id(0)
    chunk = pl.num_programs(0) - 1 - place

    @pl.when(place == 0)
    def _():
        inner_next[...] = jnp.zeros_like(inner_next)
        state_next[...] = jnp.zeros_like(state_next)
        carry[...] = jnp.zeros_like(carry)
        inner_sums_ref[...] = jnp.zeros_like(inner_sums_ref)
        state_sums_ref[...] = jnp.zeros_like(state_sums_ref)
        head_sums_ref[...] = jnp.zeros_like(head_sums_ref)
        turned_sums[...] = jnp.zeros_like(turned_sums)

    first = chunk == 0
    state_ext = jnp.concatenate(
        [jnp.where(first, 0.0, state_before_ref[...]), state_ref[...]], axis=0
    )
    state_conv = conv_taps(state_ext, state_taps_ref[...], rows)
    state_sigmoid = sigmoid(state_conv)
    state_act = state_conv * state_sigmoid
    in_vec = low(state_act[:, :N_STATE])
    out_vec = low(state_act[:, N_STATE:])
    out_turned = out_vec.T
    shifted, steps, rate, cumulative = step_terms(step_ref, head_ref)
    turned = cumulative.T
    steps_turned = steps.T
    grown = jnp.exp(cumulative)
    fade = jnp.exp(cumulative[rows - 1 : rows] - cumulative)
    tail_weight = fade * steps
    decay = grown[rows - 1 : rows]
    row_at, column_at = grid_of(rows, rows, 0), grid_of(rows, rows, 1)
    lower_mask = row_at >= column_at
    scores = back_dot(out_vec, in_vec)
    inverse, slope = stats_ref[:, 0:1], stats_ref[:, 1:2]
    lane_at = grid_of(rows, LANES, 1)
    score_grad = jnp.zeros((rows, rows), jnp.float32)
    out_grad = jnp.zeros((rows, N_STATE), jnp.float32)
    in_grad = jnp.zeros((rows, N_STATE), jnp.float32)
    row_sums = jnp.zeros((rows, LANES), jnp.float32)
    read_sums = jnp.zeros((rows, LANES), jnp.float32)
    write_sums = jnp.zeros((rows, LANES), jnp.float32)
    state_sums = jnp.zeros((1, LANES), jnp.float32)
    segment_row, segment_column = grid_of(LANES, LANES, 0), grid_of(LANES, LANES, 1)
    first_lane = grid_of(1, LANES, 1)
    for pair in range(channels // LANES):
        lanes = slice(pair * LANES, (pair + 1) * LANES)
        inner_ext = jnp.concatenate(
            [jnp.where(first, 0.0, inner_before_ref[:, lanes]), inner_ref[:, lanes]], axis=0
        )
        taps = inner_taps_ref[:, lanes]
        conv = conv_taps(inner_ext, taps, rows)
        conv_sigmoid = sigmoid(conv)
        act = conv * conv_sigmoid
        act_low = low(act)
        gating = gating_ref[:, lanes]
        gate_sigmoid = sigmoid(gating)
        gate_act = gating * gate_sigmoid
        scanned = scanned_ref[:, lanes].astype(jnp.float32)
        gated = scanned * gate_act
        grad = grad_ref[:, lanes].astype(jnp.float32)
        gated_grad = inverse * grad * gain_ref[:, lanes] - gated * slope
        rows_ref[:, lanes] = low(
            gated_grad * scanned * gate_sigmoid * (1.0 + gating * (1.0 - gate_sigmoid))
        )
        scan_grad = gated_grad * gate_act
        gain_sum = jnp.sum(grad * gated * inverse, axis=0, keepdims=True)
        skip_sum = jnp.sum(scan_grad * act, axis=0, keepdims=True)
        blocks = split_pair(low(scan_grad))
        mixing_grad = back_dot(blocks, act_low)
        mixing = []
        for side in range(2):
            head = 2 * pair + side
            gaps = cumulative[:, head : head + 1] - turned[head : head + 1, :]
            within = jnp.exp(jnp.where(lower_mask, gaps, -1e30))
            part = mixing_grad[side * rows : (side + 1) * rows] * within
            step_row = steps_turned[head : head + 1, :]
            score_grad = score_grad + part * step_row
            product = part * scores
            turned_sums[head : head + 1, :] = jnp.sum(product, axis=0, keepdims=True)
            row_sum = jnp.sum(product * step_row, axis=1, keepdims=True)
            row_sums = jnp.where(lane_at == head, row_sum, row_sums)
            mixing.append(low(scores * within))
        act_grad = row_dot(jnp.concatenate(mixing, axis=0), blocks) * pair_wide(steps, pair)
        act_grad = act_grad + skip_ref[:, lanes] * scan_grad
        saved = saved_ref[0, :, lanes]
        later = carry[:, lanes]
        later_low = low(later)
        wide_tail = pair_wide(tail_weight, pair)
        wide_grown = pair_wide(grown, pair)
        through = dense(in_vec, later_low)
        act_grad = act_grad + wide_tail * through
        raised = low(scan_grad * wide_grown)
        to_segments = (segment_column == 2 * pair + segment_row // P_SIZE).astype(jnp.bfloat16)

        def segments(values):
            high = low(values)
            rest = low(values - high.astype(jnp.float32))
            return dense(high, to_segments) + dense(rest, to_segments)

        read_sums = read_sums + segments(scan_grad * wide_grown * dense(out_vec, saved))
        write_sums = write_sums + segments(act * through)
        overlap = jnp.sum(later * saved.astype(jnp.float32), axis=0, keepdims=True)
        left = first_lane < P_SIZE
        left_sum = jnp.sum(jnp.where(left, overlap, 0.0), axis=1, keepdims=True)
        right_sum = jnp.sum(jnp.where(left, 0.0, overlap), axis=1, keepdims=True)
        state_sums = jnp.where(first_lane == 2 * pair, left_sum, state_sums)
        state_sums = jnp.where(first_lane == 2 * pair + 1, right_sum, state_sums)
        carry[:, lanes] = later * pair_wide(decay, pair) + dense(out_turned, raised)
        out_grad = out_grad + back_dot(raised, saved)
        in_grad = in_grad + back_dot(low(act * wide_tail), later_low)
        conv_grad = act_grad * conv_sigmoid * (1.0 + conv * (1.0 - conv_sigmoid))
        ext = jnp.concatenate([conv_grad, inner_next[:, lanes]], axis=0)
        inner_next[:, lanes] = conv_grad[:8]
        pre_grad = ext[3 : 3 + rows] * taps[0:1]
        for j in range(1, 4):
            pre_grad = pre_grad + ext[3 - j : 3 - j + rows] * taps[j : j + 1]
        rows_ref[:, channels + pair * LANES : channels + (pair + 1) * LANES] = low(pre_grad)
        sums = [
            jnp.sum(conv_grad * inner_ext[5 + j : 5 + j + rows], axis=0, keepdims=True)
            for j in range(4)
        ]
        zero = jnp.zeros((2, LANES), jnp.float32)
        inner_sums_ref[:, lanes] += jnp.concatenate(sums + [gain_sum, skip_sum, zero], axis=0)

    score_low = low(score_grad)
    out_grad = out_grad + dense(score_low, in_vec)
    in_grad = in_grad + row_dot(score_low, out_vec)
    column_sums = turned_sums[...].T
    upper = (column_at >= row_at).astype(jnp.float32)
    strict = (column_at < row_at).astype(jnp.float32)
    log_grad = (
        exact_dot(upper, row_sums - steps * column_sums + read_sums)
        + exact_dot(strict, tail_weight * write_sums)
        + decay * state_sums
    )
    step_grad = column_sums + log_grad * rate + fade * write_sums
    step_pre_grad = step_grad * sigmoid(shifted)
    bias_sum = jnp.sum(step_pre_grad, axis=0, keepdims=True)
    decay_sum = jnp.sum(log_grad * steps, axis=0, keepdims=True) * rate
    head_sums_ref[...] += jnp.concatenate(
        [bias_sum, decay_sum, jnp.zeros((6, LANES), jnp.float32)], axis=0
    )
    state_grad = jnp.concatenate([in_grad, out_grad], axis=1)
    state_grad = state_grad * state_sigmoid * (1.0 + state_conv * (1.0 - state_sigmoid))
    taps = state_taps_ref[...]
    ext = jnp.concatenate([state_grad, state_next[...]], axis=0)
    state_next[...] = state_grad[:8]
    pre_grad = ext[3 : 3 + rows] * taps[0:1]
    for j in range(1, 4):
        pre_grad = pre_grad + ext[3 - j : 3 - j + rows] * taps[j : j + 1]
    width = state_grad.shape[1]
    rows_ref[:, 2 * channels : 2 * channels + width] = low(pre_grad)
    rows_ref[:, 2 * channels + width :] = low(step_pre_grad)
    sums = [
        jnp.sum(state_grad * state_ext[5 + j : 5 + j + rows], axis=0, keepdims=True)
        for j in range(4)
    ]
    state_sums_ref[...] += jnp.concatenate(sums + [jnp.zeros((4, width), jnp.float32)], axis=0)


def turn(values):
    first = grid_of(values.shape[0], LANES, 1) % HD < HD // 2
    ahead = pltpu.roll(values, LANES - HD // 2, 1)
    behind = pltpu.roll(values, HD // 2, 1)
    return first, ahead, behind


def rotated(values, cosine, sine):
    first, ahead, behind = turn(values)
    return values * cosine + jnp.where(first, -ahead, behind) * sine


def rotated_back(values, cosine, sine):
    first, ahead, behind = turn(values * sine)
    return values * cosine + jnp.where(first, ahead, -behind)


def doubled(pair):
    left = grid_of(pair.shape[0], LANES, 1) < HD
    turned = pltpu.roll(pair, HD, 1)
    return jnp.where(left, pair, turned), jnp.where(left, turned, pair)


def attention_blocks(length):
    for start in range(0, length, QUERY_BLOCK):
        yield start, max(0, start - SEG_MOST), start + QUERY_BLOCK


def allowed_keys(start, low_key, high_key, segment_column_ref, segment_row_ref):
    shape = (QUERY_BLOCK, high_key - low_key)
    query_at = start + lax.broadcasted_iota(jnp.int32, shape, 0)
    key_at = low_key + lax.broadcasted_iota(jnp.int32, shape, 1)
    same = segment_column_ref[start : start + QUERY_BLOCK] == segment_row_ref[:, low_key:high_key]
    return (key_at <= query_at) & same


def attention_forward_kernel(
    projected_ref, segment_column_ref, segment_row_ref, cosine_ref, sine_ref, attended_ref, totals_ref,
    keys_ref, values_ref,
):
    length, width = projected_ref.shape
    query_width = width - LANES
    key_part, value_part = doubled(projected_ref[:, query_width:])
    keys_ref[...] = low(rotated(key_part, cosine_ref[...], sine_ref[...]))
    values_ref[...] = low(value_part)
    left = grid_of(QUERY_BLOCK, LANES, 1) < HD
    for start, low_key, high_key in attention_blocks(length):
        rows = slice(start, start + QUERY_BLOCK)
        allowed = allowed_keys(start, low_key, high_key, segment_column_ref, segment_row_ref)
        keys, values = keys_ref[low_key:high_key], values_ref[low_key:high_key]
        for pair in range(query_width // LANES):
            lanes = slice(pair * LANES, (pair + 1) * LANES)
            queries = low(rotated(projected_ref[rows, lanes], cosine_ref[rows], sine_ref[rows]))
            both_heads = split_pair(queries)
            outputs = []
            for side in range(2):
                one = both_heads[side * QUERY_BLOCK : (side + 1) * QUERY_BLOCK]
                scores = jnp.where(allowed, back_dot(one, keys) * HD**-0.5, -1e30)
                row_max = jnp.max(scores, axis=1, keepdims=True)
                weights = jnp.exp(scores - row_max)
                row_total = jnp.sum(weights, axis=1, keepdims=True)
                outputs.append(dense(low(weights * (1.0 / row_total)), values))
                head = 2 * pair + side
                totals_ref[rows, head : head + 1] = row_max + jnp.log(row_total)
            attended_ref[rows, lanes] = low(jnp.where(left, outputs[0], outputs[1]))


def attention_backward_kernel(
    projected_ref, grad_ref, totals_ref, segment_column_ref, segment_row_ref, cosine_ref, sine_ref,
    rows_ref, keys_ref, values_ref, keys_grad_ref, values_grad_ref,
):
    length, width = projected_ref.shape
    query_width = width - LANES
    key_part, value_part = doubled(projected_ref[:, query_width:])
    keys_ref[...] = low(rotated(key_part, cosine_ref[...], sine_ref[...]))
    values_ref[...] = low(value_part)
    keys_grad_ref[...] = jnp.zeros_like(keys_grad_ref)
    values_grad_ref[...] = jnp.zeros_like(values_grad_ref)
    left = grid_of(QUERY_BLOCK, LANES, 1) < HD
    for start, low_key, high_key in attention_blocks(length):
        rows = slice(start, start + QUERY_BLOCK)
        allowed = allowed_keys(start, low_key, high_key, segment_column_ref, segment_row_ref)
        keys, values = keys_ref[low_key:high_key], values_ref[low_key:high_key]
        for pair in range(query_width // LANES):
            lanes = slice(pair * LANES, (pair + 1) * LANES)
            queries = low(rotated(projected_ref[rows, lanes], cosine_ref[rows], sine_ref[rows]))
            both_heads = split_pair(queries)
            both_grads = split_pair(grad_ref[rows, lanes])
            outputs = []
            for side in range(2):
                half = slice(side * QUERY_BLOCK, (side + 1) * QUERY_BLOCK)
                one, grad = both_heads[half], both_grads[half]
                head = 2 * pair + side
                scores = jnp.where(allowed, back_dot(one, keys) * HD**-0.5, -1e30)
                probs = jnp.exp(scores - totals_ref[rows, head : head + 1])
                probs_grad = back_dot(grad, values)
                delta = jnp.sum(probs * probs_grad, axis=1, keepdims=True)
                scores_grad = low(probs * (probs_grad - delta))
                outputs.append(dense(scores_grad, keys) * HD**-0.5)
                keys_grad_ref[low_key:high_key] += row_dot(scores_grad, one) * HD**-0.5
                values_grad_ref[low_key:high_key] += row_dot(low(probs), grad)
            query_grad = jnp.where(left, outputs[0], outputs[1])
            rows_ref[rows, lanes] = low(rotated_back(query_grad, cosine_ref[rows], sine_ref[rows]))
    keys_grad = keys_grad_ref[...]
    keys_grad = keys_grad + pltpu.roll(keys_grad, HD, 1)
    keys_grad = rotated_back(keys_grad, cosine_ref[...], sine_ref[...])
    values_grad = values_grad_ref[...]
    values_grad = values_grad + pltpu.roll(values_grad, HD, 1)
    left = grid_of(length, LANES, 1) < HD
    rows_ref[:, query_width:] = low(jnp.where(left, keys_grad, values_grad))


def attention_forward(projected, segment_column, segment_row, cosine, sine):
    length, width = projected.shape
    query_width = width - LANES
    return pl.pallas_call(
        attention_forward_kernel,
        out_shape=[
            jax.ShapeDtypeStruct((length, query_width), jnp.bfloat16),
            jax.ShapeDtypeStruct((length, query_width // HD), jnp.float32),
        ],
        scratch_shapes=[
            pltpu.VMEM((length, LANES), jnp.bfloat16),
            pltpu.VMEM((length, LANES), jnp.bfloat16),
        ],
        compiler_params=pltpu.CompilerParams(vmem_limit_bytes=40 * 2**20),
        cost_estimate=pl.CostEstimate(
            flops=5 * 10**9, bytes_accessed=5 * 2**20, transcendentals=3 * 10**6
        ),
        name="attention_forward",
    )(projected, segment_column, segment_row, cosine, sine)


def attention_backward(projected, grad, totals, segment_column, segment_row, cosine, sine):
    length, width = projected.shape
    return pl.pallas_call(
        attention_backward_kernel,
        out_shape=jax.ShapeDtypeStruct((length, width), jnp.bfloat16),
        scratch_shapes=[
            pltpu.VMEM((length, LANES), jnp.bfloat16),
            pltpu.VMEM((length, LANES), jnp.bfloat16),
            pltpu.VMEM((length, LANES), jnp.float32),
            pltpu.VMEM((length, LANES), jnp.float32),
        ],
        compiler_params=pltpu.CompilerParams(vmem_limit_bytes=40 * 2**20),
        cost_estimate=pl.CostEstimate(
            flops=10**10, bytes_accessed=6 * 2**20, transcendentals=3 * 10**6
        ),
        name="attention_backward",
    )(projected, grad, totals, segment_column, segment_row, cosine, sine)


def whole(shape):
    return pl.BlockSpec(shape, lambda i: (0,) * len(shape))


def mixer_sizes(projected, tables):
    return projected.shape[0], tables[0].shape[1], tables[1].shape[1]


def mixer_forward(projected, tables):
    length, channels, state_width = mixer_sizes(projected, tables)
    count = length // SPAN

    def rows_of(width, place=0):
        return pl.BlockSpec((SPAN, width), lambda i: (i, place))

    state_place = 2 * channels // state_width
    step_place = (2 * channels + state_width) // LANES

    return pl.pallas_call(
        mixer_forward_kernel,
        grid=(count,),
        in_specs=[
            rows_of(channels, 1), rows_of(channels), rows_of(state_width, state_place), rows_of(LANES, step_place),
            whole((8, channels)), whole((8, state_width)), whole((8, LANES)), whole((1, channels)),
        ],
        out_specs=[
            rows_of(channels), rows_of(channels), rows_of(1),
            pl.BlockSpec((1, N_STATE, channels), lambda i: (i, 0, 0)),
        ],
        out_shape=[
            jax.ShapeDtypeStruct((length, channels), jnp.float32),
            jax.ShapeDtypeStruct((length, channels), jnp.bfloat16),
            jax.ShapeDtypeStruct((length, 1), jnp.float32),
            jax.ShapeDtypeStruct((count, N_STATE, channels), jnp.bfloat16),
        ],
        scratch_shapes=[
            pltpu.VMEM((8, channels), jnp.float32),
            pltpu.VMEM((8, state_width), jnp.float32),
            pltpu.VMEM((N_STATE, channels), jnp.float32),
            pltpu.VMEM((SPAN, channels), jnp.bfloat16),
        ],
        compiler_params=pltpu.CompilerParams(vmem_limit_bytes=40 * 2**20),
        cost_estimate=pl.CostEstimate(
            flops=6 * 10**9, bytes_accessed=14 * 2**20, transcendentals=4 * 10**6
        ),
        name="mixer_forward",
    )(projected, projected, projected, projected, *tables)


def mixer_backward(grad, stats, scanned, projected, saved, tables, gain_wide):
    length, channels, state_width = mixer_sizes(projected, tables)
    count = length // SPAN
    total = 2 * channels + state_width + LANES

    def rows_of(width, place=0):
        return pl.BlockSpec((SPAN, width), lambda i: (count - 1 - i, place))

    def before(width, place):
        return pl.BlockSpec(
            (8, width), lambda i: (jnp.maximum((count - 1 - i) * (SPAN // 8) - 1, 0), place)
        )

    state_place = 2 * channels // state_width
    step_place = (2 * channels + state_width) // LANES

    return pl.pallas_call(
        mixer_backward_kernel,
        grid=(count,),
        in_specs=[
            rows_of(channels), rows_of(2), rows_of(channels), rows_of(channels, 1), before(channels, 1),
            rows_of(channels), rows_of(state_width, state_place), before(state_width, state_place),
            rows_of(LANES, step_place),
            pl.BlockSpec((1, N_STATE, channels), lambda i: (count - 1 - i, 0, 0)),
            whole((8, channels)), whole((8, state_width)), whole((8, LANES)), whole((1, channels)),
            whole((1, channels)),
        ],
        out_specs=[
            rows_of(total), whole((8, channels)), whole((8, state_width)), whole((8, LANES)),
        ],
        out_shape=[
            jax.ShapeDtypeStruct((length, total), jnp.bfloat16),
            jax.ShapeDtypeStruct((8, channels), jnp.float32),
            jax.ShapeDtypeStruct((8, state_width), jnp.float32),
            jax.ShapeDtypeStruct((8, LANES), jnp.float32),
        ],
        scratch_shapes=[
            pltpu.VMEM((8, channels), jnp.float32),
            pltpu.VMEM((8, state_width), jnp.float32),
            pltpu.VMEM((N_STATE, channels), jnp.float32),
            pltpu.VMEM((LANES, SPAN), jnp.float32),
        ],
        compiler_params=pltpu.CompilerParams(vmem_limit_bytes=40 * 2**20),
        cost_estimate=pl.CostEstimate(
            flops=20 * 10**9, bytes_accessed=20 * 2**20, transcendentals=8 * 10**6
        ),
        name="mixer_backward",
    )(
        grad, stats, scanned, projected, projected, projected, projected, projected, projected, saved,
        *tables, gain_wide,
    )


def on_device(
    block_input,
    segment_ids,
    out_grad,
    gating_weight,
    inner_weight,
    state_weight,
    step_weight,
    step_bias,
    decay_log,
    skip_scale,
    inner_conv,
    state_conv,
    mixer_gain,
    mixer_proj,
    query_weight,
    key_weight,
    value_weight,
    attention_out,
    first_gain,
    second_gain,
    gate_weight,
    up_weight,
    down_projection_weight,
):
    seq_count, seq_len = segment_ids.shape
    channels = inner_weight.shape[1]
    head_local = step_weight.shape[1]
    query_heads = query_weight.shape[1] // HD
    kv_heads = key_weight.shape[1] // HD
    mixer_width = H_SSM * P_SIZE

    tokens = block_input.astype(jnp.float32)
    first_inverse = lax.rsqrt(jnp.mean(tokens * tokens, axis=-1, keepdims=True) + epsilon)
    first_vector = first_gain.astype(jnp.float32)
    normed_share = (tokens * first_inverse * first_vector).astype(jnp.bfloat16)
    normed = gather_rows(normed_share)
    model_width = normed.shape[1]
    place = lax.axis_index("tensor")
    share_rows = tokens.shape[0]
    piece_rows = share_rows // PIECES
    other_grad = swap_tensor(after(out_grad, [normed]))
    state_width = state_weight.shape[1]
    mixer_weights = jnp.concatenate(
        [gating_weight, inner_weight, state_weight, jnp.pad(step_weight, ((0, 0), (0, LANES - head_local)))],
        axis=1,
    )
    projected = dense(normed, mixer_weights)

    def eight_rows(values):
        return jnp.pad(values.astype(jnp.float32), ((0, 8 - values.shape[0]), (0, 0)))

    head_table = jnp.pad(
        jnp.stack([step_bias, -jnp.exp(decay_log)]), ((0, 6), (0, LANES - head_local))
    )
    skip_wide = jnp.repeat(skip_scale, P_SIZE)[None]
    tables = (eight_rows(inner_conv), eight_rows(state_conv), head_table, skip_wide)
    gated, scanned, squares, saved_states = mixer_forward(projected, tables)
    gated_squares = both(squares)
    mixer_inverse = lax.rsqrt(gated_squares / mixer_width + epsilon)
    mixer_vector = mixer_gain.astype(jnp.float32)
    mixer_normed = (gated * mixer_inverse * mixer_vector).astype(jnp.bfloat16)
    cosine, sine = rope_tables(seq_len)
    segments = (segment_ids.reshape(seq_len, 1), segment_ids.reshape(1, seq_len))
    attention_weights = jnp.concatenate([query_weight, key_weight, value_weight], axis=1)
    attention_inputs = dense(normed, attention_weights)
    attended, log_totals = attention_forward(attention_inputs, *segments, cosine, sine)
    second_vector = second_gain.astype(jnp.float32)

    def branch_rows(start):
        return dense(rows_at(mixer_normed, start, piece_rows), mixer_proj) + dense(
            rows_at(attended, start, piece_rows), attention_out
        )

    def piece_of(value, piece):
        return value[piece * piece_rows : (piece + 1) * piece_rows]

    residuals, second_inverses, kept, outputs, second_grads = [], [], [], [], []
    branch_own, branch_other, first_residual_grads = [], [], []
    for piece in range(PIECES):
        offset = piece * piece_rows
        other_part = branch_rows((1 - place) * share_rows + offset)
        residual = piece_of(tokens, piece) + swapped_sum(
            branch_rows(place * share_rows + offset), other_part
        )
        inverse = lax.rsqrt(jnp.mean(residual * residual, axis=-1, keepdims=True) + epsilon)
        residuals.append(residual)
        second_inverses.append(inverse)
    normed_pieces = []
    for residual, inverse in zip(residuals, second_inverses):
        normed_own = low(residual * inverse * second_vector)
        normed_pieces.append(jnp.concatenate([normed_own, swap_tensor(normed_own)], axis=0))
    gradient_pieces = []
    for piece in range(PIECES):
        normed_two = normed_pieces[piece]
        full_grad = jnp.concatenate([piece_of(out_grad, piece), piece_of(other_grad, piece)], axis=0)
        gate_pre = dense(normed_two, gate_weight)
        up_pre = dense(normed_two, up_weight)
        gate_sigmoid = jax.nn.sigmoid(gate_pre)
        gate_act = gate_pre * gate_sigmoid
        hidden = low(gate_act * up_pre)
        grad_hidden = back_dot(full_grad, down_projection_weight)
        grad_gate_pre = low(
            grad_hidden * up_pre * gate_sigmoid * (1.0 + gate_pre * (1.0 - gate_sigmoid))
        )
        grad_up_pre = low(grad_hidden * gate_act)
        kept.append((hidden, full_grad, jnp.concatenate([grad_gate_pre, grad_up_pre], axis=1)))

        def second_back(rows):
            return back_dot(grad_gate_pre[rows], gate_weight) + back_dot(grad_up_pre[rows], up_weight)

        own, other = slice(0, piece_rows), slice(piece_rows, 2 * piece_rows)
        second_other = second_back(other)
        second_own = second_back(own)
        second_grads.append(swapped_sum(second_own, second_other))
        outputs.append((dense(hidden[own], down_projection_weight), dense(hidden[other], down_projection_weight)))
    kept = [tuple(after(one, [second_own, second_other]) for one in pieces) for pieces in kept]
    hidden_rows, full_rows, gate_up_rows = [jnp.concatenate(parts, axis=0) for parts in zip(*kept)]
    normed_rows = jnp.concatenate(normed_pieces, axis=0)
    ffn_grads = jnp.concatenate(
        [low(row_dot(hidden_rows, full_rows)), low(row_dot(normed_rows, gate_up_rows))], axis=1
    )
    ffn_share = lax.psum_scatter(ffn_grads, "dp", scatter_dimension=0, tiled=True)
    ffn_sums = lax.all_gather(ffn_share, "dp", axis=0, tiled=True)
    for piece in range(PIECES):
        residual, inverse = residuals[piece], second_inverses[piece]
        grad_residual = piece_of(out_grad, piece).astype(jnp.float32) + norm_back(
            second_grads[piece], residual, inverse, second_vector
        )
        first_residual_grads.append(grad_residual)
        branch_own.append(low(grad_residual))
        branch_other.append(swap_tensor(branch_own[-1]))
    residual = jnp.concatenate(residuals, axis=0)
    grad_normed_two = jnp.concatenate(second_grads, axis=0)
    grad_second_gain = jnp.sum(
        grad_normed_two * residual * jnp.concatenate(second_inverses, axis=0), axis=0
    )
    grad_residual = jnp.concatenate(first_residual_grads, axis=0)
    branch_grad = in_order(
        place, jnp.concatenate(branch_own, axis=0), jnp.concatenate(branch_other, axis=0)
    )
    block_output = jnp.concatenate(
        [
            low(residuals[piece] + swapped_sum(own, after(other, [branch_grad])))
            for piece, (own, other) in enumerate(outputs)
        ],
        axis=0,
    )
    grad_mixer_normed = back_dot(branch_grad, mixer_proj)
    cross_part = jnp.sum(gated * (grad_mixer_normed * mixer_vector), axis=-1, keepdims=True)
    cross_sum = both(cross_part)
    grad_attended = low(back_dot(branch_grad, attention_out))
    branch_sum = DpSum(
        jnp.concatenate(
            [low(row_dot(mixer_normed, branch_grad)), low(row_dot(attended, branch_grad))], axis=0
        )
    )
    attention_rows = attention_backward(
        attention_inputs, after(grad_attended, [cross_part]), log_totals, *segments, cosine, sine
    )
    stats = jnp.concatenate(
        [mixer_inverse, mixer_inverse**3 * (cross_sum / mixer_width)], axis=1
    )
    stats = after(stats, branch_sum.advance(), [attention_rows])
    mixer_rows, inner_sums, state_sums, head_sums = mixer_backward(
        grad_mixer_normed, stats, scanned, projected, saved_states, tables, mixer_vector[None]
    )
    normed_again = after(normed, [mixer_rows])

    def first_back(start):
        return back_dot(rows_at(mixer_rows, start, share_rows), mixer_weights) + back_dot(
            rows_at(attention_rows, start, share_rows), attention_weights
        )

    grad_inputs = jnp.concatenate(
        [low(row_dot(normed_again, mixer_rows)), low(row_dot(normed_again, attention_rows))], axis=1
    )
    split = grad_inputs.shape[1] // (2 * LANES) * LANES
    input_sum = DpSum(
        grad_inputs, split, (2 * channels - split, 2 * channels + state_width - split)
    )
    mixer_rows = after(mixer_rows, [grad_inputs])
    other_part = first_back((1 - place) * share_rows)
    grad_normed = swapped_sum(first_back(place * share_rows), other_part)
    grad_first_gain = jnp.sum(grad_normed * tokens * first_inverse, axis=0)
    input_grad = grad_residual + norm_back(grad_normed, tokens, first_inverse, first_vector)
    ffn_width = gate_weight.shape[1]
    input_sum.advance(branch_sum.advance())
    input_sum.advance(branch_sum.advance())
    input_sum.advance(branch_sum.advance(), [ffn_sums])
    grad_down, grad_gate, grad_up = jnp.split(
        ffn_sums.astype(jnp.float32), [model_width, model_width + ffn_width], axis=1
    )
    input_sum.advance(branch_sum.advance())
    input_sum.advance(branch_sum.advance())
    input_sum.advance(branch_sum.advance(), [grad_down, grad_gate, grad_up])
    taps = inner_conv.shape[0]
    grad_inner_conv, grad_mixer_gain = inner_sums[:taps], inner_sums[taps]
    grad_skip_scale = jnp.sum(inner_sums[taps + 1].reshape(head_local, P_SIZE), axis=1)
    grad_state_conv = state_sums[:taps]
    grad_step_bias, grad_decay_log = head_sums[0, :head_local], head_sums[1, :head_local]
    shared_small = jnp.concatenate(
        [grad_state_conv.reshape(-1), grad_first_gain, grad_second_gain]
    )
    own_small = jnp.concatenate(
        [
            grad_inner_conv.reshape(-1),
            grad_mixer_gain,
            grad_step_bias,
            grad_decay_log,
            grad_skip_scale,
        ]
    )
    small = jnp.concatenate([both(shared_small), own_small])
    small_bits = bits_in_order(False)
    for bit in small_bits:
        got = flip(small, bit)
        if bit == small_bits[-2]:
            input_sum.advance(branch_sum.advance(), [got])
        small = small + got
    branch_sums = branch_sum.finish().astype(jnp.float32)
    grad_mixer_proj, attention_output_gradient = branch_sums[:channels], branch_sums[channels:]
    input_sum.advance([grad_mixer_proj, attention_output_gradient, small, input_grad, block_output])
    own_share, other_share, share_place = input_sum.finish()
    step_start = 2 * channels + state_width
    query_start = step_start + LANES
    key_start = query_start + query_heads * HD
    value_start = key_start + kv_heads * HD
    grad_gating, grad_inner, grad_state, grad_step, grad_query, grad_key, grad_value = unpack(
        own_share,
        other_share,
        share_place,
        [
            (0, channels),
            (channels, channels),
            (2 * channels, state_width),
            (step_start, head_local),
            (query_start, query_heads * HD),
            (key_start, kv_heads * HD),
            (value_start, kv_heads * HD),
        ],
    )
    shared_small, own_small = small[: shared_small.shape[0]], small[shared_small.shape[0] :]
    grad_state_conv, grad_first_gain, grad_second_gain = jnp.split(
        shared_small, [taps * state_width, taps * state_width + model_width]
    )
    starts = [taps * channels, (taps + 1) * channels]
    starts = starts + [starts[1] + head_local, starts[1] + 2 * head_local]
    grad_inner_conv, grad_mixer_gain, grad_step_bias, grad_decay_log, grad_skip_scale = jnp.split(
        own_small, starts
    )
    return (
        block_output,
        input_grad,
        grad_gating,
        grad_inner,
        grad_state,
        grad_step,
        grad_step_bias,
        grad_decay_log,
        grad_skip_scale,
        grad_inner_conv.reshape(taps, channels),
        grad_state_conv.reshape(taps, state_width),
        grad_mixer_gain,
        grad_mixer_proj,
        grad_query,
        grad_key,
        grad_value,
        attention_output_gradient,
        grad_first_gain,
        grad_second_gain,
        grad_gate,
        grad_up,
        grad_down,
    )


def solution(mesh):
    placed = (
        P(("dp", "tensor"), None),
        P("dp", None),
        P(("dp", "tensor"), None),
        P(None, "tensor"),
        P(None, "tensor"),
        P(),
        P(None, "tensor"),
        P("tensor"),
        P("tensor"),
        P("tensor"),
        P(None, "tensor"),
        P(),
        P("tensor"),
        P("tensor", None),
        P(None, "tensor"),
        P(None, "tensor"),
        P(None, "tensor"),
        P("tensor", None),
        P(),
        P(),
        P(None, "tensor"),
        P(None, "tensor"),
        P("tensor", None),
    )
    return jax.shard_map(
        on_device,
        mesh=mesh,
        in_specs=placed,
        out_specs=(
            P(("dp", "tensor"), None),
            P(("dp", "tensor"), None),
            P(None, "tensor"),
            P(None, "tensor"),
            P(),
            P(None, "tensor"),
            P("tensor"),
            P("tensor"),
            P("tensor"),
            P(None, "tensor"),
            P(),
            P("tensor"),
            P("tensor", None),
            P(None, "tensor"),
            P(None, "tensor"),
            P(None, "tensor"),
            P("tensor", None),
            P(),
            P(),
            P(None, "tensor"),
            P(None, "tensor"),
            P("tensor", None),
        ),
        check_vma=False,
    )
```

```python
import functools

import jax
import jax.numpy as jnp
from jax import lax
from jax.experimental import pallas as pl
from jax.experimental.pallas import tpu as pltpu
from jax.sharding import PartitionSpec as P

H_SSM = 24
P_SIZE = 64
HD = 64
SPAN = 128
QUERY_BLOCK = 256
PIECES = 2
SEG_MOST = 512
N_STATE = 128
LANES = 128


epsilon = 1e-05
rope_base = 100000000000.0
top_precision = lax.Precision.HIGHEST


def dense(left_side, right_side):
    return jnp.dot(left_side, right_side, preferred_element_type=jnp.float32)


def row_dot(left_side, right_side):
    return lax.dot_general(
        left_side, right_side, (((0,), (0,)), ((), ())), preferred_element_type=jnp.float32
    )


def back_dot(left_side, right_side):
    return lax.dot_general(
        left_side, right_side, (((1,), (1,)), ((), ())), preferred_element_type=jnp.float32
    )


def rope_tables(length):
    positions = jnp.arange(length, dtype=jnp.float32)
    frequency = rope_base ** (-jnp.arange(0, HD, 2, dtype=jnp.float32) / HD)
    angles = positions[:, None] * frequency[None, :]
    copies = [1] * (2 * LANES // HD)
    cosine, sine = jnp.cos(angles), jnp.sin(angles)
    return (
        jnp.concatenate([cosine for _ in copies], axis=1),
        jnp.concatenate([sine for _ in copies], axis=1),
    )


def norm_back(grad_values, value_tensor, inverse, gain_vector):
    scaled = grad_values * gain_vector
    return inverse * scaled - value_tensor * inverse**3 * jnp.mean(
        value_tensor * scaled, axis=-1, keepdims=True
    )


def swap_tensor(value):
    return lax.ppermute(value, "tensor", [(0, 1), (1, 0)])


def both(value):
    return value + swap_tensor(value)


def in_order(place, own, other):
    first = jnp.where(place == 0, own, other)
    second = jnp.where(place == 0, other, own)
    return jnp.concatenate([first, second], axis=0)


def gather_rows(share):
    return in_order(lax.axis_index("tensor"), share, swap_tensor(share))


def half_of(value, place):
    half = value.shape[0] // 2
    return lax.dynamic_slice_in_dim(value, place * half, half, 0)


def rows_at(value, start, count):
    return lax.dynamic_slice_in_dim(value, start, count, 0)


def swapped_sum(own, other):
    return own + swap_tensor(low(other)).astype(jnp.float32)


def flip(value, bit):
    size = lax.axis_size("dp")
    return lax.ppermute(value, "dp", [(i, i ^ bit) for i in range(size)])


def bits_in_order(far_first):
    count = lax.axis_size("dp").bit_length() - 1
    bits = [1 << i for i in range(count)]
    return bits[:1] + bits[2:] + bits[1:2] if far_first else bits


def dp_stages(whole, split=None, tensor_columns=None):
    index = lax.axis_index("dp")
    near, far = bits_in_order(False), bits_in_order(True)
    orders = [far] if split is None else [near, far]

    def place_of(bit):
        return (index // bit) % 2

    def exchange(value, bit):
        place = place_of(bit)
        return half_of(value, place), flip(half_of(value, 1 - place), bit)

    def total(keep, got):
        return low(keep.astype(jnp.float32) + got.astype(jnp.float32))

    keep, got = exchange(whole, near[0])
    (got,) = yield [got]
    share = total(keep, got)
    parts = [share] if split is None else [share[:, :split], share[:, split:]]
    for step in range(1, len(near)):
        pairs = [exchange(part, order[step]) for part, order in zip(parts, orders)]
        arrived = yield [got for _, got in pairs]
        parts = [total(keep, got) for (keep, _), got in zip(pairs, arrived)]
    if tensor_columns is not None:
        start, stop = tensor_columns
        part = parts[-1][:, start:stop]
        (got,) = yield [swap_tensor(part)]
        parts[-1] = jnp.concatenate(
            [parts[-1][:, :start], total(part, got), parts[-1][:, stop:]], axis=1
        )
    for step in range(len(near) - 1, 0, -1):
        got = [flip(part, order[step]) for part, order in zip(parts, orders)]
        got = yield got
        parts = [
            in_order(place_of(order[step]), part, other)
            for part, order, other in zip(parts, orders, got)
        ]
    share = parts[0] if split is None else jnp.concatenate(parts, axis=1)
    (got,) = yield [flip(share, near[0])]
    if split is not None:
        return share, got, place_of(near[0])
    return in_order(place_of(near[0]), share, got)


def unpack_kernel(starts, place_ref, own_ref, other_ref, *output_refs):
    half = pl.program_id(0) // (pl.num_programs(0) // 2)
    values = jnp.where(half == place_ref[0], own_ref[...], other_ref[...]).astype(jnp.float32)
    for start, output_ref in zip(starts, output_refs):
        output_ref[...] = values[:, start : start + output_ref.shape[1]]


def unpack(own, other, place, columns):
    half_rows, width = own.shape
    block = 2 * SPAN
    steps = half_rows // block
    rows = pl.BlockSpec((block, width), lambda i: (i % steps, 0))
    return pl.pallas_call(
        functools.partial(unpack_kernel, [start for start, _ in columns]),
        grid=(2 * steps,),
        in_specs=[pl.BlockSpec(memory_space=pltpu.SMEM), rows, rows],
        out_specs=[pl.BlockSpec((block, size), lambda i: (i, 0)) for _, size in columns],
        out_shape=[jax.ShapeDtypeStruct((2 * half_rows, size), jnp.float32) for _, size in columns],
        compiler_params=pltpu.CompilerParams(vmem_limit_bytes=40 * 2**20),
        cost_estimate=pl.CostEstimate(
            flops=0, bytes_accessed=16 * half_rows * width, transcendentals=0
        ),
        name="unpack",
    )(place.reshape(1).astype(jnp.int32), own, other)


class DpSum:
    def __init__(self, whole, split=None, tensor_columns=None):
        self.stages = dp_stages(low(whole), split, tensor_columns)
        self.arrived = next(self.stages)
        self.result = None

    def advance(self, *others):
        if self.result is not None:
            return []
        arrived = self.arrived
        flat = [one for several in others for one in several]
        if flat:
            arrived = list(lax.optimization_barrier((*arrived, *flat))[: len(arrived)])
        try:
            self.arrived = self.stages.send(arrived)
        except StopIteration as end:
            self.result = end.value
        return arrived

    def finish(self):
        while self.result is None:
            self.advance()
        return self.result


def after(value, *arrived):
    flat = [one for several in arrived for one in several]
    return lax.optimization_barrier((value, *flat))[0] if flat else value


def sigmoid(v):
    return 1.0 / (1.0 + jnp.exp(-v))


def softplus(v):
    return jnp.maximum(v, 0.0) + jnp.log1p(jnp.exp(-jnp.abs(v)))


def low(v):
    return v.astype(jnp.bfloat16)


def conv_taps(ext, taps, rows):
    result = ext[5 : 5 + rows] * taps[0:1]
    for j in range(1, 4):
        result = result + ext[5 + j : 5 + j + rows] * taps[j : j + 1]
    return result


def exact_dot(left_side, right_side):
    return jnp.dot(
        left_side, right_side, preferred_element_type=jnp.float32, precision=top_precision
    )


def grid_of(rows, columns, axis):
    return lax.broadcasted_iota(jnp.int32, (rows, columns), axis)


def pair_wide(values, pair):
    rows = values.shape[0]
    low_half = jnp.broadcast_to(values[:, 2 * pair : 2 * pair + 1], (rows, LANES))
    high_half = jnp.broadcast_to(values[:, 2 * pair + 1 : 2 * pair + 2], (rows, LANES))
    return jnp.where(grid_of(rows, LANES, 1) < P_SIZE, low_half, high_half)


def split_pair(values):
    left = grid_of(values.shape[0], LANES, 1) < P_SIZE
    zero = jnp.zeros_like(values)
    return jnp.concatenate([jnp.where(left, values, zero), jnp.where(left, zero, values)], axis=0)


def step_terms(step_ref, head_ref):
    rows = step_ref.shape[0]
    shifted = step_ref[...] + head_ref[0:1]
    steps = softplus(shifted)
    rate = head_ref[1:2]
    lower = (grid_of(rows, rows, 0) >= grid_of(rows, rows, 1)).astype(jnp.float32)
    cumulative = exact_dot(lower, steps * rate)
    return shifted, steps, rate, cumulative


def mixer_forward_kernel(
    inner_ref, gating_ref, state_ref, step_ref, inner_taps_ref, state_taps_ref, head_ref, skip_ref,
    gated_ref, scanned_ref, squares_ref, saved_ref,
    inner_tail, state_tail, carry, written,
):
    rows, channels = inner_ref.shape

    @pl.when(pl.program_id(0) == 0)
    def _():
        inner_tail[...] = jnp.zeros_like(inner_tail)
        state_tail[...] = jnp.zeros_like(state_tail)
        carry[...] = jnp.zeros_like(carry)

    state_pre = state_ref[...]
    state_conv = conv_taps(
        jnp.concatenate([state_tail[...], state_pre], axis=0), state_taps_ref[...], rows
    )
    state_tail[...] = state_pre[rows - 8 :]
    state_act = state_conv * sigmoid(state_conv)
    in_vec = low(state_act[:, :N_STATE])
    out_vec = low(state_act[:, N_STATE:])
    in_turned = in_vec.T
    _, steps, _, cumulative = step_terms(step_ref, head_ref)
    turned = cumulative.T
    grown = jnp.exp(cumulative)
    tail_weight = jnp.exp(cumulative[rows - 1 : rows] - cumulative) * steps
    decay = grown[rows - 1 : rows]
    lower_mask = grid_of(rows, rows, 0) >= grid_of(rows, rows, 1)
    scores = back_dot(out_vec, in_vec)
    saved = low(carry[...])
    saved_ref[0] = saved
    from_state = dense(out_vec, saved)
    squares = jnp.zeros((rows, 1), jnp.float32)
    for pair in range(channels // LANES):
        lanes = slice(pair * LANES, (pair + 1) * LANES)
        inner_pre = inner_ref[:, lanes]
        conv = conv_taps(
            jnp.concatenate([inner_tail[:, lanes], inner_pre], axis=0),
            inner_taps_ref[:, lanes],
            rows,
        )
        inner_tail[:, lanes] = inner_pre[rows - 8 :]
        act = conv * sigmoid(conv)
        mixing = []
        for head in (2 * pair, 2 * pair + 1):
            gaps = cumulative[:, head : head + 1] - turned[head : head + 1, :]
            mixing.append(low(scores * jnp.exp(jnp.where(lower_mask, gaps, -1e30))))
        mixing = jnp.concatenate(mixing, axis=1)
        scanned = dense(mixing, split_pair(low(act * pair_wide(steps, pair))))
        scanned = scanned + from_state[:, lanes] * pair_wide(grown, pair)
        scanned = scanned + act * skip_ref[:, lanes]
        written[:, lanes] = low(act * pair_wide(tail_weight, pair))
        gating = gating_ref[:, lanes]
        gated = scanned * (gating * sigmoid(gating))
        gated_ref[:, lanes] = gated
        scanned_ref[:, lanes] = low(scanned)
        squares = squares + jnp.sum(gated * gated, axis=1, keepdims=True)
    squares_ref[...] = squares
    update = dense(in_turned, written[...])
    for pair in range(channels // LANES):
        lanes = slice(pair * LANES, (pair + 1) * LANES)
        carry[:, lanes] = carry[:, lanes] * pair_wide(decay, pair) + update[:, lanes]


def mixer_backward_kernel(
    grad_ref, stats_ref, scanned_ref, inner_ref, inner_before_ref, gating_ref, state_ref,
    state_before_ref, step_ref, saved_ref, inner_taps_ref, state_taps_ref, head_ref, skip_ref, gain_ref,
    rows_ref, inner_sums_ref, state_sums_ref, head_sums_ref,
    inner_next, state_next, carry, turned_sums,
):
    rows, channels = inner_ref.shape
    place = pl.program_id(0)
    chunk = pl.num_programs(0) - 1 - place

    @pl.when(place == 0)
    def _():
        inner_next[...] = jnp.zeros_like(inner_next)
        state_next[...] = jnp.zeros_like(state_next)
        carry[...] = jnp.zeros_like(carry)
        inner_sums_ref[...] = jnp.zeros_like(inner_sums_ref)
        state_sums_ref[...] = jnp.zeros_like(state_sums_ref)
        head_sums_ref[...] = jnp.zeros_like(head_sums_ref)
        turned_sums[...] = jnp.zeros_like(turned_sums)

    first = chunk == 0
    state_ext = jnp.concatenate(
        [jnp.where(first, 0.0, state_before_ref[...]), state_ref[...]], axis=0
    )
    state_conv = conv_taps(state_ext, state_taps_ref[...], rows)
    state_sigmoid = sigmoid(state_conv)
    state_act = state_conv * state_sigmoid
    in_vec = low(state_act[:, :N_STATE])
    out_vec = low(state_act[:, N_STATE:])
    out_turned = out_vec.T
    shifted, steps, rate, cumulative = step_terms(step_ref, head_ref)
    turned = cumulative.T
    steps_turned = steps.T
    grown = jnp.exp(cumulative)
    fade = jnp.exp(cumulative[rows - 1 : rows] - cumulative)
    tail_weight = fade * steps
    decay = grown[rows - 1 : rows]
    row_at, column_at = grid_of(rows, rows, 0), grid_of(rows, rows, 1)
    lower_mask = row_at >= column_at
    scores = back_dot(out_vec, in_vec)
    inverse, slope = stats_ref[:, 0:1], stats_ref[:, 1:2]
    lane_at = grid_of(rows, LANES, 1)
    score_grad = jnp.zeros((rows, rows), jnp.float32)
    out_grad = jnp.zeros((rows, N_STATE), jnp.float32)
    in_grad = jnp.zeros((rows, N_STATE), jnp.float32)
    row_sums = jnp.zeros((rows, LANES), jnp.float32)
    read_sums = jnp.zeros((rows, LANES), jnp.float32)
    write_sums = jnp.zeros((rows, LANES), jnp.float32)
    state_sums = jnp.zeros((1, LANES), jnp.float32)
    segment_row, segment_column = grid_of(LANES, LANES, 0), grid_of(LANES, LANES, 1)
    first_lane = grid_of(1, LANES, 1)
    for pair in range(channels // LANES):
        lanes = slice(pair * LANES, (pair + 1) * LANES)
        inner_ext = jnp.concatenate(
            [jnp.where(first, 0.0, inner_before_ref[:, lanes]), inner_ref[:, lanes]], axis=0
        )
        taps = inner_taps_ref[:, lanes]
        conv = conv_taps(inner_ext, taps, rows)
        conv_sigmoid = sigmoid(conv)
        act = conv * conv_sigmoid
        act_low = low(act)
        gating = gating_ref[:, lanes]
        gate_sigmoid = sigmoid(gating)
        gate_act = gating * gate_sigmoid
        scanned = scanned_ref[:, lanes].astype(jnp.float32)
        gated = scanned * gate_act
        grad = grad_ref[:, lanes].astype(jnp.float32)
        gated_grad = inverse * grad * gain_ref[:, lanes] - gated * slope
        rows_ref[:, lanes] = low(
            gated_grad * scanned * gate_sigmoid * (1.0 + gating * (1.0 - gate_sigmoid))
        )
        scan_grad = gated_grad * gate_act
        gain_sum = jnp.sum(grad * gated * inverse, axis=0, keepdims=True)
        skip_sum = jnp.sum(scan_grad * act, axis=0, keepdims=True)
        blocks = split_pair(low(scan_grad))
        mixing_grad = back_dot(blocks, act_low)
        mixing = []
        for side in range(2):
            head = 2 * pair + side
            gaps = cumulative[:, head : head + 1] - turned[head : head + 1, :]
            within = jnp.exp(jnp.where(lower_mask, gaps, -1e30))
            part = mixing_grad[side * rows : (side + 1) * rows] * within
            step_row = steps_turned[head : head + 1, :]
            score_grad = score_grad + part * step_row
            product = part * scores
            turned_sums[head : head + 1, :] = jnp.sum(product, axis=0, keepdims=True)
            row_sum = jnp.sum(product * step_row, axis=1, keepdims=True)
            row_sums = jnp.where(lane_at == head, row_sum, row_sums)
            mixing.append(low(scores * within))
        act_grad = row_dot(jnp.concatenate(mixing, axis=0), blocks) * pair_wide(steps, pair)
        act_grad = act_grad + skip_ref[:, lanes] * scan_grad
        saved = saved_ref[0, :, lanes]
        later = carry[:, lanes]
        later_low = low(later)
        wide_tail = pair_wide(tail_weight, pair)
        wide_grown = pair_wide(grown, pair)
        through = dense(in_vec, later_low)
        act_grad = act_grad + wide_tail * through
        raised = low(scan_grad * wide_grown)
        to_segments = (segment_column == 2 * pair + segment_row // P_SIZE).astype(jnp.bfloat16)

        def segments(values):
            high = low(values)
            rest = low(values - high.astype(jnp.float32))
            return dense(high, to_segments) + dense(rest, to_segments)

        read_sums = read_sums + segments(scan_grad * wide_grown * dense(out_vec, saved))
        write_sums = write_sums + segments(act * through)
        overlap = jnp.sum(later * saved.astype(jnp.float32), axis=0, keepdims=True)
        left = first_lane < P_SIZE
        left_sum = jnp.sum(jnp.where(left, overlap, 0.0), axis=1, keepdims=True)
        right_sum = jnp.sum(jnp.where(left, 0.0, overlap), axis=1, keepdims=True)
        state_sums = jnp.where(first_lane == 2 * pair, left_sum, state_sums)
        state_sums = jnp.where(first_lane == 2 * pair + 1, right_sum, state_sums)
        carry[:, lanes] = later * pair_wide(decay, pair) + dense(out_turned, raised)
        out_grad = out_grad + back_dot(raised, saved)
        in_grad = in_grad + back_dot(low(act * wide_tail), later_low)
        conv_grad = act_grad * conv_sigmoid * (1.0 + conv * (1.0 - conv_sigmoid))
        ext = jnp.concatenate([conv_grad, inner_next[:, lanes]], axis=0)
        inner_next[:, lanes] = conv_grad[:8]
        pre_grad = ext[3 : 3 + rows] * taps[0:1]
        for j in range(1, 4):
            pre_grad = pre_grad + ext[3 - j : 3 - j + rows] * taps[j : j + 1]
        rows_ref[:, channels + pair * LANES : channels + (pair + 1) * LANES] = low(pre_grad)
        sums = [
            jnp.sum(conv_grad * inner_ext[5 + j : 5 + j + rows], axis=0, keepdims=True)
            for j in range(4)
        ]
        zero = jnp.zeros((2, LANES), jnp.float32)
        inner_sums_ref[:, lanes] += jnp.concatenate(sums + [gain_sum, skip_sum, zero], axis=0)

    score_low = low(score_grad)
    out_grad = out_grad + dense(score_low, in_vec)
    in_grad = in_grad + row_dot(score_low, out_vec)
    column_sums = turned_sums[...].T
    upper = (column_at >= row_at).astype(jnp.float32)
    strict = (column_at < row_at).astype(jnp.float32)
    log_grad = (
        exact_dot(upper, row_sums - steps * column_sums + read_sums)
        + exact_dot(strict, tail_weight * write_sums)
        + decay * state_sums
    )
    step_grad = column_sums + log_grad * rate + fade * write_sums
    step_pre_grad = step_grad * sigmoid(shifted)
    bias_sum = jnp.sum(step_pre_grad, axis=0, keepdims=True)
    decay_sum = jnp.sum(log_grad * steps, axis=0, keepdims=True) * rate
    head_sums_ref[...] += jnp.concatenate(
        [bias_sum, decay_sum, jnp.zeros((6, LANES), jnp.float32)], axis=0
    )
    state_grad = jnp.concatenate([in_grad, out_grad], axis=1)
    state_grad = state_grad * state_sigmoid * (1.0 + state_conv * (1.0 - state_sigmoid))
    taps = state_taps_ref[...]
    ext = jnp.concatenate([state_grad, state_next[...]], axis=0)
    state_next[...] = state_grad[:8]
    pre_grad = ext[3 : 3 + rows] * taps[0:1]
    for j in range(1, 4):
        pre_grad = pre_grad + ext[3 - j : 3 - j + rows] * taps[j : j + 1]
    width = state_grad.shape[1]
    rows_ref[:, 2 * channels : 2 * channels + width] = low(pre_grad)
    rows_ref[:, 2 * channels + width :] = low(step_pre_grad)
    sums = [
        jnp.sum(state_grad * state_ext[5 + j : 5 + j + rows], axis=0, keepdims=True)
        for j in range(4)
    ]
    state_sums_ref[...] += jnp.concatenate(sums + [jnp.zeros((4, width), jnp.float32)], axis=0)


def turn(values):
    first = grid_of(values.shape[0], LANES, 1) % HD < HD // 2
    ahead = pltpu.roll(values, LANES - HD // 2, 1)
    behind = pltpu.roll(values, HD // 2, 1)
    return first, ahead, behind


def rotated(values, cosine, sine):
    first, ahead, behind = turn(values)
    return values * cosine + jnp.where(first, -ahead, behind) * sine


def rotated_back(values, cosine, sine):
    first, ahead, behind = turn(values * sine)
    return values * cosine + jnp.where(first, ahead, -behind)


def doubled(pair):
    left = grid_of(pair.shape[0], LANES, 1) < HD
    turned = pltpu.roll(pair, HD, 1)
    return jnp.where(left, pair, turned), jnp.where(left, turned, pair)


def attention_blocks(length):
    for start in range(0, length, QUERY_BLOCK):
        yield start, max(0, start - SEG_MOST), start + QUERY_BLOCK


def allowed_keys(start, low_key, high_key, segment_column_ref, segment_row_ref):
    shape = (QUERY_BLOCK, high_key - low_key)
    query_at = start + lax.broadcasted_iota(jnp.int32, shape, 0)
    key_at = low_key + lax.broadcasted_iota(jnp.int32, shape, 1)
    same = segment_column_ref[start : start + QUERY_BLOCK] == segment_row_ref[:, low_key:high_key]
    return (key_at <= query_at) & same


def attention_forward_kernel(
    projected_ref, segment_column_ref, segment_row_ref, cosine_ref, sine_ref, attended_ref, totals_ref,
    keys_ref, values_ref,
):
    length, width = projected_ref.shape
    query_width = width - LANES
    key_part, value_part = doubled(projected_ref[:, query_width:])
    keys_ref[...] = low(rotated(key_part, cosine_ref[...], sine_ref[...]))
    values_ref[...] = low(value_part)
    left = grid_of(QUERY_BLOCK, LANES, 1) < HD
    for start, low_key, high_key in attention_blocks(length):
        rows = slice(start, start + QUERY_BLOCK)
        allowed = allowed_keys(start, low_key, high_key, segment_column_ref, segment_row_ref)
        keys, values = keys_ref[low_key:high_key], values_ref[low_key:high_key]
        for pair in range(query_width // LANES):
            lanes = slice(pair * LANES, (pair + 1) * LANES)
            queries = low(rotated(projected_ref[rows, lanes], cosine_ref[rows], sine_ref[rows]))
            both_heads = split_pair(queries)
            outputs = []
            for side in range(2):
                one = both_heads[side * QUERY_BLOCK : (side + 1) * QUERY_BLOCK]
                scores = jnp.where(allowed, back_dot(one, keys) * HD**-0.5, -1e30)
                row_max = jnp.max(scores, axis=1, keepdims=True)
                weights = jnp.exp(scores - row_max)
                row_total = jnp.sum(weights, axis=1, keepdims=True)
                outputs.append(dense(low(weights * (1.0 / row_total)), values))
                head = 2 * pair + side
                totals_ref[rows, head : head + 1] = row_max + jnp.log(row_total)
            attended_ref[rows, lanes] = low(jnp.where(left, outputs[0], outputs[1]))


def attention_backward_kernel(
    projected_ref, grad_ref, totals_ref, segment_column_ref, segment_row_ref, cosine_ref, sine_ref,
    rows_ref, keys_ref, values_ref, keys_grad_ref, values_grad_ref,
):
    length, width = projected_ref.shape
    query_width = width - LANES
    key_part, value_part = doubled(projected_ref[:, query_width:])
    keys_ref[...] = low(rotated(key_part, cosine_ref[...], sine_ref[...]))
    values_ref[...] = low(value_part)
    keys_grad_ref[...] = jnp.zeros_like(keys_grad_ref)
    values_grad_ref[...] = jnp.zeros_like(values_grad_ref)
    left = grid_of(QUERY_BLOCK, LANES, 1) < HD
    for start, low_key, high_key in attention_blocks(length):
        rows = slice(start, start + QUERY_BLOCK)
        allowed = allowed_keys(start, low_key, high_key, segment_column_ref, segment_row_ref)
        keys, values = keys_ref[low_key:high_key], values_ref[low_key:high_key]
        for pair in range(query_width // LANES):
            lanes = slice(pair * LANES, (pair + 1) * LANES)
            queries = low(rotated(projected_ref[rows, lanes], cosine_ref[rows], sine_ref[rows]))
            both_heads = split_pair(queries)
            both_grads = split_pair(grad_ref[rows, lanes])
            outputs = []
            for side in range(2):
                half = slice(side * QUERY_BLOCK, (side + 1) * QUERY_BLOCK)
                one, grad = both_heads[half], both_grads[half]
                head = 2 * pair + side
                scores = jnp.where(allowed, back_dot(one, keys) * HD**-0.5, -1e30)
                probs = jnp.exp(scores - totals_ref[rows, head : head + 1])
                probs_grad = back_dot(grad, values)
                delta = jnp.sum(probs * probs_grad, axis=1, keepdims=True)
                scores_grad = low(probs * (probs_grad - delta))
                outputs.append(dense(scores_grad, keys) * HD**-0.5)
                keys_grad_ref[low_key:high_key] += row_dot(scores_grad, one) * HD**-0.5
                values_grad_ref[low_key:high_key] += row_dot(low(probs), grad)
            query_grad = jnp.where(left, outputs[0], outputs[1])
            rows_ref[rows, lanes] = low(rotated_back(query_grad, cosine_ref[rows], sine_ref[rows]))
    keys_grad = keys_grad_ref[...]
    keys_grad = keys_grad + pltpu.roll(keys_grad, HD, 1)
    keys_grad = rotated_back(keys_grad, cosine_ref[...], sine_ref[...])
    values_grad = values_grad_ref[...]
    values_grad = values_grad + pltpu.roll(values_grad, HD, 1)
    left = grid_of(length, LANES, 1) < HD
    rows_ref[:, query_width:] = low(jnp.where(left, keys_grad, values_grad))


def attention_forward(projected, segment_column, segment_row, cosine, sine):
    length, width = projected.shape
    query_width = width - LANES
    return pl.pallas_call(
        attention_forward_kernel,
        out_shape=[
            jax.ShapeDtypeStruct((length, query_width), jnp.bfloat16),
            jax.ShapeDtypeStruct((length, query_width // HD), jnp.float32),
        ],
        scratch_shapes=[
            pltpu.VMEM((length, LANES), jnp.bfloat16),
            pltpu.VMEM((length, LANES), jnp.bfloat16),
        ],
        compiler_params=pltpu.CompilerParams(vmem_limit_bytes=40 * 2**20),
        cost_estimate=pl.CostEstimate(
            flops=5 * 10**9, bytes_accessed=5 * 2**20, transcendentals=3 * 10**6
        ),
        name="attention_forward",
    )(projected, segment_column, segment_row, cosine, sine)


def attention_backward(projected, grad, totals, segment_column, segment_row, cosine, sine):
    length, width = projected.shape
    return pl.pallas_call(
        attention_backward_kernel,
        out_shape=jax.ShapeDtypeStruct((length, width), jnp.bfloat16),
        scratch_shapes=[
            pltpu.VMEM((length, LANES), jnp.bfloat16),
            pltpu.VMEM((length, LANES), jnp.bfloat16),
            pltpu.VMEM((length, LANES), jnp.float32),
            pltpu.VMEM((length, LANES), jnp.float32),
        ],
        compiler_params=pltpu.CompilerParams(vmem_limit_bytes=40 * 2**20),
        cost_estimate=pl.CostEstimate(
            flops=10**10, bytes_accessed=6 * 2**20, transcendentals=3 * 10**6
        ),
        name="attention_backward",
    )(projected, grad, totals, segment_column, segment_row, cosine, sine)


def whole(shape):
    return pl.BlockSpec(shape, lambda i: (0,) * len(shape))


def mixer_sizes(projected, tables):
    return projected.shape[0], tables[0].shape[1], tables[1].shape[1]


def mixer_forward(projected, tables):
    length, channels, state_width = mixer_sizes(projected, tables)
    count = length // SPAN

    def rows_of(width, place=0):
        return pl.BlockSpec((SPAN, width), lambda i: (i, place))

    state_place = 2 * channels // state_width
    step_place = (2 * channels + state_width) // LANES

    return pl.pallas_call(
        mixer_forward_kernel,
        grid=(count,),
        in_specs=[
            rows_of(channels, 1), rows_of(channels), rows_of(state_width, state_place), rows_of(LANES, step_place),
            whole((8, channels)), whole((8, state_width)), whole((8, LANES)), whole((1, channels)),
        ],
        out_specs=[
            rows_of(channels), rows_of(channels), rows_of(1),
            pl.BlockSpec((1, N_STATE, channels), lambda i: (i, 0, 0)),
        ],
        out_shape=[
            jax.ShapeDtypeStruct((length, channels), jnp.float32),
            jax.ShapeDtypeStruct((length, channels), jnp.bfloat16),
            jax.ShapeDtypeStruct((length, 1), jnp.float32),
            jax.ShapeDtypeStruct((count, N_STATE, channels), jnp.bfloat16),
        ],
        scratch_shapes=[
            pltpu.VMEM((8, channels), jnp.float32),
            pltpu.VMEM((8, state_width), jnp.float32),
            pltpu.VMEM((N_STATE, channels), jnp.float32),
            pltpu.VMEM((SPAN, channels), jnp.bfloat16),
        ],
        compiler_params=pltpu.CompilerParams(vmem_limit_bytes=40 * 2**20),
        cost_estimate=pl.CostEstimate(
            flops=6 * 10**9, bytes_accessed=14 * 2**20, transcendentals=4 * 10**6
        ),
        name="mixer_forward",
    )(projected, projected, projected, projected, *tables)


def mixer_backward(grad, stats, scanned, projected, saved, tables, gain_wide):
    length, channels, state_width = mixer_sizes(projected, tables)
    count = length // SPAN
    total = 2 * channels + state_width + LANES

    def rows_of(width, place=0):
        return pl.BlockSpec((SPAN, width), lambda i: (count - 1 - i, place))

    def before(width, place):
        return pl.BlockSpec(
            (8, width), lambda i: (jnp.maximum((count - 1 - i) * (SPAN // 8) - 1, 0), place)
        )

    state_place = 2 * channels // state_width
    step_place = (2 * channels + state_width) // LANES

    return pl.pallas_call(
        mixer_backward_kernel,
        grid=(count,),
        in_specs=[
            rows_of(channels), rows_of(2), rows_of(channels), rows_of(channels, 1), before(channels, 1),
            rows_of(channels), rows_of(state_width, state_place), before(state_width, state_place),
            rows_of(LANES, step_place),
            pl.BlockSpec((1, N_STATE, channels), lambda i: (count - 1 - i, 0, 0)),
            whole((8, channels)), whole((8, state_width)), whole((8, LANES)), whole((1, channels)),
            whole((1, channels)),
        ],
        out_specs=[
            rows_of(total), whole((8, channels)), whole((8, state_width)), whole((8, LANES)),
        ],
        out_shape=[
            jax.ShapeDtypeStruct((length, total), jnp.bfloat16),
            jax.ShapeDtypeStruct((8, channels), jnp.float32),
            jax.ShapeDtypeStruct((8, state_width), jnp.float32),
            jax.ShapeDtypeStruct((8, LANES), jnp.float32),
        ],
        scratch_shapes=[
            pltpu.VMEM((8, channels), jnp.float32),
            pltpu.VMEM((8, state_width), jnp.float32),
            pltpu.VMEM((N_STATE, channels), jnp.float32),
            pltpu.VMEM((LANES, SPAN), jnp.float32),
        ],
        compiler_params=pltpu.CompilerParams(vmem_limit_bytes=40 * 2**20),
        cost_estimate=pl.CostEstimate(
            flops=20 * 10**9, bytes_accessed=20 * 2**20, transcendentals=8 * 10**6
        ),
        name="mixer_backward",
    )(
        grad, stats, scanned, projected, projected, projected, projected, projected, projected, saved,
        *tables, gain_wide,
    )


def on_device(
    block_input,
    segment_ids,
    out_grad,
    gating_weight,
    inner_weight,
    state_weight,
    step_weight,
    step_bias,
    decay_log,
    skip_scale,
    inner_conv,
    state_conv,
    mixer_gain,
    mixer_proj,
    query_weight,
    key_weight,
    value_weight,
    attention_out,
    first_gain,
    second_gain,
    gate_weight,
    up_weight,
    down_projection_weight,
):
    seq_count, seq_len = segment_ids.shape
    channels = inner_weight.shape[1]
    head_local = step_weight.shape[1]
    query_heads = query_weight.shape[1] // HD
    kv_heads = key_weight.shape[1] // HD
    mixer_width = H_SSM * P_SIZE

    tokens = block_input.astype(jnp.float32)
    first_inverse = lax.rsqrt(jnp.mean(tokens * tokens, axis=-1, keepdims=True) + epsilon)
    first_vector = first_gain.astype(jnp.float32)
    normed_share = (tokens * first_inverse * first_vector).astype(jnp.bfloat16)
    normed = gather_rows(normed_share)
    model_width = normed.shape[1]
    place = lax.axis_index("tensor")
    share_rows = tokens.shape[0]
    piece_rows = share_rows // PIECES
    other_grad = swap_tensor(after(out_grad, [normed]))
    state_width = state_weight.shape[1]
    mixer_weights = jnp.concatenate(
        [gating_weight, inner_weight, state_weight, jnp.pad(step_weight, ((0, 0), (0, LANES - head_local)))],
        axis=1,
    )
    projected = dense(normed, mixer_weights)

    def eight_rows(values):
        return jnp.pad(values.astype(jnp.float32), ((0, 8 - values.shape[0]), (0, 0)))

    head_table = jnp.pad(
        jnp.stack([step_bias, -jnp.exp(decay_log)]), ((0, 6), (0, LANES - head_local))
    )
    skip_wide = jnp.repeat(skip_scale, P_SIZE)[None]
    tables = (eight_rows(inner_conv), eight_rows(state_conv), head_table, skip_wide)
    gated, scanned, squares, saved_states = mixer_forward(projected, tables)
    gated_squares = both(squares)
    mixer_inverse = lax.rsqrt(gated_squares / mixer_width + epsilon)
    mixer_vector = mixer_gain.astype(jnp.float32)
    mixer_normed = (gated * mixer_inverse * mixer_vector).astype(jnp.bfloat16)
    cosine, sine = rope_tables(seq_len)
    segments = (segment_ids.reshape(seq_len, 1), segment_ids.reshape(1, seq_len))
    attention_weights = jnp.concatenate([query_weight, key_weight, value_weight], axis=1)
    attention_inputs = dense(normed, attention_weights)
    attended, log_totals = attention_forward(attention_inputs, *segments, cosine, sine)
    second_vector = second_gain.astype(jnp.float32)

    def branch_rows(start):
        return dense(rows_at(mixer_normed, start, piece_rows), mixer_proj) + dense(
            rows_at(attended, start, piece_rows), attention_out
        )

    def piece_of(value, piece):
        return value[piece * piece_rows : (piece + 1) * piece_rows]

    residuals, second_inverses, kept, outputs, second_grads = [], [], [], [], []
    branch_own, branch_other, first_residual_grads = [], [], []
    for piece in range(PIECES):
        offset = piece * piece_rows
        other_part = branch_rows((1 - place) * share_rows + offset)
        residual = piece_of(tokens, piece) + swapped_sum(
            branch_rows(place * share_rows + offset), other_part
        )
        inverse = lax.rsqrt(jnp.mean(residual * residual, axis=-1, keepdims=True) + epsilon)
        residuals.append(residual)
        second_inverses.append(inverse)
    normed_pieces = []
    for residual, inverse in zip(residuals, second_inverses):
        normed_own = low(residual * inverse * second_vector)
        normed_pieces.append(jnp.concatenate([normed_own, swap_tensor(normed_own)], axis=0))
    gradient_pieces = []
    for piece in range(PIECES):
        normed_two = normed_pieces[piece]
        full_grad = jnp.concatenate([piece_of(out_grad, piece), piece_of(other_grad, piece)], axis=0)
        gate_pre = dense(normed_two, gate_weight)
        up_pre = dense(normed_two, up_weight)
        gate_sigmoid = jax.nn.sigmoid(gate_pre)
        gate_act = gate_pre * gate_sigmoid
        hidden = low(gate_act * up_pre)
        grad_hidden = back_dot(full_grad, down_projection_weight)
        grad_gate_pre = low(
            grad_hidden * up_pre * gate_sigmoid * (1.0 + gate_pre * (1.0 - gate_sigmoid))
        )
        grad_up_pre = low(grad_hidden * gate_act)
        kept.append((hidden, full_grad, jnp.concatenate([grad_gate_pre, grad_up_pre], axis=1)))

        def second_back(rows):
            return back_dot(grad_gate_pre[rows], gate_weight) + back_dot(grad_up_pre[rows], up_weight)

        own, other = slice(0, piece_rows), slice(piece_rows, 2 * piece_rows)
        second_other = second_back(other)
        second_own = second_back(own)
        second_grads.append(swapped_sum(second_own, second_other))
        outputs.append((dense(hidden[own], down_projection_weight), dense(hidden[other], down_projection_weight)))
    kept = [tuple(after(one, [second_own, second_other]) for one in pieces) for pieces in kept]
    hidden_rows, full_rows, gate_up_rows = [jnp.concatenate(parts, axis=0) for parts in zip(*kept)]
    normed_rows = jnp.concatenate(normed_pieces, axis=0)
    ffn_grads = jnp.concatenate(
        [low(row_dot(hidden_rows, full_rows)), low(row_dot(normed_rows, gate_up_rows))], axis=1
    )
    ffn_share = lax.psum_scatter(ffn_grads, "dp", scatter_dimension=0, tiled=True)
    ffn_sums = lax.all_gather(ffn_share, "dp", axis=0, tiled=True)
    for piece in range(PIECES):
        residual, inverse = residuals[piece], second_inverses[piece]
        grad_residual = piece_of(out_grad, piece).astype(jnp.float32) + norm_back(
            second_grads[piece], residual, inverse, second_vector
        )
        first_residual_grads.append(grad_residual)
        branch_own.append(low(grad_residual))
        branch_other.append(swap_tensor(branch_own[-1]))
    residual = jnp.concatenate(residuals, axis=0)
    grad_normed_two = jnp.concatenate(second_grads, axis=0)
    grad_second_gain = jnp.sum(
        grad_normed_two * residual * jnp.concatenate(second_inverses, axis=0), axis=0
    )
    grad_residual = jnp.concatenate(first_residual_grads, axis=0)
    branch_grad = in_order(
        place, jnp.concatenate(branch_own, axis=0), jnp.concatenate(branch_other, axis=0)
    )
    block_output = jnp.concatenate(
        [
            low(residuals[piece] + swapped_sum(own, after(other, [branch_grad])))
            for piece, (own, other) in enumerate(outputs)
        ],
        axis=0,
    )
    grad_mixer_normed = back_dot(branch_grad, mixer_proj)
    cross_part = jnp.sum(gated * (grad_mixer_normed * mixer_vector), axis=-1, keepdims=True)
    cross_sum = both(cross_part)
    grad_attended = low(back_dot(branch_grad, attention_out))
    branch_sum = DpSum(
        jnp.concatenate(
            [low(row_dot(mixer_normed, branch_grad)), low(row_dot(attended, branch_grad))], axis=0
        )
    )
    attention_rows = attention_backward(
        attention_inputs, after(grad_attended, [cross_part]), log_totals, *segments, cosine, sine
    )
    stats = jnp.concatenate(
        [mixer_inverse, mixer_inverse**3 * (cross_sum / mixer_width)], axis=1
    )
    stats = after(stats, branch_sum.advance(), [attention_rows])
    mixer_rows, inner_sums, state_sums, head_sums = mixer_backward(
        grad_mixer_normed, stats, scanned, projected, saved_states, tables, mixer_vector[None]
    )
    normed_again = after(normed, [mixer_rows])

    def first_back(start):
        return back_dot(rows_at(mixer_rows, start, share_rows), mixer_weights) + back_dot(
            rows_at(attention_rows, start, share_rows), attention_weights
        )

    grad_inputs = jnp.concatenate(
        [low(row_dot(normed_again, mixer_rows)), low(row_dot(normed_again, attention_rows))], axis=1
    )
    split = grad_inputs.shape[1] // (2 * LANES) * LANES
    input_sum = DpSum(
        grad_inputs, split, (2 * channels - split, 2 * channels + state_width - split)
    )
    mixer_rows = after(mixer_rows, [grad_inputs])
    other_part = first_back((1 - place) * share_rows)
    grad_normed = swapped_sum(first_back(place * share_rows), other_part)
    grad_first_gain = jnp.sum(grad_normed * tokens * first_inverse, axis=0)
    input_grad = grad_residual + norm_back(grad_normed, tokens, first_inverse, first_vector)
    ffn_width = gate_weight.shape[1]
    input_sum.advance(branch_sum.advance())
    input_sum.advance(branch_sum.advance())
    input_sum.advance(branch_sum.advance(), [ffn_sums])
    grad_down, grad_gate, grad_up = jnp.split(
        ffn_sums.astype(jnp.float32), [model_width, model_width + ffn_width], axis=1
    )
    input_sum.advance(branch_sum.advance())
    input_sum.advance(branch_sum.advance())
    input_sum.advance(branch_sum.advance(), [grad_down, grad_gate, grad_up])
    taps = inner_conv.shape[0]
    grad_inner_conv, grad_mixer_gain = inner_sums[:taps], inner_sums[taps]
    grad_skip_scale = jnp.sum(inner_sums[taps + 1].reshape(head_local, P_SIZE), axis=1)
    grad_state_conv = state_sums[:taps]
    grad_step_bias, grad_decay_log = head_sums[0, :head_local], head_sums[1, :head_local]
    shared_small = jnp.concatenate(
        [grad_state_conv.reshape(-1), grad_first_gain, grad_second_gain]
    )
    own_small = jnp.concatenate(
        [
            grad_inner_conv.reshape(-1),
            grad_mixer_gain,
            grad_step_bias,
            grad_decay_log,
            grad_skip_scale,
        ]
    )
    small = jnp.concatenate([both(shared_small), own_small])
    small_bits = bits_in_order(False)
    for bit in small_bits:
        got = flip(small, bit)
        if bit == small_bits[-2]:
            input_sum.advance(branch_sum.advance(), [got])
        small = small + got
    branch_sums = branch_sum.finish().astype(jnp.float32)
    grad_mixer_proj, attention_output_gradient = branch_sums[:channels], branch_sums[channels:]
    input_sum.advance([grad_mixer_proj, attention_output_gradient, small, input_grad, block_output])
    own_share, other_share, share_place = input_sum.finish()
    step_start = 2 * channels + state_width
    query_start = step_start + LANES
    key_start = query_start + query_heads * HD
    value_start = key_start + kv_heads * HD
    grad_gating, grad_inner, grad_state, grad_step, grad_query, grad_key, grad_value = unpack(
        own_share,
        other_share,
        share_place,
        [
            (0, channels),
            (channels, channels),
            (2 * channels, state_width),
            (step_start, head_local),
            (query_start, query_heads * HD),
            (key_start, kv_heads * HD),
            (value_start, kv_heads * HD),
        ],
    )
    shared_small, own_small = small[: shared_small.shape[0]], small[shared_small.shape[0] :]
    grad_state_conv, grad_first_gain, grad_second_gain = jnp.split(
        shared_small, [taps * state_width, taps * state_width + model_width]
    )
    starts = [taps * channels, (taps + 1) * channels]
    starts = starts + [starts[1] + head_local, starts[1] + 2 * head_local]
    grad_inner_conv, grad_mixer_gain, grad_step_bias, grad_decay_log, grad_skip_scale = jnp.split(
        own_small, starts
    )
    return (
        block_output,
        input_grad,
        grad_gating,
        grad_inner,
        grad_state,
        grad_step,
        grad_step_bias,
        grad_decay_log,
        grad_skip_scale,
        grad_inner_conv.reshape(taps, channels),
        grad_state_conv.reshape(taps, state_width),
        grad_mixer_gain,
        grad_mixer_proj,
        grad_query,
        grad_key,
        grad_value,
        attention_output_gradient,
        grad_first_gain,
        grad_second_gain,
        grad_gate,
        grad_up,
        grad_down,
    )


def solution(mesh):
    placed = (
        P(("dp", "tensor"), None),
        P("dp", None),
        P(("dp", "tensor"), None),
        P(None, "tensor"),
        P(None, "tensor"),
        P(),
        P(None, "tensor"),
        P("tensor"),
        P("tensor"),
        P("tensor"),
        P(None, "tensor"),
        P(),
        P("tensor"),
        P("tensor", None),
        P(None, "tensor"),
        P(None, "tensor"),
        P(None, "tensor"),
        P("tensor", None),
        P(),
        P(),
        P(None, "tensor"),
        P(None, "tensor"),
        P("tensor", None),
    )
    return jax.shard_map(
        on_device,
        mesh=mesh,
        in_specs=placed,
        out_specs=(
            P(("dp", "tensor"), None),
            P(("dp", "tensor"), None),
            P(None, "tensor"),
            P(None, "tensor"),
            P(),
            P(None, "tensor"),
            P("tensor"),
            P("tensor"),
            P("tensor"),
            P(None, "tensor"),
            P(),
            P("tensor"),
            P("tensor", None),
            P(None, "tensor"),
            P(None, "tensor"),
            P(None, "tensor"),
            P("tensor", None),
            P(),
            P(),
            P(None, "tensor"),
            P(None, "tensor"),
            P("tensor", None),
        ),
        check_vma=False,
    )
```
